256 devices in a mesh: row: 64 (over z, y, x_hi), col: 4 (over x_lo, core).
Axes of the slice: x: 4 (x_hi: 2, x_lo: 2; x = x_hi * 2 + x_lo), y: 4, z: 8, core: 2. Of those that a mesh axis runs over, the one named last changes fastest.
Arguments:
- measured: float32 [64, 65536], P(None, ('row', 'col')), may hold values from -4 to 4
- generated: float32 [64, 32768], P(None, ('col', 'row')), may hold values from -3 to 3
- previous: float32 [32768], P(('col', 'row')), may hold values from -2 to 14
- row_weight: float32 [65536], P(('row', 'col')), may hold values from 0.5 to 2
- col_weight: float32 [32768], P(('col', 'row')), may hold values from 0.5 to 2
Outputs:
- row_potential: float32 [65536], P(('row', 'col'))
- column_potential: float32 [32768], P(('col', 'row'))
- row_gap: float32 [65536], P(('row', 'col'))
The draws below stay inside these ranges and needn't reach their ends.
All inputs are finite; a program needn't handle non-finite values.
Results may differ from the reference program's by a relative error of at most 0.0003.
Values sent between devices are 32-bit elements; how exact they have to be, the bound alone decides.
A program may use at most 64 MiB of HBM per device.

```python
import math
import jax
import jax.numpy as jnp
from jax import lax

DIM = 64
NR = 65536
NC = 32768


def draw_measured(key, part):
    key = jax.random.fold_in(key, 1)
    first, second = jax.random.split(key)
    base = jnp.clip(jax.random.normal(first, (DIM, NR), jnp.float32), -6.0, 6.0)
    scale = jnp.exp(jax.random.uniform(second, (1, NR), jnp.float32, -1.0, 1.0) * math.log(2.0))
    return 0.125 * base * scale


def draw_generated(key, part):
    key = jax.random.fold_in(key, 2)
    first, second, third = jax.random.split(key, 3)
    base = jnp.clip(jax.random.normal(first, (DIM, NC), jnp.float32), -6.0, 6.0)
    picked = jax.random.randint(third, (1, NC), 0, 256) == 0
    boost = jnp.where(picked, 16.0, 1.0)
    scale = jnp.exp(jax.random.uniform(second, (1, NC), jnp.float32, -1.0, 1.0) * math.log(2.0))
    return jnp.clip(0.125 * base * scale * boost, -3.0, 3.0)


def draw_previous(key, part):
    key = jax.random.fold_in(key, 3)
    first = jax.random.fold_in(key, 0)
    base = 0.3 * jnp.clip(jax.random.normal(first, (NC,), jnp.float32), -6.0, 6.0)
    return base


def shard_levels(rng, dims, shards, smallest, largest):
    def one(dim, parts):
        draws = jax.random.uniform(jax.random.fold_in(jax.random.fold_in(rng, 6), dim), (parts,), jnp.float32, smallest / len(shards), largest / len(shards))
        return jnp.repeat(jnp.exp(draws), dims[dim] // parts).reshape((-1,) + (1,) * (len(dims) - dim - 1))

    factor_of = one(*shards[0])
    for cut in shards[1:]:
        factor_of = factor_of * one(*cut)
    return factor_of


def setup_inputs(seed: int = 0) -> dict:
    arg_keys = jax.random.split(jax.random.key(seed), 6)
    measured = draw_measured(jax.random.fold_in(arg_keys[5], 71), 0)
    generated = draw_generated(jax.random.fold_in(arg_keys[5], 71), 0)
    previous = draw_previous(jax.random.fold_in(arg_keys[5], 71), 0)
    row_weight = jnp.clip(jnp.exp(math.log(2.0) - 1.3862944 * jax.random.uniform(arg_keys[3], (NR,), jnp.float32) ** shard_levels(arg_keys[3], (NR,), ((0, 256),), -0.2, 0.2)), 0.5, 2.0)
    col_weight = jnp.clip(jnp.exp(math.log(2.0) - 1.3862944 * jax.random.uniform(arg_keys[4], (NC,), jnp.float32) ** shard_levels(arg_keys[4], (NC,), ((0, 256),), -0.2, 0.2)), 0.5, 2.0)
    return {"measured": measured, "generated": generated, "previous": previous, "row_weight": row_weight, "col_weight": col_weight}


EPSILON = 0.1


def costs(left, right):
    cross = lax.dot_general(left, right, (((0,), (0,)), ((), ())), precision=lax.Precision.HIGHEST, preferred_element_type=jnp.float32)
    return jnp.sum(left * left, 0)[:, None] + jnp.sum(right * right, 0)[None, :] - 2.0 * cross


def side_lse(left, right, right_log, right_pot):
    count = left.shape[1]
    block = math.gcd(count, 1024)
    blocks = left.reshape(left.shape[0], count // block, block).transpose(1, 0, 2)

    def one(piece):
        scores = right_log[None, :] + (right_pot[None, :] - costs(piece, right)) / EPSILON
        top = jnp.max(scores, 1)
        return top + jnp.log(jnp.sum(jnp.exp(scores - top[:, None]), 1))

    return lax.map(one, blocks).reshape(-1)


def reference(measured, generated, previous, row_weight, col_weight):
    log_a = jnp.log(row_weight) - math.log(NR)
    log_b = jnp.log(col_weight) - math.log(NC)
    row_potential = -EPSILON * side_lse(measured, generated, log_b, previous)
    column_potential = -EPSILON * side_lse(generated, measured, log_a, row_potential)
    row_gap = row_potential / EPSILON + side_lse(measured, generated, log_b, column_potential)
    return row_potential, column_potential, row_gap
```

```python
import functools
import math

import jax
import jax.numpy as jnp
from jax import lax
from jax.experimental import pallas as pl
from jax.experimental.pallas import tpu as pltpu
from jax.sharding import PartitionSpec as P

EPSILON = 0.1
LOG2E = 1.0 / math.log(2.0)
LN2 = math.log(2.0)
MESH = pl.DeviceIdType.MESH
F32 = jnp.float32
BF16 = jnp.bfloat16

GRID = {"z": 8, "y": 4, "xh": 2, "xl": 2}
XB = 256
YB = 128
DIM = 64


def kernel(
    measured,
    generated,
    previous,
    row_weight,
    col_weight,
    row_out,
    col_out,
    gap_out,
    xraw,
    yraw,
    yt,
    xaug,
    scores,
    cstat,
    sstat,
    row_stat_out,
    row_stat_in,
    rbuf,
    col_stat_out,
    col_stat_in,
    qbuf,
    w_out,
    w_in,
    x_send,
    x_recv,
    y_send,
    y_recv,
    row_send,
    row_recv,
    r_send,
    r_recv,
    col_send,
    col_recv,
    q_send,
    q_recv,
    w_send,
    w_recv,
):
    NZ, NY, NXH, NXL = GRID["z"], GRID["y"], GRID["xh"], GRID["xl"]
    NX = NXH * NXL
    NQ, NP = NX * NY, NZ * 2
    NJ = NP * YB
    NI = NQ * XB
    NL = NI // 128
    ndev = NQ * NP

    row = lax.axis_index("row")
    col = lax.axis_index("col")
    z = row // (NY * NXH)
    y = (row // NXH) % NY
    x = (row % NXH) * NXL + col // 2
    core = col % 2

    def device(dz, dy, dx, dc):
        zz, yy, xx = (z + dz) % NZ, (y + dy) % NY, (x + dx) % NX
        return ((zz * NY + yy) * NXH + xx // NXL, (xx % NXL) * 2 + (core + dc) % 2)

    def xslot(dy, dx):
        return (dy % NY) * NX + dx % NX

    def yslot(dz, dc):
        return (dz % NZ) * 2 + dc % 2

    def copy(src, dst, send, recv, dev):
        return pltpu.make_async_remote_copy(
            src_ref=src, dst_ref=dst, send_sem=send, recv_sem=recv, device_id=dev, device_id_type=MESH
        )

    plane = [(dy, dx) for dy in range(NY) for dx in range(NX) if (dy, dx) != (0, 0)]
    line = [(dz, dc) for dz in range(NZ) for dc in range(2) if (dz, dc) != (0, 0)]

    barrier = pltpu.get_barrier_semaphore()
    for dy, dx in plane:
        pl.semaphore_signal(barrier, inc=1, device_id=device(0, dy, dx, 0), device_id_type=MESH)
    for dz, dc in line:
        pl.semaphore_signal(barrier, inc=1, device_id=device(dz, 0, 0, dc), device_id_type=MESH)

    scale = 2.0 * LOG2E / EPSILON
    xraw[0] = measured[...] * scale
    gen = generated[...]
    log_b = jnp.log(col_weight[...]) - math.log(YB * ndev)
    ysq = jnp.sum(gen * gen, axis=0, keepdims=True)
    u = (log_b + (previous[...] - ysq) / EPSILON) * LOG2E
    yraw[0, 0:DIM] = gen
    yraw[0, DIM : DIM + 8] = jnp.broadcast_to(u, (8, YB))
    log_a = jnp.log(row_weight[...]) - math.log(XB * ndev)
    xsq = jnp.sum(measured[...] * measured[...], axis=0, keepdims=True)

    pl.semaphore_wait(barrier, len(plane) + len(line))

    pending = []

    def start(c):
        c.start()
        pending.append(c)

    half = DIM // 2
    counter = [0]

    def send_x(slot, part, dst_slot, dev):
        at = pl.ds(part * half, half)
        n = counter[0]
        counter[0] += 1
        start(copy(xraw.at[slot, at], xraw.at[dst_slot, at], x_send.at[n], x_recv.at[dst_slot, part], dev))

    def wait_x(slot, part):
        at = pl.ds(part * half, half)
        copy(xraw.at[slot, at], xraw.at[slot, at], x_send.at[0], x_recv.at[slot, part], device(0, 0, 1, 0)).wait_recv()

    def send_y(n, slot, dst_slot, dev):
        start(copy(yraw.at[slot], yraw.at[dst_slot], y_send.at[n], y_recv.at[dst_slot], dev))

    def wait_y(slot):
        copy(yraw.at[slot], yraw.at[slot], y_send.at[0], y_recv.at[slot], device(0, 0, 0, 1)).wait_recv()

    def near_first(n):
        return sorted(range(1, n), key=lambda d: min(d, n - d))

    for ez in near_first(NZ):
        send_y(ez, 0, yslot(-ez, 0), device(ez, 0, 0, 0))
    send_y(0, 0, yslot(0, 1), device(0, 0, 0, 1))
    for e in near_first(max(NX, NY)):
        if e < NX:
            send_x(0, 0, xslot(0, -e), device(0, 0, e, 0))
        if e < NY:
            send_x(0, 1, xslot(-e, 0), device(0, e, 0, 0))
    for e in near_first(max(NX, NY)):
        if e < NX:
            send_x(0, 1, xslot(0, -e), device(0, 0, e, 0))
        if e < NY:
            send_x(0, 0, xslot(-e, 0), device(0, e, 0, 0))

    def forward_x(d):
        if d < NX:
            wait_x(xslot(0, d), 0)
            for ey in near_first(NY):
                send_x(xslot(0, d), 0, xslot(-ey, d), device(0, ey, 0, 0))
        if d < NY:
            wait_x(xslot(d, 0), 1)
            for ex in near_first(NX):
                send_x(xslot(d, 0), 1, xslot(d, -ex), device(0, 0, ex, 0))

    def forward_y(dz):
        wait_y(yslot(dz, 0))
        send_y(NZ + dz, yslot(dz, 0), yslot(dz, 1), device(0, 0, 0, 1))

    xs, ys = near_first(max(NX, NY)), near_first(NZ)
    for k in range(max(len(xs), len(ys))):
        if k < len(xs):
            forward_x(xs[k])
        if k < len(ys):
            forward_y(ys[k])

    xaug[3 * DIM :] = jnp.ones((DIM, XB), BF16)

    def split(v):
        hi = v.astype(BF16).astype(F32)
        return hi, v - hi

    def turn_y(slot):
        v = yraw[slot, 0:DIM]
        hi, lo = split(v)
        t = yraw[slot, DIM : DIM + 8]
        t1, rest = split(t)
        t2, t3 = split(rest)
        sub = lax.broadcasted_iota(jnp.int32, (8, YB), 0)
        extra = jnp.where(sub == 0, t1, jnp.where(sub == 1, t2, jnp.where(sub == 2, t3, 0.0)))
        at = pl.ds(pl.multiple_of(slot * YB, YB), YB)
        yt[at, 0 : 2 * DIM] = jnp.concatenate([hi, hi], axis=0).T.astype(BF16)
        yt[at, 2 * DIM :] = jnp.concatenate([lo, extra, jnp.zeros((DIM - 8, YB), F32)], axis=0).T.astype(BF16)

    for dz in range(NZ):
        wait_y(yslot(dz, 1))
    for dy, dx in plane:
        for part in range(2):
            if not ((dy == 0 and part == 0) or (dx == 0 and part == 1)):
                wait_x(xslot(dy, dx), part)

    def turn_loop(slot, carry):
        turn_y(slot)
        return carry

    lax.fori_loop(0, NP, turn_loop, 0)

    CH = 256
    sub256 = lax.broadcasted_iota(jnp.int32, (8, XB), 0)
    sub128 = lax.broadcasted_iota(jnp.int32, (8, YB), 0)

    def row_block(b):
        v = xraw[b]
        hi = v.astype(BF16)
        lo = (v - hi.astype(F32)).astype(BF16)
        xaug[0:DIM] = hi
        xaug[DIM : 2 * DIM] = lo
        xaug[2 * DIM : 3 * DIM] = hi
        lanes = pl.ds(pl.multiple_of(b * XB, XB), XB)
        top = jnp.full((8, XB), -3e38, F32)
        total = jnp.zeros((8, XB), F32)
        for c in range(NJ // CH):
            res = jnp.dot(yt[c * CH : (c + 1) * CH], xaug[...], preferred_element_type=F32)
            scores[c * CH : (c + 1) * CH, lanes] = res
            r3 = res.reshape(CH // 8, 8, XB)
            new = jnp.maximum(top, jnp.max(r3, axis=0))
            total = total * jnp.exp2(top - new) + jnp.sum(jnp.exp2(r3 - new[None]), axis=0)
            top = new
        best = jnp.max(top, axis=0, keepdims=True)
        summed = jnp.sum(total * jnp.exp2(top - best), axis=0, keepdims=True)
        return jnp.where(sub256 < 4, best, summed)

    def row_loop(b, carry):
        row_stat_out[b] = row_block(b)
        dy, dx = b // NX, b % NX
        dst = ((NY - dy) % NY) * NX + (NX - dx) % NX
        copy(row_stat_out.at[b], row_stat_in.at[dst], row_send.at[b], row_recv.at[dst], device(0, dy, dx, 0)).start()
        return carry

    lax.fori_loop(1, NQ, row_loop, 0)
    row_stat_in[0] = row_block(0)

    def wait_in(buf, slot, send, recv):
        copy(buf.at[slot], buf.at[slot], send.at[slot], recv.at[slot], device(0, 0, 1, 0)).wait_recv()

    def wait_out(buf, slot, send, recv):
        copy(buf.at[slot], buf.at[slot], send.at[slot], recv.at[slot], device(0, 0, 1, 0)).wait_send()

    for k in range(1, NQ):
        wait_in(row_stat_in, k, row_send, row_recv)

    def combined(ref, n):
        stats = [ref[k] for k in range(n)]
        best = functools.reduce(jnp.maximum, [s[0:1] for s in stats])
        summed = functools.reduce(jnp.add, [s[4:5] * jnp.exp2(s[0:1] - best) for s in stats])
        return best + jnp.log(summed) * LOG2E

    row_lse = combined(row_stat_in, NQ)
    rbuf[0] = jnp.broadcast_to(log_a * LOG2E - row_lse, (8, XB))
    for dy, dx in plane:
        s, d = xslot(dy, dx), xslot(-dy, -dx)
        copy(rbuf.at[0], rbuf.at[d], r_send.at[s], r_recv.at[d], device(0, dy, dx, 0)).start()
    row_out[...] = xsq - (EPSILON * LN2) * row_lse
    for k in range(1, NQ):
        wait_in(rbuf, k, r_send, r_recv)

    eye = lax.broadcasted_iota(jnp.int32, (YB, YB), 0) == lax.broadcasted_iota(jnp.int32, (YB, YB), 1)

    def across(v):
        return jnp.sum(jnp.where(eye, v, 0.0), axis=0, keepdims=True)

    def col_block(b):
        base = pl.multiple_of(b * YB, YB)

        def tile(t, carry):
            at = pl.ds(pl.multiple_of(base + t * 8, 8), 8)
            vals = [
                scores[at, l * 128 : (l + 1) * 128] + rbuf[l // 2, :, (l % 2) * 128 : (l % 2 + 1) * 128]
                for l in range(NL)
            ]
            tops = vals
            while len(tops) > 1:
                tops = [jnp.maximum(tops[i], tops[i + 1]) for i in range(0, len(tops), 2)]
            top = tops[0]
            parts = []
            for l in range(NL):
                p = jnp.exp2(vals[l] - top)
                scores[at, l * 128 : (l + 1) * 128] = p
                if l < 4:
                    parts.append(p)
                else:
                    parts[l % 4] = parts[l % 4] + p
            cstat[at, :] = top
            sstat[pl.ds(pl.multiple_of(t * 8, 8), 8), :] = functools.reduce(jnp.add, parts)
            return carry

        lax.fori_loop(0, YB // 8, tile, 0, unroll=4)
        c = cstat[pl.ds(base, YB), :]
        best = jnp.max(c, axis=1, keepdims=True)
        summed = jnp.sum(sstat[...] * jnp.exp2(c - best), axis=1, keepdims=True)
        return jnp.where(sub128 < 4, across(best), across(summed))

    def col_loop(b, carry):
        col_stat_out[b] = col_block(b)
        dz, dc = b // 2, b % 2
        dst = ((NZ - dz) % NZ) * 2 + dc
        copy(col_stat_out.at[b], col_stat_in.at[dst], col_send.at[b], col_recv.at[dst], device(dz, 0, 0, dc)).start()
        return carry

    lax.fori_loop(1, NP, col_loop, 0)
    col_stat_in[0] = col_block(0)
    for k in range(1, NP):
        wait_in(col_stat_in, k, col_send, col_recv)
    col_lse = combined(col_stat_in, NP)
    qbuf[0] = jnp.broadcast_to(log_b * LOG2E - col_lse, (8, YB))
    for dz, dc in line:
        s, d = yslot(dz, dc), yslot(-dz, dc)
        copy(qbuf.at[0], qbuf.at[d], q_send.at[s], q_recv.at[d], device(dz, 0, 0, dc)).start()
    col_out[...] = previous[...] + EPSILON * log_b - (EPSILON * LN2) * col_lse

    def gap_block(b, acc):
        base = pl.multiple_of(b * YB, YB)
        q = jnp.sum(jnp.where(eye, qbuf[b, 0:1], 0.0), axis=1, keepdims=True)
        sstat[...] = jnp.exp2(cstat[pl.ds(base, YB), :] + q)

        def tile(t, acc):
            at = pl.ds(pl.multiple_of(base + t * 8, 8), 8)
            g = sstat[pl.ds(pl.multiple_of(t * 8, 8), 8), :]
            return [acc[l] + scores[at, l * 128 : (l + 1) * 128] * g for l in range(NL)]

        return lax.fori_loop(0, YB // 8, tile, acc, unroll=4)

    def gap_loop(b, acc):
        wait_in(qbuf, b, q_send, q_recv)
        return gap_block(b, acc)

    acc = gap_block(0, [jnp.zeros((8, 128), F32) for _ in range(NL)])
    acc = lax.fori_loop(1, NP, gap_loop, acc)
    for k in range(NQ):
        for h in range(2):
            total = jnp.sum(acc[2 * k + h], axis=0, keepdims=True)
            at = slice(h * 128, (h + 1) * 128)
            if k == 0:
                w_in[0, :, at] = jnp.broadcast_to(total, (8, 128))
            else:
                w_out[k, :, at] = jnp.broadcast_to(total, (8, 128))
        if k > 0:
            dy, dx = k // NX, k % NX
            d = xslot(-dy, -dx)
            copy(w_out.at[k], w_in.at[d], w_send.at[k], w_recv.at[d], device(0, dy, dx, 0)).start()

    for c in pending:
        c.wait_send()
    for k in range(1, NQ):
        wait_out(row_stat_out, k, row_send, row_recv)
        wait_out(rbuf, k, r_send, r_recv)
    for k in range(1, NP):
        wait_out(col_stat_out, k, col_send, col_recv)
        wait_out(qbuf, k, q_send, q_recv)

    for k in range(1, NQ):
        wait_in(w_in, k, w_send, w_recv)
    mass = functools.reduce(jnp.add, [w_in[k, 0:1] for k in range(NQ)])
    gap_out[...] = jnp.log(mass) - log_a
    for k in range(1, NQ):
        wait_out(w_out, k, w_send, w_recv)


def body(measured, generated, previous, row_weight, col_weight):
    NQ = GRID["y"] * GRID["xh"] * GRID["xl"]
    NP = GRID["z"] * 2
    NJ, NI = NP * YB, NQ * XB
    dma = pltpu.SemaphoreType.DMA
    row, col, gap = pl.pallas_call(
        kernel,
        out_shape=(
            jax.ShapeDtypeStruct((1, XB), F32),
            jax.ShapeDtypeStruct((1, YB), F32),
            jax.ShapeDtypeStruct((1, XB), F32),
        ),
        in_specs=[pl.BlockSpec(memory_space=pltpu.VMEM)] * 5,
        out_specs=(pl.BlockSpec(memory_space=pltpu.VMEM),) * 3,
        scratch_shapes=[
            pltpu.VMEM((NQ, DIM, XB), F32),
            pltpu.VMEM((NP, DIM + 8, YB), F32),
            pltpu.VMEM((NJ, 4 * DIM), BF16),
            pltpu.VMEM((4 * DIM, XB), BF16),
            pltpu.VMEM((NJ, NI), F32),
            pltpu.VMEM((NJ, 128), F32),
            pltpu.VMEM((YB, 128), F32),
            pltpu.VMEM((NQ, 8, XB), F32),
            pltpu.VMEM((NQ, 8, XB), F32),
            pltpu.VMEM((NQ, 8, XB), F32),
            pltpu.VMEM((NP, 8, YB), F32),
            pltpu.VMEM((NP, 8, YB), F32),
            pltpu.VMEM((NP, 8, YB), F32),
            pltpu.VMEM((NQ, 8, XB), F32),
            pltpu.VMEM((NQ, 8, XB), F32),
            dma((2 * NQ,)),
            dma((NQ, 2)),
            dma((NP,)),
            dma((NP,)),
            dma((NQ,)),
            dma((NQ,)),
            dma((NQ,)),
            dma((NQ,)),
            dma((NP,)),
            dma((NP,)),
            dma((NP,)),
            dma((NP,)),
            dma((NQ,)),
            dma((NQ,)),
        ],
        compiler_params=pltpu.CompilerParams(
            collective_id=0, has_side_effects=True, vmem_limit_bytes=48 * 1024 * 1024
        ),
    )(
        measured,
        generated,
        previous.reshape(1, YB),
        row_weight.reshape(1, XB),
        col_weight.reshape(1, YB),
    )
    return row.reshape(XB), col.reshape(YB), gap.reshape(XB)


def solution(mesh):
    placed = (
        P(None, ("row", "col")),
        P(None, ("col", "row")),
        P(("col", "row")),
        P(("row", "col")),
        P(("col", "row")),
    )
    return jax.shard_map(
        body,
        mesh=mesh,
        in_specs=placed,
        out_specs=(P(("row", "col")), P(("col", "row")), P(("row", "col"))),
        check_vma=False,
    )
```

```python
import functools
import math

import jax
import jax.numpy as jnp
from jax import lax
from jax.experimental import pallas as pl
from jax.experimental.pallas import tpu as pltpu
from jax.sharding import PartitionSpec as P

EPSILON = 0.1
LOG2E = 1.0 / math.log(2.0)
LN2 = math.log(2.0)
MESH = pl.DeviceIdType.MESH
F32 = jnp.float32
BF16 = jnp.bfloat16

GRID = {"z": 8, "y": 4, "xh": 2, "xl": 2}
XB = 256
YB = 128
DIM = 64


def kernel(
    measured_hbm,
    generated_hbm,
    previous_hbm,
    row_weight_hbm,
    col_weight_hbm,
    row_out,
    col_out,
    gap_out,
    measured,
    generated,
    previous,
    row_weight,
    col_weight,
    xraw,
    yraw,
    yt,
    xaug,
    cstat,
    sstat,
    row_stat_out,
    row_stat_in,
    rbuf,
    rfull,
    col_stat_out,
    col_stat_in,
    qbuf,
    w_out,
    w_in,
    in_sem,
    x_send,
    x_recv,
    y_send,
    y_recv,
    row_send,
    row_recv,
    r_send,
    r_recv,
    col_send,
    col_recv,
    q_send,
    q_recv,
    w_send,
    w_recv,
    *scores,
):
    NZ, NY, NXH, NXL = GRID["z"], GRID["y"], GRID["xh"], GRID["xl"]
    NX = NXH * NXL
    NQ, NP = NX * NY, NZ * 2
    NI = NQ * XB
    NL = NI // 128
    ndev = NQ * NP

    loads = [
        pltpu.make_async_copy(src, dst, in_sem.at[n])
        for n, (src, dst) in enumerate(
            [
                (generated_hbm, generated),
                (previous_hbm, previous),
                (col_weight_hbm, col_weight),
                (measured_hbm, measured),
                (row_weight_hbm, row_weight),
            ]
        )
    ]
    for c in loads:
        c.start()

    row = lax.axis_index("row")
    col = lax.axis_index("col")
    z = row // (NY * NXH)
    y = (row // NXH) % NY
    x = (row % NXH) * NXL + col // 2
    core = col % 2

    def device(dz, dy, dx, dc):
        zz, yy, xx = (z + dz) % NZ, (y + dy) % NY, (x + dx) % NX
        return ((zz * NY + yy) * NXH + xx // NXL, (xx % NXL) * 2 + (core + dc) % 2)

    def xslot(dy, dx):
        return (dy % NY) * NX + dx % NX

    def yslot(dz, dc):
        return (dz % NZ) * 2 + dc % 2

    def copy(src, dst, send, recv, dev):
        return pltpu.make_async_remote_copy(
            src_ref=src, dst_ref=dst, send_sem=send, recv_sem=recv, device_id=dev, device_id_type=MESH
        )

    def near_first(n):
        return sorted(range(1, n), key=lambda d: min(d, n - d))

    plane = [(dy, dx) for dy in range(NY) for dx in range(NX) if (dy, dx) != (0, 0)]
    line = [(dz, dc) for dz in range(NZ) for dc in range(2) if (dz, dc) != (0, 0)]

    barrier = pltpu.get_barrier_semaphore()
    for dy, dx in plane:
        pl.semaphore_signal(barrier, inc=1, device_id=device(0, dy, dx, 0), device_id_type=MESH)
    for dz, dc in line:
        pl.semaphore_signal(barrier, inc=1, device_id=device(dz, 0, 0, dc), device_id_type=MESH)

    for c in loads:
        c.wait()
    scale = 2.0 * LOG2E / EPSILON
    xraw[0] = measured[...] * scale
    gen = generated[...]
    log_b = jnp.log(col_weight[...]) - math.log(YB * ndev)
    ysq = jnp.sum(gen * gen, axis=0, keepdims=True)
    u = (log_b + (previous[...] - ysq) / EPSILON) * LOG2E
    yraw[0, 0:DIM] = gen
    yraw[0, DIM : DIM + 8] = jnp.broadcast_to(u, (8, YB))
    log_a = jnp.log(row_weight[...]) - math.log(XB * ndev)
    xsq = jnp.sum(measured[...] * measured[...], axis=0, keepdims=True)
    xaug[:, 3 * DIM :] = jnp.ones((NQ // 2, DIM, 2 * XB), BF16)

    pl.semaphore_wait(barrier, len(plane) + len(line))

    pending = []

    def start(c):
        c.start()
        pending.append(c)

    half = DIM // 2
    counter = [0]

    def send_x(slot, part, dst_slot, dev):
        at = pl.ds(part * half, half)
        n = counter[0]
        counter[0] += 1
        start(copy(xraw.at[slot, at], xraw.at[dst_slot, at], x_send.at[n], x_recv.at[dst_slot, part], dev))

    def wait_x(slot, part):
        at = pl.ds(part * half, half)
        copy(xraw.at[slot, at], xraw.at[slot, at], x_send.at[0], x_recv.at[slot, part], device(0, 0, 1, 0)).wait_recv()

    def send_y(n, slot, dst_slot, dev):
        start(copy(yraw.at[slot], yraw.at[dst_slot], y_send.at[n], y_recv.at[dst_slot], dev))

    def wait_y(slot):
        copy(yraw.at[slot], yraw.at[slot], y_send.at[0], y_recv.at[slot], device(0, 0, 0, 1)).wait_recv()

    for ez in near_first(NZ):
        send_y(ez, 0, yslot(-ez, 0), device(ez, 0, 0, 0))
    send_y(0, 0, yslot(0, 1), device(0, 0, 0, 1))
    for part in range(2):
        for e in near_first(max(NX, NY)):
            if e < NX:
                send_x(0, part, xslot(0, -e), device(0, 0, e, 0))
            if e < NY:
                send_x(0, 1 - part, xslot(-e, 0), device(0, e, 0, 0))

    def forward_x(d):
        if d < NX:
            wait_x(xslot(0, d), 0)
            for ey in near_first(NY):
                send_x(xslot(0, d), 0, xslot(-ey, d), device(0, ey, 0, 0))
        if d < NY:
            wait_x(xslot(d, 0), 1)
            for ex in near_first(NX):
                send_x(xslot(d, 0), 1, xslot(d, -ex), device(0, 0, ex, 0))

    def forward_y(dz):
        wait_y(yslot(dz, 0))
        send_y(NZ + dz, yslot(dz, 0), yslot(dz, 1), device(0, 0, 0, 1))

    def split(v):
        hi = v.astype(BF16).astype(F32)
        return hi, v - hi

    sub128 = lax.broadcasted_iota(jnp.int32, (8, YB), 0)

    def turn_y(slot):
        hi, lo = split(yraw[slot, 0:DIM])
        t1, rest = split(yraw[slot, DIM : DIM + 8])
        t2, t3 = split(rest)
        extra = jnp.where(sub128 == 0, t1, jnp.where(sub128 == 1, t2, jnp.where(sub128 == 2, t3, 0.0)))
        at = slice(slot * YB, (slot + 1) * YB)
        yt[at, 0 : 2 * DIM] = jnp.concatenate([hi, hi], axis=0).T.astype(BF16)
        yt[at, 2 * DIM :] = jnp.concatenate([lo, extra, jnp.zeros((DIM - 8, YB), F32)], axis=0).T.astype(BF16)

    def take_x(slot):
        v = xraw[slot]
        hi = v.astype(BF16)
        lo = (v - hi.astype(F32)).astype(BF16)
        at = slice((slot % 2) * XB, (slot % 2 + 1) * XB)
        xaug[slot // 2, 0:DIM, at] = hi
        xaug[slot // 2, DIM : 2 * DIM, at] = lo
        xaug[slot // 2, 2 * DIM : 3 * DIM, at] = hi

    waited = set()

    def ready_x(pair):
        for slot in (2 * pair, 2 * pair + 1):
            dy, dx = slot // NX, slot % NX
            for part in range(2):
                if slot > 0 and not (dy == 0 and part == 0) and not (dx == 0 and part == 1):
                    wait_x(slot, part)
            take_x(slot)

    CH = 2 * YB
    PW = 2 * XB

    def dot_stage(pair, c):
        scores[pair][c * CH : (c + 1) * CH] = jnp.dot(
            yt[c * CH : (c + 1) * CH], xaug[pair], preferred_element_type=F32
        )

    def rows8(pair, c, k):
        return scores[pair][c * CH + k * 8 : c * CH + (k + 1) * 8]

    def max_stage(pair, c, accs):
        accs = list(accs)
        for k in range(CH // 8):
            accs[k % 2] = jnp.maximum(accs[k % 2], rows8(pair, c, k))
        return accs

    def exp_stage(pair, c, top, accs):
        accs = list(accs)
        for k in range(CH // 8):
            accs[k % 2] = accs[k % 2] + jnp.exp2(rows8(pair, c, k) - top)
        return accs

    def finish_rows(pair, top, total):
        best = jnp.max(top, axis=0, keepdims=True)
        summed = jnp.sum(total * jnp.exp2(top - best), axis=0, keepdims=True)
        for h in range(2):
            slot = 2 * pair + h
            ref = row_stat_in if slot == 0 else row_stat_out
            ref[slot, :, 0:XB] = best[:, h * XB : (h + 1) * XB]
            ref[slot, :, XB:] = summed[:, h * XB : (h + 1) * XB]

    def send_rows(pair):
        for slot in (2 * pair, 2 * pair + 1):
            if slot > 0:
                dy, dx = slot // NX, slot % NX
                dst = xslot(-dy, -dx)
                copy(
                    row_stat_out.at[slot], row_stat_in.at[dst], row_send.at[slot], row_recv.at[dst], device(0, dy, dx, 0)
                ).start()

    for d in near_first(max(NX, NY))[:2]:
        forward_x(d)
    turn_y(0)
    order = [0] + near_first(NZ)
    late = near_first(max(NX, NY))[2:]
    lag = 2
    for n in range(NZ + lag):
        if 0 < n < NZ:
            forward_y(order[n])
            turn_y(yslot(order[n], 0))
        if n == 2:
            for d in late:
                forward_x(d)
            ready_x(0)
        if n >= lag:
            dz = order[n - lag]
            wait_y(yslot(dz, 1))
            turn_y(yslot(dz, 1))
            dot_stage(0, dz)

    near = lambda dy: min(dy, NY - dy)
    pairs = sorted(range(NQ // 2), key=lambda p: (near(2 * p // NX), p))
    state = {}
    for step in range(1, len(pairs) + 3):
        one = pairs[step] if step < len(pairs) else None
        two = pairs[step - 1] if 0 <= step - 1 < len(pairs) else None
        three = pairs[step - 2] if 0 <= step - 2 < len(pairs) else None
        if step >= 4:
            send_rows(pairs[step - 4])
        if one is not None:
            ready_x(one)
        tops = [jnp.full((8, PW), -3e38, F32)] * 2
        sums = [jnp.zeros((8, PW), F32)] * 2
        for c in range(NZ):
            if one is not None:
                dot_stage(one, c)
            if two is not None:
                tops = max_stage(two, c, tops)
            if three is not None:
                sums = exp_stage(three, c, state[three], sums)
        if step >= 3 and step - 3 < len(pairs):
            finish_rows(*state.pop("done"))
        if two is not None:
            state[two] = jnp.maximum(*tops)
        if three is not None:
            state["done"] = (three, state.pop(three), sums[0] + sums[1])
    send_rows(pairs[-1])

    def wait_in(buf, slot, send, recv):
        copy(buf.at[slot], buf.at[slot], send.at[slot], recv.at[slot], device(0, 0, 1, 0)).wait_recv()

    def wait_out(buf, slot, send, recv):
        copy(buf.at[slot], buf.at[slot], send.at[slot], recv.at[slot], device(0, 0, 1, 0)).wait_send()

    for k in range(1, NQ):
        wait_in(row_stat_in, k, row_send, row_recv)

    def combined(ref, n, width):
        tops = [ref[k, :, 0:width] for k in range(n)]
        best = functools.reduce(jnp.maximum, tops)
        summed = functools.reduce(jnp.add, [ref[k, :, width:] * jnp.exp2(tops[k] - best) for k in range(n)])
        return best + jnp.log(summed) * LOG2E

    row_lse = combined(row_stat_in, NQ, XB)
    rbuf[0] = log_a * LOG2E - row_lse
    for dy, dx in plane:
        s, d = xslot(dy, dx), xslot(-dy, -dx)
        copy(rbuf.at[0], rbuf.at[d], r_send.at[s], r_recv.at[d], device(0, dy, dx, 0)).start()
    row_out[...] = xsq - (EPSILON * LN2) * row_lse
    for k in range(1, NQ):
        wait_in(rbuf, k, r_send, r_recv)
    for k in range(NQ):
        rfull[:, k * XB : (k + 1) * XB] = jnp.broadcast_to(rbuf[k], (8, XB))

    eye = lax.broadcasted_iota(jnp.int32, (YB, YB), 0) == lax.broadcasted_iota(jnp.int32, (YB, YB), 1)
    per = PW // 128

    def across(v):
        return jnp.sum(jnp.where(eye, v, 0.0), axis=0, keepdims=True)

    def rows_of(b):
        return pl.ds(pl.multiple_of(b * YB, YB), YB)

    def col_tiles(b):
        at = rows_of(b)
        blocks = [s.at[at] for s in scores]
        cblock, sblock = cstat.at[at], sstat.at[at]
        for t in range(YB // 8):
            r8 = slice(t * 8, (t + 1) * 8)
            vals = [
                blocks[l // per][r8, (l % per) * 128 : (l % per + 1) * 128] + rfull[:, l * 128 : (l + 1) * 128]
                for l in range(NL)
            ]
            tops = vals
            while len(tops) > 1:
                tops = [jnp.maximum(tops[i], tops[i + 1]) for i in range(0, len(tops), 2)]
            top = tops[0]
            parts = [None] * 4
            for l in range(NL):
                p = jnp.exp2(vals[l] - top)
                blocks[l // per][r8, (l % per) * 128 : (l % per + 1) * 128] = p
                parts[l % 4] = p if l < 4 else parts[l % 4] + p
            cblock[r8] = top
            sblock[r8] = (parts[0] + parts[1]) + (parts[2] + parts[3])

    def col_stats(b):
        c = cstat[rows_of(b), :]
        best = jnp.max(c, axis=1, keepdims=True)
        summed = jnp.sum(sstat[rows_of(b), :] * jnp.exp2(c - best), axis=1, keepdims=True)
        return across(best), across(summed)

    def put_stats(ref, b, stats):
        ref[b, :, 0:YB] = stats[0]
        ref[b, :, YB:] = stats[1]

    def send_cols(b):
        dz, dc = b // 2, b % 2
        dst = ((NZ - dz) % NZ) * 2 + dc
        copy(col_stat_out.at[b], col_stat_in.at[dst], col_send.at[b], col_recv.at[dst], device(dz, 0, 0, dc)).start()

    def col_loop(b, carry):
        put_stats(col_stat_out, b - 1, col_stats(b - 1))
        col_tiles(b)
        send_cols(b - 1)
        return carry

    col_tiles(1)
    lax.fori_loop(2, NP, col_loop, 0)
    put_stats(col_stat_out, NP - 1, col_stats(NP - 1))
    col_tiles(0)
    send_cols(NP - 1)
    put_stats(col_stat_in, 0, col_stats(0))
    for k in range(1, NP):
        wait_in(col_stat_in, k, col_send, col_recv)
    col_lse = combined(col_stat_in, NP, YB)
    qbuf[0] = log_b * LOG2E - col_lse
    for dz, dc in line:
        s, d = yslot(dz, dc), yslot(-dz, dc)
        copy(qbuf.at[0], qbuf.at[d], q_send.at[s], q_recv.at[d], device(dz, 0, 0, dc)).start()
    col_out[...] = previous[...] + EPSILON * log_b - (EPSILON * LN2) * col_lse

    for b in range(NP):
        if b > 0:
            wait_in(qbuf, b, q_send, q_recv)
        at = slice(b * YB, (b + 1) * YB)
        cstat[at] = jnp.exp2(cstat[at] + jnp.sum(jnp.where(eye, qbuf[b], 0.0), axis=1, keepdims=True))

    def gap_loop(b, acc):
        at = rows_of(b)
        blocks = [s.at[at] for s in scores]
        gblock = cstat.at[at]
        for t in range(YB // 8):
            r8 = slice(t * 8, (t + 1) * 8)
            g = gblock[r8]
            acc = [acc[l] + blocks[l // per][r8, (l % per) * 128 : (l % per + 1) * 128] * g for l in range(NL)]
        return acc

    acc = lax.fori_loop(0, NP, gap_loop, [jnp.zeros((8, 128), F32) for _ in range(NL)])
    for k in range(NQ):
        for h in range(2):
            ref = w_in if k == 0 else w_out
            ref[k, :, h * 128 : (h + 1) * 128] = jnp.sum(acc[2 * k + h], axis=0, keepdims=True)
    for dy, dx in plane:
        s, d = xslot(dy, dx), xslot(-dy, -dx)
        copy(w_out.at[s], w_in.at[d], w_send.at[s], w_recv.at[d], device(0, dy, dx, 0)).start()

    for c in pending:
        c.wait_send()
    for k in range(1, NQ):
        wait_out(row_stat_out, k, row_send, row_recv)
        wait_out(rbuf, k, r_send, r_recv)
    for k in range(1, NP):
        wait_out(col_stat_out, k, col_send, col_recv)
        wait_out(qbuf, k, q_send, q_recv)

    for k in range(1, NQ):
        wait_in(w_in, k, w_send, w_recv)
    mass = functools.reduce(jnp.add, [w_in[k] for k in range(NQ)])
    gap_out[...] = jnp.log(mass) - log_a
    for k in range(1, NQ):
        wait_out(w_out, k, w_send, w_recv)


def body(measured, generated, previous, row_weight, col_weight):
    NQ = GRID["y"] * GRID["xh"] * GRID["xl"]
    NP = GRID["z"] * 2
    NJ, NI = NP * YB, NQ * XB
    dma = pltpu.SemaphoreType.DMA
    row, col, gap = pl.pallas_call(
        kernel,
        out_shape=(
            jax.ShapeDtypeStruct((1, XB), F32),
            jax.ShapeDtypeStruct((1, YB), F32),
            jax.ShapeDtypeStruct((1, XB), F32),
        ),
        in_specs=[pl.BlockSpec(memory_space=pltpu.HBM)] * 5,
        out_specs=(pl.BlockSpec(memory_space=pltpu.VMEM),) * 3,
        scratch_shapes=[
            pltpu.VMEM((DIM, XB), F32),
            pltpu.VMEM((DIM, YB), F32),
            pltpu.VMEM((1, YB), F32),
            pltpu.VMEM((1, XB), F32),
            pltpu.VMEM((1, YB), F32),
            pltpu.VMEM((NQ, DIM, XB), F32),
            pltpu.VMEM((NP, DIM + 8, YB), F32),
            pltpu.VMEM((NJ, 4 * DIM), BF16),
            pltpu.VMEM((NQ // 2, 4 * DIM, 2 * XB), BF16),
            pltpu.VMEM((NJ, 128), F32),
            pltpu.VMEM((NJ, 128), F32),
            pltpu.VMEM((NQ, 1, 2 * XB), F32),
            pltpu.VMEM((NQ, 1, 2 * XB), F32),
            pltpu.VMEM((NQ, 1, XB), F32),
            pltpu.VMEM((8, NI), F32),
            pltpu.VMEM((NP, 1, 2 * YB), F32),
            pltpu.VMEM((NP, 1, 2 * YB), F32),
            pltpu.VMEM((NP, 1, YB), F32),
            pltpu.VMEM((NQ, 1, XB), F32),
            pltpu.VMEM((NQ, 1, XB), F32),
            dma((5,)),
            dma((2 * NQ,)),
            dma((NQ, 2)),
            dma((NP,)),
            dma((NP,)),
            dma((NQ,)),
            dma((NQ,)),
            dma((NQ,)),
            dma((NQ,)),
            dma((NP,)),
            dma((NP,)),
            dma((NP,)),
            dma((NP,)),
            dma((NQ,)),
            dma((NQ,)),
            *[pltpu.VMEM((NJ, 2 * XB), F32) for _ in range(NQ // 2)],
        ],
        compiler_params=pltpu.CompilerParams(
            collective_id=0, has_side_effects=True, vmem_limit_bytes=48 * 1024 * 1024
        ),
    )(
        measured,
        generated,
        previous.reshape(1, YB),
        row_weight.reshape(1, XB),
        col_weight.reshape(1, YB),
    )
    return row.reshape(XB), col.reshape(YB), gap.reshape(XB)


def solution(mesh):
    placed = (
        P(None, ("row", "col")),
        P(None, ("col", "row")),
        P(("col", "row")),
        P(("row", "col")),
        P(("col", "row")),
    )
    return jax.shard_map(
        body,
        mesh=mesh,
        in_specs=placed,
        out_specs=(P(("row", "col")), P(("col", "row")), P(("row", "col"))),
        check_vma=False,
    )
```

```python
import functools
import math

import jax
import jax.numpy as jnp
from jax import lax
from jax.experimental import pallas as pl
from jax.experimental.pallas import tpu as pltpu
from jax.sharding import PartitionSpec as P

EPSILON = 0.1
LOG2E = 1.0 / math.log(2.0)
LN2 = math.log(2.0)
MESH = pl.DeviceIdType.MESH
F32 = jnp.float32
BF16 = jnp.bfloat16

GRID = {"z": 8, "y": 4, "xh": 2, "xl": 2}
XB = 256
YB = 128
DIM = 64
QUARTERS = 4


def kernel(
    measured_hbm,
    generated_hbm,
    previous_hbm,
    row_weight_hbm,
    col_weight_hbm,
    row_out,
    col_out,
    gap_out,
    measured,
    generated,
    previous,
    row_weight,
    col_weight,
    xraw,
    yraw,
    yt,
    xaug,
    cstat,
    sstat,
    row_stat_out,
    row_stat_in,
    rbuf,
    rfull,
    col_stat_out,
    col_stat_in,
    qbuf,
    w_out,
    w_in,
    in_sem,
    x_send,
    x_recv,
    y_send,
    y_recv,
    row_send,
    row_recv,
    r_send,
    r_recv,
    col_send,
    col_recv,
    q_send,
    q_recv,
    w_send,
    w_recv,
    *parts,
):
    NZ, NY, NXH, NXL = GRID["z"], GRID["y"], GRID["xh"], GRID["xl"]
    NX = NXH * NXL
    NQ, NP = NX * NY, NZ * 2
    NI = NQ * XB
    NL = NI // 128
    ndev = NQ * NP

    QR = NP * YB // QUARTERS
    quarter = [parts[h * (NQ // 2) : (h + 1) * (NQ // 2)] for h in range(QUARTERS + 1)]

    loads = [
        pltpu.make_async_copy(src, dst, in_sem.at[n])
        for n, (src, dst) in enumerate(
            [
                (generated_hbm, generated),
                (previous_hbm, previous),
                (col_weight_hbm, col_weight),
                (measured_hbm, measured),
                (row_weight_hbm, row_weight),
            ]
        )
    ]
    for c in loads:
        c.start()

    row = lax.axis_index("row")
    col = lax.axis_index("col")
    z = row // (NY * NXH)
    y = (row // NXH) % NY
    x = (row % NXH) * NXL + col // 2
    core = col % 2

    def device(dz, dy, dx, dc):
        zz, yy, xx = (z + dz) % NZ, (y + dy) % NY, (x + dx) % NX
        return ((zz * NY + yy) * NXH + xx // NXL, (xx % NXL) * 2 + (core + dc) % 2)

    def xslot(dy, dx):
        return (dy % NY) * NX + dx % NX

    def yslot(dz, dc):
        return (dz % NZ) * 2 + dc % 2

    def copy(src, dst, send, recv, dev):
        return pltpu.make_async_remote_copy(
            src_ref=src, dst_ref=dst, send_sem=send, recv_sem=recv, device_id=dev, device_id_type=MESH
        )

    def near_first(n):
        return sorted(range(1, n), key=lambda d: min(d, n - d))

    plane = [(dy, dx) for dy in range(NY) for dx in range(NX) if (dy, dx) != (0, 0)]
    line = [(dz, dc) for dz in range(NZ) for dc in range(2) if (dz, dc) != (0, 0)]

    barrier = pltpu.get_barrier_semaphore()
    for dy, dx in plane:
        pl.semaphore_signal(barrier, inc=1, device_id=device(0, dy, dx, 0), device_id_type=MESH)
    for dz, dc in line:
        pl.semaphore_signal(barrier, inc=1, device_id=device(dz, 0, 0, dc), device_id_type=MESH)

    for c in loads:
        c.wait()
    scale = 2.0 * LOG2E / EPSILON
    xraw[0] = measured[...] * scale
    gen = generated[...]
    log_b = jnp.log(col_weight[...]) - math.log(YB * ndev)
    ysq = jnp.sum(gen * gen, axis=0, keepdims=True)
    u = (log_b + (previous[...] - ysq) / EPSILON) * LOG2E
    yraw[0, 0:DIM] = gen
    yraw[0, DIM : DIM + 8] = jnp.broadcast_to(u, (8, YB))
    log_a = jnp.log(row_weight[...]) - math.log(XB * ndev)
    xsq = jnp.sum(measured[...] * measured[...], axis=0, keepdims=True)
    xaug[:, 3 * DIM :] = jnp.ones((NQ // 2, DIM, 2 * XB), BF16)

    pl.semaphore_wait(barrier, len(plane) + len(line))

    pending = []

    def start(c):
        c.start()
        pending.append(c)

    half = DIM // 2
    counter = [0]

    def send_x(slot, part, dst_slot, dev):
        at = pl.ds(part * half, half)
        n = counter[0]
        counter[0] += 1
        start(copy(xraw.at[slot, at], xraw.at[dst_slot, at], x_send.at[n], x_recv.at[dst_slot, part], dev))

    def wait_x(slot, part):
        at = pl.ds(part * half, half)
        copy(xraw.at[slot, at], xraw.at[slot, at], x_send.at[0], x_recv.at[slot, part], device(0, 0, 1, 0)).wait_recv()

    def send_y(n, slot, dst_slot, dev):
        start(copy(yraw.at[slot], yraw.at[dst_slot], y_send.at[n], y_recv.at[dst_slot], dev))

    def wait_y(slot):
        copy(yraw.at[slot], yraw.at[slot], y_send.at[0], y_recv.at[slot], device(0, 0, 0, 1)).wait_recv()

    for ez in near_first(NZ):
        send_y(ez, 0, yslot(-ez, 0), device(ez, 0, 0, 0))
    send_y(0, 0, yslot(0, 1), device(0, 0, 0, 1))
    for part in range(2):
        for e in near_first(max(NX, NY)):
            if e < NX:
                send_x(0, part, xslot(0, -e), device(0, 0, e, 0))
            if e < NY:
                send_x(0, 1 - part, xslot(-e, 0), device(0, e, 0, 0))

    def forward_x(d):
        if d < NX:
            wait_x(xslot(0, d), 0)
            for ey in near_first(NY):
                send_x(xslot(0, d), 0, xslot(-ey, d), device(0, ey, 0, 0))
        if d < NY:
            wait_x(xslot(d, 0), 1)
            for ex in near_first(NX):
                send_x(xslot(d, 0), 1, xslot(d, -ex), device(0, 0, ex, 0))

    def forward_y(dz):
        wait_y(yslot(dz, 0))
        send_y(NZ + dz, yslot(dz, 0), yslot(dz, 1), device(0, 0, 0, 1))

    def split(v):
        hi = v.astype(BF16).astype(F32)
        return hi, v - hi

    sub128 = lax.broadcasted_iota(jnp.int32, (8, YB), 0)

    def turn_y(slot):
        hi, lo = split(yraw[slot, 0:DIM])
        t1, rest = split(yraw[slot, DIM : DIM + 8])
        t2, t3 = split(rest)
        extra = jnp.where(sub128 == 0, t1, jnp.where(sub128 == 1, t2, jnp.where(sub128 == 2, t3, 0.0)))
        at = slice(slot * YB, (slot + 1) * YB)
        yt[at, 0 : 2 * DIM] = jnp.concatenate([hi, hi], axis=0).T.astype(BF16)
        yt[at, 2 * DIM :] = jnp.concatenate([lo, extra, jnp.zeros((DIM - 8, YB), F32)], axis=0).T.astype(BF16)

    def take_x(slot):
        v = xraw[slot]
        hi = v.astype(BF16)
        lo = (v - hi.astype(F32)).astype(BF16)
        at = slice((slot % 2) * XB, (slot % 2 + 1) * XB)
        xaug[slot // 2, 0:DIM, at] = hi
        xaug[slot // 2, DIM : 2 * DIM, at] = lo
        xaug[slot // 2, 2 * DIM : 3 * DIM, at] = hi

    waited = set()

    def ready_x(pair):
        for slot in (2 * pair, 2 * pair + 1):
            dy, dx = slot // NX, slot % NX
            for part in range(2):
                if slot > 0 and not (dy == 0 and part == 0) and not (dx == 0 and part == 1):
                    wait_x(slot, part)
            take_x(slot)

    CH = 2 * YB
    PW = 2 * XB

    def dot_stage(pair, c):
        for n in range(max(1, CH // QR)):
            size = min(CH, QR)
            r = c * CH + n * size
            quarter[r // QR][pair][r % QR : r % QR + size] = jnp.dot(
                yt[r : r + size], xaug[pair], preferred_element_type=F32
            )

    def rows8(pair, c, k):
        r = c * CH + k * 8
        return quarter[r // QR][pair][r % QR : r % QR + 8]

    def max_stage(pair, c, accs):
        accs = list(accs)
        for k in range(CH // 8):
            accs[k % 2] = jnp.maximum(accs[k % 2], rows8(pair, c, k))
        return accs

    def exp_stage(pair, c, top, accs):
        accs = list(accs)
        for k in range(CH // 8):
            accs[k % 2] = accs[k % 2] + jnp.exp2(rows8(pair, c, k) - top)
        return accs

    def finish_rows(pair, top, total):
        best = jnp.max(top, axis=0, keepdims=True)
        summed = jnp.sum(total * jnp.exp2(top - best), axis=0, keepdims=True)
        for h in range(2):
            slot = 2 * pair + h
            ref = row_stat_in if slot == 0 else row_stat_out
            ref[slot, :, 0:XB] = best[:, h * XB : (h + 1) * XB]
            ref[slot, :, XB:] = summed[:, h * XB : (h + 1) * XB]

    def send_rows(pair):
        for slot in (2 * pair, 2 * pair + 1):
            if slot > 0:
                dy, dx = slot // NX, slot % NX
                dst = xslot(-dy, -dx)
                copy(
                    row_stat_out.at[slot], row_stat_in.at[dst], row_send.at[slot], row_recv.at[dst], device(0, dy, dx, 0)
                ).start()

    for d in near_first(max(NX, NY))[:2]:
        forward_x(d)
    turn_y(0)
    order = [0] + near_first(NZ)
    late = near_first(max(NX, NY))[2:]
    lag = 2
    for n in range(NZ + lag):
        if 0 < n < NZ:
            forward_y(order[n])
            turn_y(yslot(order[n], 0))
        if n == 2:
            for d in late:
                forward_x(d)
            ready_x(0)
        if n >= lag:
            dz = order[n - lag]
            wait_y(yslot(dz, 1))
            turn_y(yslot(dz, 1))
            dot_stage(0, dz)

    near = lambda dy: min(dy, NY - dy)
    pairs = sorted(range(NQ // 2), key=lambda p: (near(2 * p // NX), p))
    state = {}
    for step in range(1, len(pairs) + 3):
        one = pairs[step] if step < len(pairs) else None
        two = pairs[step - 1] if 0 <= step - 1 < len(pairs) else None
        three = pairs[step - 2] if 0 <= step - 2 < len(pairs) else None
        if step >= 4:
            send_rows(pairs[step - 4])
        if one is not None:
            ready_x(one)
        tops = [jnp.full((8, PW), -3e38, F32)] * 2
        sums = [jnp.zeros((8, PW), F32)] * 2
        for c in range(NZ):
            if one is not None:
                dot_stage(one, c)
            if two is not None:
                tops = max_stage(two, c, tops)
            if three is not None:
                sums = exp_stage(three, c, state[three], sums)
        if step >= 3 and step - 3 < len(pairs):
            finish_rows(*state.pop("done"))
        if two is not None:
            state[two] = jnp.maximum(*tops)
        if three is not None:
            state["done"] = (three, state.pop(three), sums[0] + sums[1])
    send_rows(pairs[-1])

    def wait_in(buf, slot, send, recv):
        copy(buf.at[slot], buf.at[slot], send.at[slot], recv.at[slot], device(0, 0, 1, 0)).wait_recv()

    def wait_out(buf, slot, send, recv):
        copy(buf.at[slot], buf.at[slot], send.at[slot], recv.at[slot], device(0, 0, 1, 0)).wait_send()

    for k in range(1, NQ):
        wait_in(row_stat_in, k, row_send, row_recv)

    def combined(ref, n, width):
        tops = [ref[k, :, 0:width] for k in range(n)]
        best = functools.reduce(jnp.maximum, tops)
        summed = functools.reduce(jnp.add, [ref[k, :, width:] * jnp.exp2(tops[k] - best) for k in range(n)])
        return best + jnp.log(summed) * LOG2E

    row_lse = combined(row_stat_in, NQ, XB)
    rbuf[0] = log_a * LOG2E - row_lse
    for dy, dx in plane:
        s, d = xslot(dy, dx), xslot(-dy, -dx)
        copy(rbuf.at[0], rbuf.at[d], r_send.at[s], r_recv.at[d], device(0, dy, dx, 0)).start()
    row_out[...] = xsq - (EPSILON * LN2) * row_lse
    for k in range(1, NQ):
        wait_in(rbuf, k, r_send, r_recv)
    for k in range(NQ):
        rfull[:, k * XB : (k + 1) * XB] = jnp.broadcast_to(rbuf[k], (8, XB))

    eye = lax.broadcasted_iota(jnp.int32, (YB, YB), 0) == lax.broadcasted_iota(jnp.int32, (YB, YB), 1)
    per = PW // 128

    def across(v):
        return jnp.sum(jnp.where(eye, v, 0.0), axis=0, keepdims=True)

    def rows_of(b):
        return pl.ds(pl.multiple_of(b * YB, YB), YB)

    BQ = QR // YB

    def tiles_of(h, b):
        at = pl.ds(pl.multiple_of((b - h * BQ) * YB, YB), YB)
        return [s.at[at] for s in quarter[h]]

    def col_tiles(h, b):
        blocks, puts = tiles_of(h, b), [s.at[pl.ds(pl.multiple_of((b - h * BQ) * YB, YB), YB)] for s in quarter[h - 1]]
        cblock, sblock = cstat.at[rows_of(b)], sstat.at[rows_of(b)]
        for t in range(YB // 8):
            r8 = slice(t * 8, (t + 1) * 8)
            vals = [
                blocks[l // per][r8, (l % per) * 128 : (l % per + 1) * 128] + rfull[:, l * 128 : (l + 1) * 128]
                for l in range(NL)
            ]
            tops = vals
            while len(tops) > 1:
                tops = [jnp.maximum(tops[i], tops[i + 1]) for i in range(0, len(tops), 2)]
            top = tops[0]
            sums = [None] * 4
            for l in range(NL):
                e = jnp.exp2(vals[l] - top)
                puts[l // per][r8, (l % per) * 128 : (l % per + 1) * 128] = e
                sums[l % 4] = e if l < 4 else sums[l % 4] + e
            cblock[r8] = top
            sblock[r8] = (sums[0] + sums[1]) + (sums[2] + sums[3])

    def col_stats(b):
        c = cstat[rows_of(b), :]
        best = jnp.max(c, axis=1, keepdims=True)
        summed = jnp.sum(sstat[rows_of(b), :] * jnp.exp2(c - best), axis=1, keepdims=True)
        return across(best), across(summed)

    def put_stats(ref, b, stats):
        ref[b, :, 0:YB] = stats[0]
        ref[b, :, YB:] = stats[1]

    def send_cols(b):
        dz, dc = b // 2, b % 2
        dst = ((NZ - dz) % NZ) * 2 + dc
        copy(col_stat_out.at[b], col_stat_in.at[dst], col_send.at[b], col_recv.at[dst], device(dz, 0, 0, dc)).start()

    def col_loop(h):
        def step(b, carry):
            put_stats(col_stat_out, b - 1, col_stats(b - 1))
            col_tiles(h, b)
            send_cols(b - 1)
            return carry

        return step

    col_tiles(0, 0)
    put_stats(col_stat_in, 0, col_stats(0))
    for h in range(QUARTERS):
        if h == 0:
            if BQ > 1:
                col_tiles(0, 1)
            lax.fori_loop(2, BQ, col_loop(0), 0)
        elif h == 1 and BQ == 1:
            col_tiles(1, 1)
        else:
            lax.fori_loop(h * BQ, (h + 1) * BQ, col_loop(h), 0)
    put_stats(col_stat_out, NP - 1, col_stats(NP - 1))
    send_cols(NP - 1)
    for k in range(1, NP):
        wait_in(col_stat_in, k, col_send, col_recv)
    col_lse = combined(col_stat_in, NP, YB)
    qbuf[0] = log_b * LOG2E - col_lse
    for dz, dc in line:
        s, d = yslot(dz, dc), yslot(-dz, dc)
        copy(qbuf.at[0], qbuf.at[d], q_send.at[s], q_recv.at[d], device(dz, 0, 0, dc)).start()
    col_out[...] = previous[...] + EPSILON * log_b - (EPSILON * LN2) * col_lse

    for b in range(NP):
        if b > 0:
            wait_in(qbuf, b, q_send, q_recv)
        at = slice(b * YB, (b + 1) * YB)
        cstat[at] = jnp.exp2(cstat[at] + jnp.sum(jnp.where(eye, qbuf[b], 0.0), axis=1, keepdims=True))

    def gap_loop(h):
        def step(b, acc):
            at = pl.ds(pl.multiple_of((b - h * BQ) * YB, YB), YB)
            blocks = [s.at[at] for s in quarter[h - 1]]
            gblock = cstat.at[rows_of(b)]
            for t in range(YB // 8):
                r8 = slice(t * 8, (t + 1) * 8)
                g = gblock[r8]
                acc = [acc[l] + blocks[l // per][r8, (l % per) * 128 : (l % per + 1) * 128] * g for l in range(NL)]
            return acc

        return step

    acc = [jnp.zeros((8, 128), F32) for _ in range(NL)]
    for h in range(QUARTERS):
        acc = lax.fori_loop(h * BQ, (h + 1) * BQ, gap_loop(h), acc)
    for k in range(NQ):
        for h in range(2):
            ref = w_in if k == 0 else w_out
            ref[k, :, h * 128 : (h + 1) * 128] = jnp.sum(acc[2 * k + h], axis=0, keepdims=True)
    for dy, dx in plane:
        s, d = xslot(dy, dx), xslot(-dy, -dx)
        copy(w_out.at[s], w_in.at[d], w_send.at[s], w_recv.at[d], device(0, dy, dx, 0)).start()

    for c in pending:
        c.wait_send()
    for k in range(1, NQ):
        wait_out(row_stat_out, k, row_send, row_recv)
        wait_out(rbuf, k, r_send, r_recv)
    for k in range(1, NP):
        wait_out(col_stat_out, k, col_send, col_recv)
        wait_out(qbuf, k, q_send, q_recv)

    for k in range(1, NQ):
        wait_in(w_in, k, w_send, w_recv)
    mass = functools.reduce(jnp.add, [w_in[k] for k in range(NQ)])
    gap_out[...] = jnp.log(mass) - log_a
    for k in range(1, NQ):
        wait_out(w_out, k, w_send, w_recv)


def put_results(row, col, gap, row_out, col_out, gap_out, sem):
    copies = [
        pltpu.make_async_copy(src, dst, sem.at[n])
        for n, (src, dst) in enumerate([(row, row_out), (col, col_out), (gap, gap_out)])
    ]
    for c in copies:
        c.start()
    for c in copies:
        c.wait()


def body(measured, generated, previous, row_weight, col_weight):
    NQ = GRID["y"] * GRID["xh"] * GRID["xl"]
    NP = GRID["z"] * 2
    NJ, NI = NP * YB, NQ * XB
    dma = pltpu.SemaphoreType.DMA
    row, col, gap = pl.pallas_call(
        kernel,
        out_shape=(
            jax.ShapeDtypeStruct((1, XB), F32),
            jax.ShapeDtypeStruct((1, YB), F32),
            jax.ShapeDtypeStruct((1, XB), F32),
        ),
        in_specs=[pl.BlockSpec(memory_space=pltpu.HBM)] * 5,
        out_specs=(pl.BlockSpec(memory_space=pltpu.VMEM),) * 3,
        scratch_shapes=[
            pltpu.VMEM((DIM, XB), F32),
            pltpu.VMEM((DIM, YB), F32),
            pltpu.VMEM((1, YB), F32),
            pltpu.VMEM((1, XB), F32),
            pltpu.VMEM((1, YB), F32),
            pltpu.VMEM((NQ, DIM, XB), F32),
            pltpu.VMEM((NP, DIM + 8, YB), F32),
            pltpu.VMEM((NJ, 4 * DIM), BF16),
            pltpu.VMEM((NQ // 2, 4 * DIM, 2 * XB), BF16),
            pltpu.VMEM((NJ, 128), F32),
            pltpu.VMEM((NJ, 128), F32),
            pltpu.VMEM((NQ, 1, 2 * XB), F32),
            pltpu.VMEM((NQ, 1, 2 * XB), F32),
            pltpu.VMEM((NQ, 1, XB), F32),
            pltpu.VMEM((8, NI), F32),
            pltpu.VMEM((NP, 1, 2 * YB), F32),
            pltpu.VMEM((NP, 1, 2 * YB), F32),
            pltpu.VMEM((NP, 1, YB), F32),
            pltpu.VMEM((NQ, 1, XB), F32),
            pltpu.VMEM((NQ, 1, XB), F32),
            dma((5,)),
            dma((2 * NQ,)),
            dma((NQ, 2)),
            dma((NP,)),
            dma((NP,)),
            dma((NQ,)),
            dma((NQ,)),
            dma((NQ,)),
            dma((NQ,)),
            dma((NP,)),
            dma((NP,)),
            dma((NP,)),
            dma((NP,)),
            dma((NQ,)),
            dma((NQ,)),
            *[pltpu.VMEM((NJ // QUARTERS, 2 * XB), F32) for _ in range((QUARTERS + 1) * (NQ // 2))],
        ],
        compiler_params=pltpu.CompilerParams(
            collective_id=0, has_side_effects=True, vmem_limit_bytes=50 * 1024 * 1024
        ),
    )(
        *[
            pltpu.with_memory_space_constraint(v, pltpu.HBM)
            for v in (
                measured,
                generated,
                previous.reshape(1, YB),
                row_weight.reshape(1, XB),
                col_weight.reshape(1, YB),
            )
        ]
    )
    row, col, gap = pl.pallas_call(
        put_results,
        out_shape=(
            jax.ShapeDtypeStruct((1, XB), F32),
            jax.ShapeDtypeStruct((1, YB), F32),
            jax.ShapeDtypeStruct((1, XB), F32),
        ),
        in_specs=[pl.BlockSpec(memory_space=pltpu.VMEM)] * 3,
        out_specs=(pl.BlockSpec(memory_space=pl.ANY),) * 3,
        scratch_shapes=[dma((3,))],
        compiler_params=pltpu.CompilerParams(vmem_limit_bytes=1024 * 1024),
    )(row, col, gap)
    return row.reshape(XB), col.reshape(YB), gap.reshape(XB)


def solution(mesh):
    placed = (
        P(None, ("row", "col")),
        P(None, ("col", "row")),
        P(("col", "row")),
        P(("row", "col")),
        P(("col", "row")),
    )
    return jax.shard_map(
        body,
        mesh=mesh,
        in_specs=placed,
        out_specs=(P(("row", "col")), P(("col", "row")), P(("row", "col"))),
        check_vma=False,
    )
```

```python
import functools
import math

import jax
import jax.numpy as jnp
from jax import lax
from jax.experimental import pallas as pl
from jax.experimental.pallas import tpu as pltpu
from jax.sharding import PartitionSpec as P

EPSILON = 0.1
LOG2E = 1.0 / math.log(2.0)
LN2 = math.log(2.0)
MESH = pl.DeviceIdType.MESH
F32 = jnp.float32
BF16 = jnp.bfloat16

GRID = {"z": 8, "y": 4, "xh": 2, "xl": 2}
XB = 256
YB = 128
DIM = 64
QUARTERS = 4


ROOT = (
    0.9999999403953552,
    0.010830347426235676,
    5.863578917342238e-05,
    2.108754131313617e-07,
    5.476839537443823e-10,
    8.743147807306617e-13,
)


def power(x):
    x = jnp.maximum(x, -64.0)
    p = jnp.full_like(x, ROOT[-1])
    for c in ROOT[-2::-1]:
        p = p * x + c
    for _ in range(6):
        p = p * p
    return p


def exp2(x, n):
    return power(x) if n % 8 in (1, 4, 6) else jnp.exp2(x)


def kernel(
    measured_hbm,
    generated_hbm,
    previous_hbm,
    row_weight_hbm,
    col_weight_hbm,
    row_out,
    col_out,
    gap_out,
    measured,
    generated,
    previous,
    row_weight,
    col_weight,
    xraw,
    yraw,
    yt,
    xaug,
    cstat,
    sstat,
    row_stat_out,
    row_stat_in,
    rbuf,
    rfull,
    col_stat_out,
    col_stat_in,
    qbuf,
    w_out,
    w_in,
    in_sem,
    x_send,
    x_recv,
    y_send,
    y_recv,
    row_send,
    row_recv,
    r_send,
    r_recv,
    col_send,
    col_recv,
    q_send,
    q_recv,
    w_send,
    w_recv,
    *parts,
):
    NZ, NY, NXH, NXL = GRID["z"], GRID["y"], GRID["xh"], GRID["xl"]
    NX = NXH * NXL
    NQ, NP = NX * NY, NZ * 2
    NI = NQ * XB
    NL = NI // 128
    ndev = NQ * NP

    QR = NP * YB // QUARTERS
    quarter = [parts[h * (NQ // 2) : (h + 1) * (NQ // 2)] for h in range(QUARTERS + 1)]

    loads = [
        pltpu.make_async_copy(src, dst, in_sem.at[n])
        for n, (src, dst) in enumerate(
            [
                (generated_hbm, generated),
                (previous_hbm, previous),
                (col_weight_hbm, col_weight),
                (measured_hbm, measured),
                (row_weight_hbm, row_weight),
            ]
        )
    ]
    for c in loads:
        c.start()

    row = lax.axis_index("row")
    col = lax.axis_index("col")
    z = row // (NY * NXH)
    y = (row // NXH) % NY
    x = (row % NXH) * NXL + col // 2
    core = col % 2

    def device(dz, dy, dx, dc):
        zz, yy, xx = (z + dz) % NZ, (y + dy) % NY, (x + dx) % NX
        return ((zz * NY + yy) * NXH + xx // NXL, (xx % NXL) * 2 + (core + dc) % 2)

    def xslot(dy, dx):
        return (dy % NY) * NX + dx % NX

    def yslot(dz, dc):
        return (dz % NZ) * 2 + dc % 2

    def copy(src, dst, send, recv, dev):
        return pltpu.make_async_remote_copy(
            src_ref=src, dst_ref=dst, send_sem=send, recv_sem=recv, device_id=dev, device_id_type=MESH
        )

    def near_first(n):
        return sorted(range(1, n), key=lambda d: min(d, n - d))

    plane = [(dy, dx) for dy in range(NY) for dx in range(NX) if (dy, dx) != (0, 0)]
    line = [(dz, dc) for dz in range(NZ) for dc in range(2) if (dz, dc) != (0, 0)]

    barrier = pltpu.get_barrier_semaphore()
    for dy, dx in plane:
        pl.semaphore_signal(barrier, inc=1, device_id=device(0, dy, dx, 0), device_id_type=MESH)
    for dz, dc in line:
        pl.semaphore_signal(barrier, inc=1, device_id=device(dz, 0, 0, dc), device_id_type=MESH)

    for c in loads:
        c.wait()
    scale = 2.0 * LOG2E / EPSILON
    xraw[0] = measured[...] * scale
    gen = generated[...]
    log_b = jnp.log(col_weight[...]) - math.log(YB * ndev)
    ysq = jnp.sum(gen * gen, axis=0, keepdims=True)
    u = (log_b + (previous[...] - ysq) / EPSILON) * LOG2E
    yraw[0, 0:DIM] = gen
    yraw[0, DIM : DIM + 8] = jnp.broadcast_to(u, (8, YB))
    log_a = jnp.log(row_weight[...]) - math.log(XB * ndev)
    xsq = jnp.sum(measured[...] * measured[...], axis=0, keepdims=True)
    xaug[:, 3 * DIM :] = jnp.ones((NQ // 2, DIM, 2 * XB), BF16)

    pl.semaphore_wait(barrier, len(plane) + len(line))

    pending = []

    def start(c):
        c.start()
        pending.append(c)

    half = DIM // 2
    counter = [0]

    def send_x(slot, part, dst_slot, dev):
        at = pl.ds(part * half, half)
        n = counter[0]
        counter[0] += 1
        start(copy(xraw.at[slot, at], xraw.at[dst_slot, at], x_send.at[n], x_recv.at[dst_slot, part], dev))

    def wait_x(slot, part):
        at = pl.ds(part * half, half)
        copy(xraw.at[slot, at], xraw.at[slot, at], x_send.at[0], x_recv.at[slot, part], device(0, 0, 1, 0)).wait_recv()

    def send_y(n, slot, dst_slot, dev):
        start(copy(yraw.at[slot], yraw.at[dst_slot], y_send.at[n], y_recv.at[dst_slot], dev))

    def wait_y(slot):
        copy(yraw.at[slot], yraw.at[slot], y_send.at[0], y_recv.at[slot], device(0, 0, 0, 1)).wait_recv()

    for ez in near_first(NZ):
        send_y(ez, 0, yslot(-ez, 0), device(ez, 0, 0, 0))
    send_y(0, 0, yslot(0, 1), device(0, 0, 0, 1))
    for part in range(2):
        for e in near_first(max(NX, NY)):
            if e < NX:
                send_x(0, part, xslot(0, -e), device(0, 0, e, 0))
            if e < NY:
                send_x(0, 1 - part, xslot(-e, 0), device(0, e, 0, 0))

    def forward_x(d):
        if d < NX:
            wait_x(xslot(0, d), 0)
            for ey in near_first(NY):
                send_x(xslot(0, d), 0, xslot(-ey, d), device(0, ey, 0, 0))
        if d < NY:
            wait_x(xslot(d, 0), 1)
            for ex in near_first(NX):
                send_x(xslot(d, 0), 1, xslot(d, -ex), device(0, 0, ex, 0))

    def forward_y(dz):
        wait_y(yslot(dz, 0))
        send_y(NZ + dz, yslot(dz, 0), yslot(dz, 1), device(0, 0, 0, 1))

    def split(v):
        hi = v.astype(BF16).astype(F32)
        return hi, v - hi

    sub128 = lax.broadcasted_iota(jnp.int32, (8, YB), 0)

    def turn_y(slot):
        hi, lo = split(yraw[slot, 0:DIM])
        t1, rest = split(yraw[slot, DIM : DIM + 8])
        t2, t3 = split(rest)
        extra = jnp.where(sub128 == 0, t1, jnp.where(sub128 == 1, t2, jnp.where(sub128 == 2, t3, 0.0)))
        at = slice(slot * YB, (slot + 1) * YB)
        yt[at, 0 : 2 * DIM] = jnp.concatenate([hi, hi], axis=0).T.astype(BF16)
        yt[at, 2 * DIM :] = jnp.concatenate([lo, extra, jnp.zeros((DIM - 8, YB), F32)], axis=0).T.astype(BF16)

    def take_x(slot):
        v = xraw[slot]
        hi = v.astype(BF16)
        lo = (v - hi.astype(F32)).astype(BF16)
        at = slice((slot % 2) * XB, (slot % 2 + 1) * XB)
        xaug[slot // 2, 0:DIM, at] = hi
        xaug[slot // 2, DIM : 2 * DIM, at] = lo
        xaug[slot // 2, 2 * DIM : 3 * DIM, at] = hi

    waited = set()

    def ready_x(pair):
        for slot in (2 * pair, 2 * pair + 1):
            dy, dx = slot // NX, slot % NX
            for part in range(2):
                if slot > 0 and not (dy == 0 and part == 0) and not (dx == 0 and part == 1):
                    wait_x(slot, part)
            take_x(slot)

    CH = 2 * YB
    PW = 2 * XB

    def dot_stage(pair, c):
        for n in range(max(1, CH // QR)):
            size = min(CH, QR)
            r = c * CH + n * size
            quarter[r // QR][pair][r % QR : r % QR + size] = jnp.dot(
                yt[r : r + size], xaug[pair], preferred_element_type=F32
            )

    def rows8(pair, c, k):
        r = c * CH + k * 8
        return quarter[r // QR][pair][r % QR : r % QR + 8]

    def max_stage(pair, c, accs):
        accs = list(accs)
        for k in range(CH // 8):
            accs[k % 2] = jnp.maximum(accs[k % 2], rows8(pair, c, k))
        return accs

    def exp_stage(pair, c, top, accs):
        accs = list(accs)
        for k in range(CH // 8):
            accs[k % 2] = accs[k % 2] + exp2(rows8(pair, c, k) - top, k)
        return accs

    def finish_rows(pair, top, total):
        best = jnp.max(top, axis=0, keepdims=True)
        summed = jnp.sum(total * jnp.exp2(top - best), axis=0, keepdims=True)
        for h in range(2):
            slot = 2 * pair + h
            ref = row_stat_in if slot == 0 else row_stat_out
            ref[slot, :, 0:XB] = best[:, h * XB : (h + 1) * XB]
            ref[slot, :, XB:] = summed[:, h * XB : (h + 1) * XB]

    def send_rows(pair):
        for slot in (2 * pair, 2 * pair + 1):
            if slot > 0:
                dy, dx = slot // NX, slot % NX
                dst = xslot(-dy, -dx)
                copy(
                    row_stat_out.at[slot], row_stat_in.at[dst], row_send.at[slot], row_recv.at[dst], device(0, dy, dx, 0)
                ).start()

    for d in near_first(max(NX, NY))[:2]:
        forward_x(d)
    turn_y(0)
    order = [0] + near_first(NZ)
    late = near_first(max(NX, NY))[2:]
    lag = 2
    for n in range(NZ + lag):
        if 0 < n < NZ:
            forward_y(order[n])
            turn_y(yslot(order[n], 0))
        if n == 2:
            for d in late:
                forward_x(d)
            ready_x(0)
        if n >= lag:
            dz = order[n - lag]
            wait_y(yslot(dz, 1))
            turn_y(yslot(dz, 1))
            dot_stage(0, dz)

    near = lambda dy: min(dy, NY - dy)
    pairs = sorted(range(NQ // 2), key=lambda p: (near(2 * p // NX), p))
    state = {}
    for step in range(1, len(pairs) + 3):
        one = pairs[step] if step < len(pairs) else None
        two = pairs[step - 1] if 0 <= step - 1 < len(pairs) else None
        three = pairs[step - 2] if 0 <= step - 2 < len(pairs) else None
        if step >= 4:
            send_rows(pairs[step - 4])
        if one is not None:
            ready_x(one)
        tops = [jnp.full((8, PW), -3e38, F32)] * 2
        sums = [jnp.zeros((8, PW), F32)] * 2
        for c in range(NZ):
            if one is not None:
                dot_stage(one, c)
            if two is not None:
                tops = max_stage(two, c, tops)
            if three is not None:
                sums = exp_stage(three, c, state[three], sums)
        if step >= 3 and step - 3 < len(pairs):
            finish_rows(*state.pop("done"))
        if two is not None:
            state[two] = jnp.maximum(*tops)
        if three is not None:
            state["done"] = (three, state.pop(three), sums[0] + sums[1])
    send_rows(pairs[-1])

    def wait_in(buf, slot, send, recv):
        copy(buf.at[slot], buf.at[slot], send.at[slot], recv.at[slot], device(0, 0, 1, 0)).wait_recv()

    def wait_out(buf, slot, send, recv):
        copy(buf.at[slot], buf.at[slot], send.at[slot], recv.at[slot], device(0, 0, 1, 0)).wait_send()

    for k in range(1, NQ):
        wait_in(row_stat_in, k, row_send, row_recv)

    def combined(ref, n, width):
        tops = [ref[k, :, 0:width] for k in range(n)]
        best = functools.reduce(jnp.maximum, tops)
        summed = functools.reduce(jnp.add, [ref[k, :, width:] * jnp.exp2(tops[k] - best) for k in range(n)])
        return best + jnp.log(summed) * LOG2E

    row_lse = combined(row_stat_in, NQ, XB)
    rbuf[0] = log_a * LOG2E - row_lse
    for dy, dx in plane:
        s, d = xslot(dy, dx), xslot(-dy, -dx)
        copy(rbuf.at[0], rbuf.at[d], r_send.at[s], r_recv.at[d], device(0, dy, dx, 0)).start()
    row_out[...] = xsq - (EPSILON * LN2) * row_lse
    for k in range(1, NQ):
        wait_in(rbuf, k, r_send, r_recv)
    for k in range(NQ):
        rfull[:, k * XB : (k + 1) * XB] = jnp.broadcast_to(rbuf[k], (8, XB))

    eye = lax.broadcasted_iota(jnp.int32, (YB, YB), 0) == lax.broadcasted_iota(jnp.int32, (YB, YB), 1)
    per = PW // 128

    def across(v):
        return jnp.sum(jnp.where(eye, v, 0.0), axis=0, keepdims=True)

    def rows_of(b):
        return pl.ds(pl.multiple_of(b * YB, YB), YB)

    BQ = QR // YB

    def tiles_of(h, b):
        at = pl.ds(pl.multiple_of((b - h * BQ) * YB, YB), YB)
        return [s.at[at] for s in quarter[h]]

    def col_tiles(h, b):
        blocks, puts = tiles_of(h, b), [s.at[pl.ds(pl.multiple_of((b - h * BQ) * YB, YB), YB)] for s in quarter[h - 1]]
        cblock, sblock = cstat.at[rows_of(b)], sstat.at[rows_of(b)]
        for t in range(YB // 8):
            r8 = slice(t * 8, (t + 1) * 8)
            vals = [
                blocks[l // per][r8, (l % per) * 128 : (l % per + 1) * 128] + rfull[:, l * 128 : (l + 1) * 128]
                for l in range(NL)
            ]
            tops = vals
            while len(tops) > 1:
                tops = [jnp.maximum(tops[i], tops[i + 1]) for i in range(0, len(tops), 2)]
            top = tops[0]
            sums = [None] * 4
            for l in range(NL):
                e = exp2(vals[l] - top, l)
                puts[l // per][r8, (l % per) * 128 : (l % per + 1) * 128] = e
                sums[l % 4] = e if l < 4 else sums[l % 4] + e
            cblock[r8] = top
            sblock[r8] = (sums[0] + sums[1]) + (sums[2] + sums[3])

    def col_stats(b):
        c = cstat[rows_of(b), :]
        best = jnp.max(c, axis=1, keepdims=True)
        summed = jnp.sum(sstat[rows_of(b), :] * jnp.exp2(c - best), axis=1, keepdims=True)
        return across(best), across(summed)

    def put_stats(ref, b, stats):
        ref[b, :, 0:YB] = stats[0]
        ref[b, :, YB:] = stats[1]

    def send_cols(b):
        dz, dc = b // 2, b % 2
        dst = ((NZ - dz) % NZ) * 2 + dc
        copy(col_stat_out.at[b], col_stat_in.at[dst], col_send.at[b], col_recv.at[dst], device(dz, 0, 0, dc)).start()

    def col_loop(h):
        def step(b, carry):
            put_stats(col_stat_out, b - 1, col_stats(b - 1))
            col_tiles(h, b)
            send_cols(b - 1)
            return carry

        return step

    col_tiles(0, 0)
    put_stats(col_stat_in, 0, col_stats(0))
    for h in range(QUARTERS):
        if h == 0:
            if BQ > 1:
                col_tiles(0, 1)
            lax.fori_loop(2, BQ, col_loop(0), 0)
        elif h == 1 and BQ == 1:
            col_tiles(1, 1)
        else:
            lax.fori_loop(h * BQ, (h + 1) * BQ, col_loop(h), 0)
    put_stats(col_stat_out, NP - 1, col_stats(NP - 1))
    send_cols(NP - 1)
    for k in range(1, NP):
        wait_in(col_stat_in, k, col_send, col_recv)
    col_lse = combined(col_stat_in, NP, YB)
    qbuf[0] = log_b * LOG2E - col_lse
    for dz, dc in line:
        s, d = yslot(dz, dc), yslot(-dz, dc)
        copy(qbuf.at[0], qbuf.at[d], q_send.at[s], q_recv.at[d], device(dz, 0, 0, dc)).start()
    col_out[...] = previous[...] + EPSILON * log_b - (EPSILON * LN2) * col_lse

    for b in range(NP):
        if b > 0:
            wait_in(qbuf, b, q_send, q_recv)
        at = slice(b * YB, (b + 1) * YB)
        cstat[at] = jnp.exp2(cstat[at] + jnp.sum(jnp.where(eye, qbuf[b], 0.0), axis=1, keepdims=True))

    def gap_loop(h):
        def step(b, acc):
            at = pl.ds(pl.multiple_of((b - h * BQ) * YB, YB), YB)
            blocks = [s.at[at] for s in quarter[h - 1]]
            gblock = cstat.at[rows_of(b)]
            for t in range(YB // 8):
                r8 = slice(t * 8, (t + 1) * 8)
                g = gblock[r8]
                acc = [acc[l] + blocks[l // per][r8, (l % per) * 128 : (l % per + 1) * 128] * g for l in range(NL)]
            return acc

        return step

    acc = [jnp.zeros((8, 128), F32) for _ in range(NL)]
    for h in range(QUARTERS):
        acc = lax.fori_loop(h * BQ, (h + 1) * BQ, gap_loop(h), acc)
    for k in range(NQ):
        for h in range(2):
            ref = w_in if k == 0 else w_out
            ref[k, :, h * 128 : (h + 1) * 128] = jnp.sum(acc[2 * k + h], axis=0, keepdims=True)
    for dy, dx in plane:
        s, d = xslot(dy, dx), xslot(-dy, -dx)
        copy(w_out.at[s], w_in.at[d], w_send.at[s], w_recv.at[d], device(0, dy, dx, 0)).start()

    for c in pending:
        c.wait_send()
    for k in range(1, NQ):
        wait_out(row_stat_out, k, row_send, row_recv)
        wait_out(rbuf, k, r_send, r_recv)
    for k in range(1, NP):
        wait_out(col_stat_out, k, col_send, col_recv)
        wait_out(qbuf, k, q_send, q_recv)

    for k in range(1, NQ):
        wait_in(w_in, k, w_send, w_recv)
    mass = functools.reduce(jnp.add, [w_in[k] for k in range(NQ)])
    gap_out[...] = jnp.log(mass) - log_a
    for k in range(1, NQ):
        wait_out(w_out, k, w_send, w_recv)


def put_results(row, col, gap, row_out, col_out, gap_out, sem):
    copies = [
        pltpu.make_async_copy(src, dst, sem.at[n])
        for n, (src, dst) in enumerate([(row, row_out), (col, col_out), (gap, gap_out)])
    ]
    for c in copies:
        c.start()
    for c in copies:
        c.wait()


def body(measured, generated, previous, row_weight, col_weight):
    NQ = GRID["y"] * GRID["xh"] * GRID["xl"]
    NP = GRID["z"] * 2
    NJ, NI = NP * YB, NQ * XB
    dma = pltpu.SemaphoreType.DMA
    row, col, gap = pl.pallas_call(
        kernel,
        out_shape=(
            jax.ShapeDtypeStruct((1, XB), F32),
            jax.ShapeDtypeStruct((1, YB), F32),
            jax.ShapeDtypeStruct((1, XB), F32),
        ),
        in_specs=[pl.BlockSpec(memory_space=pltpu.HBM)] * 5,
        out_specs=(pl.BlockSpec(memory_space=pltpu.VMEM),) * 3,
        scratch_shapes=[
            pltpu.VMEM((DIM, XB), F32),
            pltpu.VMEM((DIM, YB), F32),
            pltpu.VMEM((1, YB), F32),
            pltpu.VMEM((1, XB), F32),
            pltpu.VMEM((1, YB), F32),
            pltpu.VMEM((NQ, DIM, XB), F32),
            pltpu.VMEM((NP, DIM + 8, YB), F32),
            pltpu.VMEM((NJ, 4 * DIM), BF16),
            pltpu.VMEM((NQ // 2, 4 * DIM, 2 * XB), BF16),
            pltpu.VMEM((NJ, 128), F32),
            pltpu.VMEM((NJ, 128), F32),
            pltpu.VMEM((NQ, 1, 2 * XB), F32),
            pltpu.VMEM((NQ, 1, 2 * XB), F32),
            pltpu.VMEM((NQ, 1, XB), F32),
            pltpu.VMEM((8, NI), F32),
            pltpu.VMEM((NP, 1, 2 * YB), F32),
            pltpu.VMEM((NP, 1, 2 * YB), F32),
            pltpu.VMEM((NP, 1, YB), F32),
            pltpu.VMEM((NQ, 1, XB), F32),
            pltpu.VMEM((NQ, 1, XB), F32),
            dma((5,)),
            dma((2 * NQ,)),
            dma((NQ, 2)),
            dma((NP,)),
            dma((NP,)),
            dma((NQ,)),
            dma((NQ,)),
            dma((NQ,)),
            dma((NQ,)),
            dma((NP,)),
            dma((NP,)),
            dma((NP,)),
            dma((NP,)),
            dma((NQ,)),
            dma((NQ,)),
            *[pltpu.VMEM((NJ // QUARTERS, 2 * XB), F32) for _ in range((QUARTERS + 1) * (NQ // 2))],
        ],
        compiler_params=pltpu.CompilerParams(
            collective_id=0, has_side_effects=True, vmem_limit_bytes=50 * 1024 * 1024
        ),
    )(
        *[
            pltpu.with_memory_space_constraint(v, pltpu.HBM)
            for v in (
                measured,
                generated,
                previous.reshape(1, YB),
                row_weight.reshape(1, XB),
                col_weight.reshape(1, YB),
            )
        ]
    )
    row, col, gap = pl.pallas_call(
        put_results,
        out_shape=(
            jax.ShapeDtypeStruct((1, XB), F32),
            jax.ShapeDtypeStruct((1, YB), F32),
            jax.ShapeDtypeStruct((1, XB), F32),
        ),
        in_specs=[pl.BlockSpec(memory_space=pltpu.VMEM)] * 3,
        out_specs=(pl.BlockSpec(memory_space=pl.ANY),) * 3,
        scratch_shapes=[dma((3,))],
        compiler_params=pltpu.CompilerParams(vmem_limit_bytes=1024 * 1024),
    )(row, col, gap)
    return row.reshape(XB), col.reshape(YB), gap.reshape(XB)


def solution(mesh):
    placed = (
        P(None, ("row", "col")),
        P(None, ("col", "row")),
        P(("col", "row")),
        P(("row", "col")),
        P(("col", "row")),
    )
    return jax.shard_map(
        body,
        mesh=mesh,
        in_specs=placed,
        out_specs=(P(("row", "col")), P(("col", "row")), P(("row", "col"))),
        check_vma=False,
    )
```

```python
import functools
import math

import jax
import jax.numpy as jnp
from jax import lax
from jax.experimental import pallas as pl
from jax.experimental.pallas import tpu as pltpu
from jax.sharding import PartitionSpec as P

EPSILON = 0.1
LOG2E = 1.0 / math.log(2.0)
LN2 = math.log(2.0)
MESH = pl.DeviceIdType.MESH
F32 = jnp.float32
BF16 = jnp.bfloat16

GRID = {"z": 8, "y": 4, "xh": 2, "xl": 2}
XB = 256
YB = 128
DIM = 64


def kernel(
    measured_hbm,
    generated_hbm,
    previous_hbm,
    row_weight_hbm,
    col_weight_hbm,
    row_out,
    col_out,
    gap_out,
    measured,
    generated,
    previous,
    row_weight,
    col_weight,
    xraw,
    yraw,
    yt,
    xaug,
    scores,
    row8,
    cstat,
    sstat,
    gbuf,
    row_stat_out,
    row_stat_in,
    rbuf,
    rfull,
    col_stat_out,
    col_stat_in,
    qbuf,
    w_out,
    w_in,
    in_sem,
    x_send,
    x_recv,
    y_send,
    y_recv,
    row_send,
    row_recv,
    r_send,
    r_recv,
    col_send,
    col_recv,
    q_send,
    q_recv,
    w_send,
    w_recv,
):
    NZ, NY, NXH, NXL = GRID["z"], GRID["y"], GRID["xh"], GRID["xl"]
    NX = NXH * NXL
    NQ, NP = NX * NY, NZ * 2
    NI = NQ * XB
    NL = NI // 128
    ndev = NQ * NP

    loads = [
        pltpu.make_async_copy(src, dst, in_sem.at[n])
        for n, (src, dst) in enumerate(
            [
                (generated_hbm, generated),
                (previous_hbm, previous),
                (col_weight_hbm, col_weight),
                (measured_hbm, measured),
                (row_weight_hbm, row_weight),
            ]
        )
    ]
    for c in loads:
        c.start()

    row = lax.axis_index("row")
    col = lax.axis_index("col")
    z = row // (NY * NXH)
    y = (row // NXH) % NY
    x = (row % NXH) * NXL + col // 2
    core = col % 2

    def device(dz, dy, dx, dc):
        zz, yy, xx = (z + dz) % NZ, (y + dy) % NY, (x + dx) % NX
        return ((zz * NY + yy) * NXH + xx // NXL, (xx % NXL) * 2 + (core + dc) % 2)

    def plane(k):
        dy, dx = k // NX, k % NX
        return device(0, dy, dx, 0), ((NY - dy) % NY) * NX + (NX - dx) % NX

    def line(k):
        dz, dc = k // 2, k % 2
        return device(dz, 0, 0, dc), ((NZ - dz) % NZ) * 2 + dc

    def copy(src, dst, send, recv, dev):
        return pltpu.make_async_remote_copy(
            src_ref=src, dst_ref=dst, send_sem=send, recv_sem=recv, device_id=dev, device_id_type=MESH
        )

    def loop(lo, hi, fn):
        def step(k, carry):
            fn(k)
            return carry

        lax.fori_loop(lo, hi, step, 0)

    def near(n, size):
        return (size + (2 * (n % 2) - 1) * ((n + 1) // 2)) % size

    barrier = pltpu.get_barrier_semaphore()
    loop(1, NQ, lambda k: pl.semaphore_signal(barrier, inc=1, device_id=plane(k)[0], device_id_type=MESH))
    loop(1, NP, lambda k: pl.semaphore_signal(barrier, inc=1, device_id=line(k)[0], device_id_type=MESH))

    for c in loads:
        c.wait()
    scale = 2.0 * LOG2E / EPSILON
    xraw[0] = measured[...] * scale
    gen = generated[...]
    log_b = jnp.log(col_weight[...]) - math.log(YB * ndev)
    ysq = jnp.sum(gen * gen, axis=0, keepdims=True)
    u = (log_b + (previous[...] - ysq) / EPSILON) * LOG2E
    yraw[0, 0:DIM] = gen
    yraw[0, DIM : DIM + 8] = jnp.broadcast_to(u, (8, YB))
    log_a = jnp.log(row_weight[...]) - math.log(XB * ndev)
    xsq = jnp.sum(measured[...] * measured[...], axis=0, keepdims=True)
    xaug[:, 3 * DIM :] = jnp.ones((NQ // 2, DIM, 2 * XB), BF16)

    pl.semaphore_wait(barrier, NQ + NP - 2)

    half = DIM // 2

    def x_copy(slot, part, dst_slot, n, dev):
        at = pl.ds(part * half, half)
        return copy(xraw.at[slot, at], xraw.at[dst_slot, at], x_send.at[n], x_recv.at[dst_slot, part], dev)

    def wait_x(slot, part):
        x_copy(slot, part, slot, 0, device(0, 0, 1, 0)).wait_recv()

    def y_copy(n, slot, dst_slot, dev):
        return copy(yraw.at[slot], yraw.at[dst_slot], y_send.at[n], y_recv.at[dst_slot], dev)

    def wait_y(slot):
        y_copy(0, slot, slot, device(0, 0, 0, 1)).wait_recv()

    def send_y(n):
        ez = near(n, NZ)
        y_copy(n, 0, ((NZ - ez) % NZ) * 2, device(ez, 0, 0, 0)).start()

    def send_x(n):
        e = near(n, NX)
        back = (NX - e) % NX
        m = 2 * (n - 1)
        x_copy(0, 0, back, m, device(0, 0, e, 0)).start()
        x_copy(0, 1, back * NX, m + 1, device(0, e, 0, 0)).start()

    def send_x_rest(n):
        e = near(n, NX)
        back = (NX - e) % NX
        m = 2 * (NX - 1) + 2 * (n - 1)
        x_copy(0, 1, back, m, device(0, 0, e, 0)).start()
        x_copy(0, 0, back * NX, m + 1, device(0, e, 0, 0)).start()

    def forward_x(n):
        d = near(n, NX)
        wait_x(d, 0)
        wait_x(d * NX, 1)
        for k in range(1, NX):
            e = near(k, NX)
            back = (NX - e) % NX
            m = 4 * (NX - 1) + 2 * (NX - 1) * (n - 1) + 2 * (k - 1)
            x_copy(d, 0, back * NX + d, m, device(0, e, 0, 0)).start()
            x_copy(d * NX, 1, d * NX + back, m + 1, device(0, 0, e, 0)).start()

    def forward_y(n):
        slot = near(n, NZ) * 2
        wait_y(slot)
        y_copy(NZ + n, slot, slot + 1, device(0, 0, 0, 1)).start()

    y_copy(0, 0, 1, device(0, 0, 0, 1)).start()
    loop(1, NZ, send_y)
    loop(1, NX, send_x)
    loop(1, NX, send_x_rest)

    def split(v):
        hi = v.astype(BF16).astype(F32)
        return hi, v - hi

    sub128 = lax.broadcasted_iota(jnp.int32, (8, YB), 0)

    def turn_y(slot):
        hi, lo = split(yraw[slot, 0:DIM])
        t1, rest = split(yraw[slot, DIM : DIM + 8])
        t2, t3 = split(rest)
        extra = jnp.where(sub128 == 0, t1, jnp.where(sub128 == 1, t2, jnp.where(sub128 == 2, t3, 0.0)))
        at = pl.ds(pl.multiple_of(slot * YB, YB), YB)
        yt[at, 0 : 2 * DIM] = jnp.concatenate([hi, hi], axis=0).T.astype(BF16)
        yt[at, 2 * DIM :] = jnp.concatenate([lo, extra, jnp.zeros((DIM - 8, YB), F32)], axis=0).T.astype(BF16)

    def ready_x(pair):
        dy = pair // (NX // 2)
        for h in range(2):
            dx = (pair % (NX // 2)) * 2 + h

            @pl.when(dy > 0)
            def _():
                wait_x(2 * pair + h, 0)

            @pl.when(dx > 0)
            def _():
                wait_x(2 * pair + h, 1)

        for h in range(2):
            v = xraw[2 * pair + h]
            hi = v.astype(BF16)
            lo = (v - hi.astype(F32)).astype(BF16)
            at = slice(h * XB, (h + 1) * XB)
            xaug[pair, 0:DIM, at] = hi
            xaug[pair, DIM : 2 * DIM, at] = lo
            xaug[pair, 2 * DIM : 3 * DIM, at] = hi

    CH = 2 * YB
    PW = 2 * XB
    NPAIR = NQ // 2

    def rows_at(c):
        return pl.ds(pl.multiple_of(c * CH, CH), CH)

    def dot_stage(pair, c):
        scores[pair, rows_at(c)] = jnp.dot(yt[rows_at(c)], xaug[pair], preferred_element_type=F32)

    def max_stage(pair, c, accs):
        block = scores.at[pair, rows_at(c)]
        accs = list(accs)
        for k in range(CH // 8):
            accs[k % 2] = jnp.maximum(accs[k % 2], block[k * 8 : k * 8 + 8])
        return accs

    def exp_stage(pair, c, top, accs):
        block = scores.at[pair, rows_at(c)]
        accs = list(accs)
        for k in range(CH // 8):
            accs[k % 2] = accs[k % 2] + jnp.exp2(block[k * 8 : k * 8 + 8] - top)
        return accs

    turn_y(0)
    loop(1, NX, forward_x)

    def second_core(n):
        slot = near(n, NZ) * 2 + 1
        wait_y(slot)
        turn_y(slot)
        dot_stage(0, slot // 2)

    def arrive(n):
        forward_y(n)
        slot = near(n, NZ) * 2
        wait_y(near(n - 1, NZ) * 2 + 1)
        turn_y(slot)
        turn_y(near(n - 1, NZ) * 2 + 1)
        dot_stage(0, near(n - 1, NZ))

    forward_y(1)
    ready_x(0)
    turn_y(near(1, NZ) * 2)
    second_core(0)
    loop(2, NZ, arrive)
    second_core(NZ - 1)

    low = jnp.full((8, PW), -3e38, F32)
    zero = jnp.zeros((8, PW), F32)

    def row_step(one, two, three, top):
        def chunk(c, carry):
            tops, sums = carry[:2], carry[2:]
            if three is not None:
                sums = exp_stage(three, c, top, sums)
            if two is not None:
                tops = max_stage(two, c, tops)
            if one is not None:
                dot_stage(one, c)
            return (*tops, *sums)

        out = lax.fori_loop(0, NZ, chunk, (low, low, zero, zero), unroll=2)
        if three is not None:
            row8[three, 0] = top
            row8[three, 1] = out[2] + out[3]
        return jnp.maximum(out[0], out[1])

    def row_loop(step, top):
        ready_x(step)
        return row_step(step, step - 1, step - 2, top)

    ready_x(1)
    top = row_step(1, 0, None, None)
    top = lax.fori_loop(2, NPAIR, row_loop, top)
    top = row_step(None, NPAIR - 1, NPAIR - 2, top)
    row_step(None, None, NPAIR - 1, top)
    for pair in range(NPAIR):
        best = jnp.max(row8[pair, 0], axis=0, keepdims=True)
        summed = jnp.sum(row8[pair, 1] * jnp.exp2(row8[pair, 0] - best), axis=0, keepdims=True)
        for h in range(2):
            slot = 2 * pair + h
            ref = row_stat_in if slot == 0 else row_stat_out
            ref[slot, :, 0:XB] = best[:, h * XB : (h + 1) * XB]
            ref[slot, :, XB:] = summed[:, h * XB : (h + 1) * XB]

    def send_part(src, dst, send, recv, where, k):
        dev, slot = where(k)
        copy(src.at[k], dst.at[slot], send.at[k], recv.at[slot], dev).start()

    def send_all(src, dst, send, recv, where, k):
        dev, slot = where(k)
        copy(src.at[0], dst.at[slot], send.at[k], recv.at[slot], dev).start()

    def wait_in(buf, send, recv, n):
        loop(1, n, lambda k: copy(buf.at[k], buf.at[k], send.at[k], recv.at[k], device(0, 0, 1, 0)).wait_recv())

    def wait_out(buf, send, recv, n):
        loop(1, n, lambda k: copy(buf.at[k], buf.at[k], send.at[k], recv.at[k], device(0, 0, 1, 0)).wait_send())

    def combined(ref, n, width):
        tops = [ref[k, :, 0:width] for k in range(n)]
        best = functools.reduce(jnp.maximum, tops)
        summed = functools.reduce(jnp.add, [ref[k, :, width:] * jnp.exp2(tops[k] - best) for k in range(n)])
        return best + jnp.log(summed) * LOG2E

    loop(1, NQ, lambda k: send_part(row_stat_out, row_stat_in, row_send, row_recv, plane, k))
    wait_in(row_stat_in, row_send, row_recv, NQ)
    row_lse = combined(row_stat_in, NQ, XB)
    rbuf[0] = log_a * LOG2E - row_lse
    loop(1, NQ, lambda k: send_all(rbuf, rbuf, r_send, r_recv, plane, k))
    row_out[...] = xsq - (EPSILON * LN2) * row_lse
    wait_in(rbuf, r_send, r_recv, NQ)
    for k in range(NQ):
        rfull[:, k * XB : (k + 1) * XB] = jnp.broadcast_to(rbuf[k], (8, XB))

    eye = lax.broadcasted_iota(jnp.int32, (YB, YB), 0) == lax.broadcasted_iota(jnp.int32, (YB, YB), 1)
    per = PW // 128

    def across(v):
        return jnp.sum(jnp.where(eye, v, 0.0), axis=0, keepdims=True)

    def rows_of(b):
        return pl.ds(pl.multiple_of(b * YB, YB), YB)

    def lanes(l):
        return slice((l % per) * 128, (l % per + 1) * 128)

    def col_tiles(b):
        blocks = [scores.at[pair, rows_of(b)] for pair in range(NPAIR)]
        cblock, sblock = cstat.at[rows_of(b)], sstat.at[rows_of(b)]
        for t in range(YB // 8):
            r8 = slice(t * 8, (t + 1) * 8)
            vals = [blocks[l // per][r8, lanes(l)] + rfull[:, l * 128 : (l + 1) * 128] for l in range(NL)]
            tops = vals
            while len(tops) > 1:
                tops = [jnp.maximum(tops[i], tops[i + 1]) for i in range(0, len(tops), 2)]
            top = tops[0]
            sums = [None] * 4
            for l in range(NL):
                e = jnp.exp2(vals[l] - top)
                blocks[l // per][r8, lanes(l)] = e
                sums[l % 4] = e if l < 4 else sums[l % 4] + e
            cblock[r8] = top
            sblock[r8] = (sums[0] + sums[1]) + (sums[2] + sums[3])

    def put_stats(b):
        c = cstat[rows_of(b), :]
        best = jnp.max(c, axis=1, keepdims=True)
        summed = jnp.sum(sstat[rows_of(b), :] * jnp.exp2(c - best), axis=1, keepdims=True)
        col_stat_out[b, :, 0:YB] = across(best)
        col_stat_out[b, :, YB:] = across(summed)

    def col_loop(b):
        put_stats(b - 1)
        col_tiles(b)

        @pl.when(b > 1)
        def _():
            send_part(col_stat_out, col_stat_in, col_send, col_recv, line, b - 1)

    col_tiles(0)
    loop(1, NP, col_loop)
    put_stats(NP - 1)
    send_part(col_stat_out, col_stat_in, col_send, col_recv, line, NP - 1)
    col_stat_in[0] = col_stat_out[0]
    wait_in(col_stat_in, col_send, col_recv, NP)
    col_lse = combined(col_stat_in, NP, YB)
    qbuf[0] = log_b * LOG2E - col_lse
    loop(1, NP, lambda k: send_all(qbuf, qbuf, q_send, q_recv, line, k))
    col_out[...] = previous[...] + EPSILON * log_b - (EPSILON * LN2) * col_lse

    def factors(b):
        q = jnp.sum(jnp.where(eye, qbuf[b], 0.0), axis=1, keepdims=True)
        gbuf[b % 2] = jnp.exp2(cstat[rows_of(b), :] + q)

    def gap_loop(b, acc):
        blocks = [scores.at[pair, rows_of(b)] for pair in range(NPAIR)]
        gblock = gbuf.at[b % 2]
        for t in range(YB // 8):
            r8 = slice(t * 8, (t + 1) * 8)
            g = gblock[r8]
            acc = [acc[l] + blocks[l // per][r8, lanes(l)] * g for l in range(NL)]
            if t == YB // 16:
                factors(jnp.minimum(b + 1, NP - 1))
        return acc

    factors(0)
    wait_in(qbuf, q_send, q_recv, NP)
    acc = lax.fori_loop(0, NP, gap_loop, [jnp.zeros((8, 128), F32) for _ in range(NL)])
    for k in range(NQ):
        for h in range(2):
            ref = w_in if k == 0 else w_out
            ref[k, :, h * 128 : (h + 1) * 128] = jnp.sum(acc[2 * k + h], axis=0, keepdims=True)
    loop(1, NQ, lambda k: send_part(w_out, w_in, w_send, w_recv, plane, k))

    loop(0, 2 * NQ - 2, lambda n: x_copy(0, 0, 0, n, device(0, 0, 1, 0)).wait_send())
    loop(0, NZ, lambda n: y_copy(n, 0, 0, device(0, 0, 0, 1)).wait_send())
    loop(NZ + 1, 2 * NZ, lambda n: y_copy(n, 0, 0, device(0, 0, 0, 1)).wait_send())
    wait_out(row_stat_out, row_send, row_recv, NQ)
    wait_out(rbuf, r_send, r_recv, NQ)
    wait_out(col_stat_out, col_send, col_recv, NP)
    wait_out(qbuf, q_send, q_recv, NP)

    wait_in(w_in, w_send, w_recv, NQ)
    mass = functools.reduce(jnp.add, [w_in[k] for k in range(NQ)])
    gap_out[...] = jnp.log(mass) - log_a
    wait_out(w_out, w_send, w_recv, NQ)


def put_results(row, col, gap, row_out, col_out, gap_out, sem):
    copies = [
        pltpu.make_async_copy(src, dst, sem.at[n])
        for n, (src, dst) in enumerate([(row, row_out), (col, col_out), (gap, gap_out)])
    ]
    for c in copies:
        c.start()
    for c in copies:
        c.wait()


def body(measured, generated, previous, row_weight, col_weight):
    NQ = GRID["y"] * GRID["xh"] * GRID["xl"]
    NP = GRID["z"] * 2
    NJ, NI = NP * YB, NQ * XB
    dma = pltpu.SemaphoreType.DMA
    row, col, gap = pl.pallas_call(
        kernel,
        out_shape=(
            jax.ShapeDtypeStruct((1, XB), F32),
            jax.ShapeDtypeStruct((1, YB), F32),
            jax.ShapeDtypeStruct((1, XB), F32),
        ),
        in_specs=[pl.BlockSpec(memory_space=pltpu.HBM)] * 5,
        out_specs=(pl.BlockSpec(memory_space=pltpu.VMEM),) * 3,
        scratch_shapes=[
            pltpu.VMEM((DIM, XB), F32),
            pltpu.VMEM((DIM, YB), F32),
            pltpu.VMEM((1, YB), F32),
            pltpu.VMEM((1, XB), F32),
            pltpu.VMEM((1, YB), F32),
            pltpu.VMEM((NQ, DIM, XB), F32),
            pltpu.VMEM((NP, DIM + 8, YB), F32),
            pltpu.VMEM((NJ, 4 * DIM), BF16),
            pltpu.VMEM((NQ // 2, 4 * DIM, 2 * XB), BF16),
            pltpu.VMEM((NQ // 2, NJ, 2 * XB), F32),
            pltpu.VMEM((NQ // 2, 2, 8, 2 * XB), F32),
            pltpu.VMEM((NJ, 128), F32),
            pltpu.VMEM((NJ, 128), F32),
            pltpu.VMEM((2, YB, 128), F32),
            pltpu.VMEM((NQ, 1, 2 * XB), F32),
            pltpu.VMEM((NQ, 1, 2 * XB), F32),
            pltpu.VMEM((NQ, 1, XB), F32),
            pltpu.VMEM((8, NI), F32),
            pltpu.VMEM((NP, 1, 2 * YB), F32),
            pltpu.VMEM((NP, 1, 2 * YB), F32),
            pltpu.VMEM((NP, 1, YB), F32),
            pltpu.VMEM((NQ, 1, XB), F32),
            pltpu.VMEM((NQ, 1, XB), F32),
            dma((5,)),
            dma((2 * NQ,)),
            dma((NQ, 2)),
            dma((NP,)),
            dma((NP,)),
            dma((NQ,)),
            dma((NQ,)),
            dma((NQ,)),
            dma((NQ,)),
            dma((NP,)),
            dma((NP,)),
            dma((NP,)),
            dma((NP,)),
            dma((NQ,)),
            dma((NQ,)),
        ],
        compiler_params=pltpu.CompilerParams(
            collective_id=0, has_side_effects=True, vmem_limit_bytes=46 * 1024 * 1024
        ),
    )(
        *[
            pltpu.with_memory_space_constraint(v, pltpu.HBM)
            for v in (
                measured,
                generated,
                previous.reshape(1, YB),
                row_weight.reshape(1, XB),
                col_weight.reshape(1, YB),
            )
        ]
    )
    row, col, gap = pl.pallas_call(
        put_results,
        out_shape=(
            jax.ShapeDtypeStruct((1, XB), F32),
            jax.ShapeDtypeStruct((1, YB), F32),
            jax.ShapeDtypeStruct((1, XB), F32),
        ),
        in_specs=[pl.BlockSpec(memory_space=pltpu.VMEM)] * 3,
        out_specs=(pl.BlockSpec(memory_space=pl.ANY),) * 3,
        scratch_shapes=[dma((3,))],
        compiler_params=pltpu.CompilerParams(vmem_limit_bytes=1024 * 1024),
    )(row, col, gap)
    return row.reshape(XB), col.reshape(YB), gap.reshape(XB)


def solution(mesh):
    placed = (
        P(None, ("row", "col")),
        P(None, ("col", "row")),
        P(("col", "row")),
        P(("row", "col")),
        P(("col", "row")),
    )
    return jax.shard_map(
        body,
        mesh=mesh,
        in_specs=placed,
        out_specs=(P(("row", "col")), P(("col", "row")), P(("row", "col"))),
        check_vma=False,
    )
```

```python
import functools
import math

import jax
import jax.numpy as jnp
from jax import lax
from jax.experimental import pallas as pl
from jax.experimental.pallas import tpu as pltpu
from jax.sharding import PartitionSpec as P

EPSILON = 0.1
LOG2E = 1.0 / math.log(2.0)
LN2 = math.log(2.0)
MESH = pl.DeviceIdType.MESH
F32 = jnp.float32
BF16 = jnp.bfloat16

GRID = {"z": 8, "y": 4, "xh": 2, "xl": 2}
XB = 256
YB = 128
DIM = 64


def kernel(
    measured_hbm,
    generated_hbm,
    previous_hbm,
    row_weight_hbm,
    col_weight_hbm,
    row_out,
    col_out,
    gap_out,
    measured,
    generated,
    previous,
    row_weight,
    col_weight,
    xraw,
    yraw,
    yt,
    xaug,
    scores,
    row8,
    cstat,
    sstat,
    gbuf,
    rl,
    rx,
    ry,
    rfull,
    cl,
    cc,
    cz,
    w,
    wx,
    wy,
    in_sem,
    x_send,
    x_recv,
    y_send,
    y_recv,
    rx_send,
    rx_recv,
    ry_send,
    ry_recv,
    cc_send,
    cc_recv,
    cz_send,
    cz_recv,
    wx_send,
    wx_recv,
    wy_send,
    wy_recv,
):
    NZ, NY, NXH, NXL = GRID["z"], GRID["y"], GRID["xh"], GRID["xl"]
    NX = NXH * NXL
    NQ, NP = NX * NY, NZ * 2
    NI = NQ * XB
    NL = NI // 128
    ndev = NQ * NP

    loads = [
        pltpu.make_async_copy(src, dst, in_sem.at[n])
        for n, (src, dst) in enumerate(
            [
                (generated_hbm, generated),
                (previous_hbm, previous),
                (col_weight_hbm, col_weight),
                (measured_hbm, measured),
                (row_weight_hbm, row_weight),
            ]
        )
    ]
    for c in loads:
        c.start()

    row = lax.axis_index("row")
    col = lax.axis_index("col")
    z = row // (NY * NXH)
    y = (row // NXH) % NY
    x = (row % NXH) * NXL + col // 2
    core = col % 2

    def device(dz, dy, dx, dc):
        zz, yy, xx = (z + dz) % NZ, (y + dy) % NY, (x + dx) % NX
        return ((zz * NY + yy) * NXH + xx // NXL, (xx % NXL) * 2 + (core + dc) % 2)

    def copy(src, dst, send, recv, dev):
        return pltpu.make_async_remote_copy(
            src_ref=src, dst_ref=dst, send_sem=send, recv_sem=recv, device_id=dev, device_id_type=MESH
        )

    def loop(lo, hi, fn):
        def step(k, carry):
            fn(k)
            return carry

        lax.fori_loop(lo, hi, step, 0)

    def others(size):
        return sorted(range(1, size), key=lambda d: min(d, size - d))

    def along_x(e):
        return device(0, 0, e, 0)

    def along_y(e):
        return device(0, e, 0, 0)

    def along_z(e):
        return device(e, 0, 0, 0)

    sibling = device(0, 0, 0, 1)
    partners = [along_x(e) for e in others(NX)] + [along_y(e) for e in others(NY)]
    partners += [along_z(e) for e in others(NZ)] + [sibling]
    barrier = pltpu.get_barrier_semaphore()
    for dev in partners:
        pl.semaphore_signal(barrier, inc=1, device_id=dev, device_id_type=MESH)

    for c in loads:
        c.wait()
    scale = 2.0 * LOG2E / EPSILON
    xraw[0, 0] = measured[...] * scale
    gen = generated[...]
    log_b = jnp.log(col_weight[...]) - math.log(YB * ndev)
    ysq = jnp.sum(gen * gen, axis=0, keepdims=True)
    u = (log_b + (previous[...] - ysq) / EPSILON) * LOG2E
    yraw[0, 0, 0:DIM] = gen
    yraw[0, 0, DIM : DIM + 8] = jnp.broadcast_to(u, (8, YB))
    log_a = jnp.log(row_weight[...]) - math.log(XB * ndev)
    xsq = jnp.sum(measured[...] * measured[...], axis=0, keepdims=True)
    xaug[:, 3 * DIM :] = jnp.ones((NQ // 2, DIM, 2 * XB), BF16)

    pl.semaphore_wait(barrier, len(partners))

    pending = []

    def send(src, dst, send_sem, recv_sem, dev):
        c = copy(src, dst, send_sem, recv_sem, dev)
        c.start()
        pending.append(c)

    def arrived(ref, send_sem, recv_sem):
        copy(ref, ref, send_sem, recv_sem, sibling).wait_recv()

    first, second = slice(0, DIM // 2), slice(DIM // 2, DIM)

    for e in others(NZ):
        back = (NZ - e) % NZ
        send(yraw.at[0, 0], yraw.at[back, 0], y_send.at[0, e], y_recv.at[back, 0], along_z(e))
    send(yraw.at[0, 0], yraw.at[0, 1], y_send.at[0, 0], y_recv.at[0, 1], sibling)
    for e in others(NX):
        back = (NX - e) % NX
        send(xraw.at[0, 0, first], xraw.at[0, back, first], x_send.at[0, e], x_recv.at[0, back], along_x(e))
        send(xraw.at[0, 0, second], xraw.at[back, 0, second], x_send.at[1, e], x_recv.at[1, back], along_y(e))
    for e in others(NX):
        back = (NX - e) % NX
        send(xraw.at[0, 0, second], xraw.at[0, back, second], x_send.at[2, e], x_recv.at[2, back], along_x(e))
        send(xraw.at[0, 0, first], xraw.at[back, 0, first], x_send.at[3, e], x_recv.at[3, back], along_y(e))

    def forward_x():
        for e in others(NX):
            arrived(xraw.at[0, e, first], x_send.at[0, e], x_recv.at[0, e])
            arrived(xraw.at[e, 0, second], x_send.at[1, e], x_recv.at[1, e])
        for e in others(NX):
            back = (NX - e) % NX
            send(xraw.at[0, 1:, first], xraw.at[back, 1:, first], x_send.at[4, e], x_recv.at[4, back], along_y(e))
            send(xraw.at[1:, 0, second], xraw.at[1:, back, second], x_send.at[5, e], x_recv.at[5, back], along_x(e))

    def split(v):
        hi = v.astype(BF16).astype(F32)
        return hi, v - hi

    sub128 = lax.broadcasted_iota(jnp.int32, (8, YB), 0)

    def turn_y(slot):
        hi, lo = split(yraw[slot // 2, slot % 2, 0:DIM])
        t1, rest = split(yraw[slot // 2, slot % 2, DIM : DIM + 8])
        t2, t3 = split(rest)
        extra = jnp.where(sub128 == 0, t1, jnp.where(sub128 == 1, t2, jnp.where(sub128 == 2, t3, 0.0)))
        at = slice(slot * YB, (slot + 1) * YB)
        yt[at, 0 : 2 * DIM] = jnp.concatenate([hi, hi], axis=0).T.astype(BF16)
        yt[at, 2 * DIM :] = jnp.concatenate([lo, extra, jnp.zeros((DIM - 8, YB), F32)], axis=0).T.astype(BF16)

    def ready_x(pair):
        for h in range(2):
            v = xraw[pair // (NX // 2), (pair % (NX // 2)) * 2 + h]
            hi = v.astype(BF16)
            lo = (v - hi.astype(F32)).astype(BF16)
            at = slice(h * XB, (h + 1) * XB)
            xaug[pair, 0:DIM, at] = hi
            xaug[pair, DIM : 2 * DIM, at] = lo
            xaug[pair, 2 * DIM : 3 * DIM, at] = hi

    CH = 2 * YB
    PW = 2 * XB
    NPAIR = NQ // 2

    def rows_at(c):
        return pl.ds(pl.multiple_of(c * CH, CH), CH)

    def dot_stage(pair, c):
        scores[pair, rows_at(c)] = jnp.dot(yt[rows_at(c)], xaug[pair], preferred_element_type=F32)

    def max_stage(pair, c, accs):
        block = scores.at[pair, rows_at(c)]
        accs = list(accs)
        for k in range(CH // 8):
            accs[k % 2] = jnp.maximum(accs[k % 2], block[k * 8 : k * 8 + 8])
        return accs

    def exp_stage(pair, c, top, accs):
        block = scores.at[pair, rows_at(c)]
        accs = list(accs)
        for k in range(CH // 8):
            accs[k % 2] = accs[k % 2] + jnp.exp2(block[k * 8 : k * 8 + 8] - top)
        return accs

    turn_y(0)
    batches = [(1, 3), (NZ - 2, NZ), (3, NZ - 2)] if NZ == 8 else [(1, NZ)]
    for n in range(len(batches) + 1):
        if n < len(batches):
            lo, hi = batches[n]
            for dz in range(lo, hi):
                arrived(yraw.at[dz, 0], y_send.at[0, dz], y_recv.at[dz, 0])
            send(yraw.at[lo:hi, 0], yraw.at[lo:hi, 1], y_send.at[1, lo], y_recv.at[lo, 1], sibling)
            for dz in range(lo, hi):
                turn_y(2 * dz)
        if n == 0:
            forward_x()
            for e in others(NX):
                arrived(xraw.at[0, e, second], x_send.at[2, e], x_recv.at[2, e])
            ready_x(0)
            if NX > 2:
                ready_x(1)
            arrived(yraw.at[0, 1], y_send.at[0, 0], y_recv.at[0, 1])
            turn_y(1)
            dot_stage(0, 0)
        else:
            lo, hi = batches[n - 1]
            arrived(yraw.at[lo:hi, 1], y_send.at[1, lo], y_recv.at[lo, 1])
            for dz in range(lo, hi):
                turn_y(2 * dz + 1)
            for dz in range(lo, hi):
                dot_stage(0, dz)

    low = jnp.full((8, PW), -3e38, F32)
    zero = jnp.zeros((8, PW), F32)

    def row_step(one, two, three, top):
        def chunk(c, carry):
            tops, sums = carry[:2], carry[2:]
            if three is not None:
                sums = exp_stage(three, c, top, sums)
            if two is not None:
                tops = max_stage(two, c, tops)
            if one is not None:
                dot_stage(one, c)
            return (*tops, *sums)

        out = lax.fori_loop(0, NZ, chunk, (low, low, zero, zero), unroll=NZ)
        if three is not None:
            row8[three, 0] = top
            row8[three, 1] = out[2] + out[3]
        return jnp.maximum(out[0], out[1])

    def row_loop(step, top):
        ready_x(step)
        return row_step(step, step - 1, step - 2, top)

    def last_x():
        for e in others(NX):
            arrived(xraw.at[e, 0, first], x_send.at[3, e], x_recv.at[3, e])
            arrived(xraw.at[e, 1:, first], x_send.at[4, e], x_recv.at[4, e])
            arrived(xraw.at[1:, e, second], x_send.at[5, e], x_recv.at[5, e])

    if NX == 2:
        last_x()
        ready_x(1)
    top = row_step(1, 0, None, None)
    if NX > 2:
        last_x()
    top = lax.fori_loop(2, NPAIR, row_loop, top)
    top = row_step(None, NPAIR - 1, NPAIR - 2, top)
    row_step(None, None, NPAIR - 1, top)

    def log2(v):
        return jnp.log(v) * LOG2E

    def lse(values):
        best = functools.reduce(jnp.maximum, values)
        return best + log2(functools.reduce(jnp.add, [jnp.exp2(v - best) for v in values]))

    for pair in range(NPAIR):
        best = jnp.max(row8[pair, 0], axis=0, keepdims=True)
        local = best + log2(jnp.sum(row8[pair, 1] * jnp.exp2(row8[pair, 0] - best), axis=0, keepdims=True))
        for h in range(2):
            rl[0, 2 * pair + h] = local[:, h * XB : (h + 1) * XB]
    rl[0, NQ] = log_a * LOG2E
    for e in others(NX):
        back = (NX - e) % NX
        send(rl.at[0, 0 : NQ + 1], rx.at[back], rx_send.at[e], rx_recv.at[back], along_x(e))
    for e in others(NX):
        arrived(rx.at[e], rx_send.at[e], rx_recv.at[e])
    for dy in range(NY):
        for dx in range(NX):
            rl[1, dy * NX + dx] = lse(
                [rl[0, dy * NX + dx]] + [rx[e, dy * NX + (dx - e) % NX] for e in range(1, NX)]
            )
    rl[1, NQ] = rl[0, NQ]
    for e in range(1, NX):
        rl[1, NQ + e] = rx[e, NQ]
    for e in others(NY):
        back = (NY - e) % NY
        send(rl.at[1], ry.at[back], ry_send.at[e], ry_recv.at[back], along_y(e))
    for e in others(NY):
        arrived(ry.at[e], ry_send.at[e], ry_recv.at[e])
    for dy in range(NY):
        for dx in range(NX):
            k = dy * NX + dx
            full = lse([rl[1, k]] + [ry[e, ((dy - e) % NY) * NX + dx] for e in range(1, NY)])
            mass = rl[1, NQ + dx] if dy == 0 else ry[dy, NQ + dx]
            rfull[:, k * XB : (k + 1) * XB] = jnp.broadcast_to(mass - full, (8, XB))
            if k == 0:
                row_out[...] = xsq - (EPSILON * LN2) * full

    eye = lax.broadcasted_iota(jnp.int32, (YB, YB), 0) == lax.broadcasted_iota(jnp.int32, (YB, YB), 1)
    per = PW // 128

    def across(v):
        return jnp.sum(jnp.where(eye, v, 0.0), axis=0, keepdims=True)

    def rows_of(b):
        return pl.ds(pl.multiple_of(b * YB, YB), YB)

    def lanes(l):
        return slice((l % per) * 128, (l % per + 1) * 128)

    def col_tiles(b):
        blocks = [scores.at[pair, rows_of(b)] for pair in range(NPAIR)]
        cblock, sblock = cstat.at[rows_of(b)], sstat.at[rows_of(b)]
        for t in range(YB // 8):
            r8 = slice(t * 8, (t + 1) * 8)
            vals = [blocks[l // per][r8, lanes(l)] + rfull[:, l * 128 : (l + 1) * 128] for l in range(NL)]
            tops = vals
            while len(tops) > 1:
                tops = [jnp.maximum(tops[i], tops[i + 1]) for i in range(0, len(tops), 2)]
            top = tops[0]
            sums = [None] * 4
            for l in range(NL):
                e = jnp.exp2(vals[l] - top)
                blocks[l // per][r8, lanes(l)] = e
                sums[l % 4] = e if l < 4 else sums[l % 4] + e
            cblock[r8] = top
            sblock[r8] = (sums[0] + sums[1]) + (sums[2] + sums[3])

    def put_stats(b):
        c = cstat[rows_of(b), :]
        best = jnp.max(c, axis=1, keepdims=True)
        summed = jnp.sum(sstat[rows_of(b), :] * jnp.exp2(c - best), axis=1, keepdims=True)
        cl[0, b] = across(best) + log2(across(summed))

    def col_loop(b):
        put_stats(b - 1)
        col_tiles(b)

    col_tiles(0)
    loop(1, NP, col_loop)
    put_stats(NP - 1)

    cl[0, NP] = log_b * LOG2E
    send(cl.at[0, 0 : NP + 1], cc, cc_send, cc_recv, sibling)
    arrived(cc, cc_send, cc_recv)
    for dz in range(NZ):
        for dc in range(2):
            cl[1, 2 * dz + dc] = lse([cl[0, 2 * dz + dc], cc[2 * dz + 1 - dc]])
    cl[1, NP] = cl[0, NP]
    cl[1, NP + 1] = cc[NP]
    for e in others(NZ):
        back = (NZ - e) % NZ
        send(cl.at[1], cz.at[back], cz_send.at[e], cz_recv.at[back], along_z(e))
    for e in others(NZ):
        arrived(cz.at[e], cz_send.at[e], cz_recv.at[e])
    for dz in range(NZ):
        for dc in range(2):
            k = 2 * dz + dc
            full = lse([cl[1, k]] + [cz[e, 2 * ((dz - e) % NZ) + dc] for e in range(1, NZ)])
            mass = cl[1, NP + dc] if dz == 0 else cz[dz, NP + dc]
            cl[2, k] = mass - full
            if k == 0:
                col_out[...] = previous[...] + EPSILON * log_b - (EPSILON * LN2) * full

    def factors(b):
        q = jnp.sum(jnp.where(eye, cl[2, b], 0.0), axis=1, keepdims=True)
        gbuf[b % 2] = jnp.exp2(cstat[rows_of(b), :] + q)

    def gap_loop(b, acc):
        blocks = [scores.at[pair, rows_of(b)] for pair in range(NPAIR)]
        gblock = gbuf.at[b % 2]
        for t in range(YB // 8):
            r8 = slice(t * 8, (t + 1) * 8)
            g = gblock[r8]
            acc = [acc[l] + blocks[l // per][r8, lanes(l)] * g for l in range(NL)]
            if t == YB // 16:
                factors(jnp.minimum(b + 1, NP - 1))
        return acc

    factors(0)
    acc = lax.fori_loop(0, NP, gap_loop, [jnp.zeros((8, 128), F32) for _ in range(NL)])
    for k in range(NQ):
        for h in range(2):
            w[k // NX, k % NX, :, h * 128 : (h + 1) * 128] = jnp.sum(acc[2 * k + h], axis=0, keepdims=True)
    for e in others(NX):
        back = (NX - e) % NX
        send(w.at[:, e], wx.at[back], wx_send.at[e], wx_recv.at[back], along_x(e))
    for e in others(NX):
        arrived(wx.at[e], wx_send.at[e], wx_recv.at[e])
    for dy in range(NY):
        w[dy, 0] = functools.reduce(jnp.add, [w[dy, 0]] + [wx[e, dy] for e in range(1, NX)])
    for e in others(NY):
        back = (NY - e) % NY
        send(w.at[e, 0], wy.at[back], wy_send.at[e], wy_recv.at[back], along_y(e))
    for e in others(NY):
        arrived(wy.at[e], wy_send.at[e], wy_recv.at[e])
    gap_out[...] = jnp.log(functools.reduce(jnp.add, [w[0, 0]] + [wy[e] for e in range(1, NY)])) - log_a

    for c in pending:
        c.wait_send()


def put_results(row, col, gap, row_out, col_out, gap_out, sem):
    copies = [
        pltpu.make_async_copy(src, dst, sem.at[n])
        for n, (src, dst) in enumerate([(row, row_out), (col, col_out), (gap, gap_out)])
    ]
    for c in copies:
        c.start()
    for c in copies:
        c.wait()


def body(measured, generated, previous, row_weight, col_weight):
    NZ, NY, NX = GRID["z"], GRID["y"], GRID["xh"] * GRID["xl"]
    NQ, NP = NX * NY, NZ * 2
    NJ, NI = NP * YB, NQ * XB
    dma = pltpu.SemaphoreType.DMA
    row, col, gap = pl.pallas_call(
        kernel,
        out_shape=(
            jax.ShapeDtypeStruct((1, XB), F32),
            jax.ShapeDtypeStruct((1, YB), F32),
            jax.ShapeDtypeStruct((1, XB), F32),
        ),
        in_specs=[pl.BlockSpec(memory_space=pltpu.HBM)] * 5,
        out_specs=(pl.BlockSpec(memory_space=pltpu.VMEM),) * 3,
        scratch_shapes=[
            pltpu.VMEM((DIM, XB), F32),
            pltpu.VMEM((DIM, YB), F32),
            pltpu.VMEM((1, YB), F32),
            pltpu.VMEM((1, XB), F32),
            pltpu.VMEM((1, YB), F32),
            pltpu.VMEM((NY, NX, DIM, XB), F32),
            pltpu.VMEM((NZ, 2, DIM + 8, YB), F32),
            pltpu.VMEM((NJ, 4 * DIM), BF16),
            pltpu.VMEM((NQ // 2, 4 * DIM, 2 * XB), BF16),
            pltpu.VMEM((NQ // 2, NJ, 2 * XB), F32),
            pltpu.VMEM((NQ // 2, 2, 8, 2 * XB), F32),
            pltpu.VMEM((NJ, 128), F32),
            pltpu.VMEM((NJ, 128), F32),
            pltpu.VMEM((2, YB, 128), F32),
            pltpu.VMEM((2, NQ + NX, 1, XB), F32),
            pltpu.VMEM((NX, NQ + 1, 1, XB), F32),
            pltpu.VMEM((NY, NQ + NX, 1, XB), F32),
            pltpu.VMEM((8, NI), F32),
            pltpu.VMEM((3, NP + 2, 1, YB), F32),
            pltpu.VMEM((NP + 1, 1, YB), F32),
            pltpu.VMEM((NZ, NP + 2, 1, YB), F32),
            pltpu.VMEM((NY, NX, 1, XB), F32),
            pltpu.VMEM((NX, NY, 1, XB), F32),
            pltpu.VMEM((NY, 1, XB), F32),
            dma((5,)),
            dma((6, NX)),
            dma((6, NX)),
            dma((2, NZ)),
            dma((NZ, 2)),
            dma((NX,)),
            dma((NX,)),
            dma((NY,)),
            dma((NY,)),
            dma,
            dma,
            dma((NZ,)),
            dma((NZ,)),
            dma((NX,)),
            dma((NX,)),
            dma((NY,)),
            dma((NY,)),
        ],
        compiler_params=pltpu.CompilerParams(
            collective_id=0, has_side_effects=True, vmem_limit_bytes=46 * 1024 * 1024
        ),
    )(
        *[
            pltpu.with_memory_space_constraint(v, pltpu.HBM)
            for v in (
                measured,
                generated,
                previous.reshape(1, YB),
                row_weight.reshape(1, XB),
                col_weight.reshape(1, YB),
            )
        ]
    )
    row, col, gap = pl.pallas_call(
        put_results,
        out_shape=(
            jax.ShapeDtypeStruct((1, XB), F32),
            jax.ShapeDtypeStruct((1, YB), F32),
            jax.ShapeDtypeStruct((1, XB), F32),
        ),
        in_specs=[pl.BlockSpec(memory_space=pltpu.VMEM)] * 3,
        out_specs=(pl.BlockSpec(memory_space=pl.ANY),) * 3,
        scratch_shapes=[dma((3,))],
        compiler_params=pltpu.CompilerParams(vmem_limit_bytes=1024 * 1024),
    )(row, col, gap)
    return row.reshape(XB), col.reshape(YB), gap.reshape(XB)


def solution(mesh):
    placed = (
        P(None, ("row", "col")),
        P(None, ("col", "row")),
        P(("col", "row")),
        P(("row", "col")),
        P(("col", "row")),
    )
    return jax.shard_map(
        body,
        mesh=mesh,
        in_specs=placed,
        out_specs=(P(("row", "col")), P(("col", "row")), P(("row", "col"))),
        check_vma=False,
    )
```

```python
import functools
import math

import jax
import jax.numpy as jnp
from jax import lax
from jax.experimental import pallas as pl
from jax.experimental.pallas import tpu as pltpu
from jax.sharding import PartitionSpec as P

EPSILON = 0.1
LOG2E = 1.0 / math.log(2.0)
LN2 = math.log(2.0)
MESH = pl.DeviceIdType.MESH
F32 = jnp.float32
BF16 = jnp.bfloat16

GRID = {"z": 8, "y": 4, "xh": 2, "xl": 2}
XB = 256
YB = 128
DIM = 64


def kernel(
    measured_hbm,
    generated_hbm,
    previous_hbm,
    row_weight_hbm,
    col_weight_hbm,
    row_out,
    col_out,
    gap_out,
    measured,
    generated,
    previous,
    row_weight,
    col_weight,
    xraw,
    yraw,
    yt,
    xaug,
    scores,
    row8,
    cstat,
    sstat,
    gbuf,
    rl,
    rx,
    ry,
    rfull,
    cl,
    cc,
    cz,
    w,
    wx,
    wy,
    in_sem,
    x_send,
    x_recv,
    y_send,
    y_recv,
    rx_send,
    rx_recv,
    ry_send,
    ry_recv,
    cc_send,
    cc_recv,
    cz_send,
    cz_recv,
    wx_send,
    wx_recv,
    wy_send,
    wy_recv,
):
    NZ, NY, NXH, NXL = GRID["z"], GRID["y"], GRID["xh"], GRID["xl"]
    NX = NXH * NXL
    NQ, NP = NX * NY, NZ * 2
    NI = NQ * XB
    NL = NI // 128
    ndev = NQ * NP

    loads = [
        pltpu.make_async_copy(src, dst, in_sem.at[n])
        for n, (src, dst) in enumerate(
            [
                (generated_hbm, generated),
                (previous_hbm, previous),
                (col_weight_hbm, col_weight),
                (measured_hbm, measured),
                (row_weight_hbm, row_weight),
            ]
        )
    ]
    for c in loads:
        c.start()

    row = lax.axis_index("row")
    col = lax.axis_index("col")
    z = row // (NY * NXH)
    y = (row // NXH) % NY
    x = (row % NXH) * NXL + col // 2
    core = col % 2

    def device(dz, dy, dx, dc):
        zz, yy, xx = (z + dz) % NZ, (y + dy) % NY, (x + dx) % NX
        return ((zz * NY + yy) * NXH + xx // NXL, (xx % NXL) * 2 + (core + dc) % 2)

    def copy(src, dst, send, recv, dev):
        return pltpu.make_async_remote_copy(
            src_ref=src, dst_ref=dst, send_sem=send, recv_sem=recv, device_id=dev, device_id_type=MESH
        )

    def loop(lo, hi, fn):
        def step(k, carry):
            fn(k)
            return carry

        lax.fori_loop(lo, hi, step, 0)

    def others(size):
        return sorted(range(1, size), key=lambda d: min(d, size - d))

    def along_x(e):
        return device(0, 0, e, 0)

    def along_y(e):
        return device(0, e, 0, 0)

    def along_z(e):
        return device(e, 0, 0, 0)

    sibling = device(0, 0, 0, 1)
    partners = [along_x(e) for e in others(NX)] + [along_y(e) for e in others(NY)]
    partners += [along_z(e) for e in others(NZ)] + [sibling]
    barrier = pltpu.get_barrier_semaphore()
    for dev in partners:
        pl.semaphore_signal(barrier, inc=1, device_id=dev, device_id_type=MESH)

    for c in loads:
        c.wait()
    scale = 2.0 * LOG2E / EPSILON
    xraw[0, 0] = measured[...] * scale
    gen = generated[...]
    log_b = jnp.log(col_weight[...]) - math.log(YB * ndev)
    ysq = jnp.sum(gen * gen, axis=0, keepdims=True)
    u = (log_b + (previous[...] - ysq) / EPSILON) * LOG2E
    yraw[0, 0, 0:DIM] = gen
    yraw[0, 0, DIM : DIM + 8] = jnp.broadcast_to(u, (8, YB))
    log_a = jnp.log(row_weight[...]) - math.log(XB * ndev)
    xsq = jnp.sum(measured[...] * measured[...], axis=0, keepdims=True)
    xaug[:, 3 * DIM :] = jnp.ones((NQ // 2, DIM, 2 * XB), BF16)

    pl.semaphore_wait(barrier, len(partners))

    pending = []

    def send(src, dst, send_sem, recv_sem, dev):
        c = copy(src, dst, send_sem, recv_sem, dev)
        c.start()
        pending.append(c)

    def arrived(ref, send_sem, recv_sem):
        copy(ref, ref, send_sem, recv_sem, sibling).wait_recv()

    def cuts(lo, hi, mid):
        return {None: slice(lo, hi), 0: slice(lo, mid), 1: slice(mid, hi)}

    ax, bx = cuts(0, DIM // 2, DIM // 4), cuts(DIM // 2, DIM, 3 * DIM // 4)
    yrows = cuts(0, DIM + 8, 40)

    def ring_send(d, n, ref, send_sem, recv_sem, along):
        to = d + 1
        if 2 * to < n:
            send(ref(d, None), ref(to, None), send_sem.at[2 * d], recv_sem.at[to], along(n - 1))
            send(ref((n - d) % n, None), ref(n - to, None), send_sem.at[2 * d + 1], recv_sem.at[n - to], along(1))
        elif 2 * to == n:
            send(ref(d, 0), ref(to, 0), send_sem.at[2 * d], recv_sem.at[to], along(n - 1))
            send(ref((n - d) % n, 1), ref(to, 1), send_sem.at[2 * d + 1], recv_sem.at[0], along(1))

    def ring_wait(d, n, ref, send_sem, recv_sem):
        to = d + 1
        if 2 * to < n:
            arrived(ref(to, None), send_sem.at[0], recv_sem.at[to])
            arrived(ref(n - to, None), send_sem.at[0], recv_sem.at[n - to])
        elif 2 * to == n:
            arrived(ref(to, 0), send_sem.at[0], recv_sem.at[to])
            arrived(ref(to, 1), send_sem.at[0], recv_sem.at[0])

    def y_ring(s, part):
        return yraw.at[s, 0, yrows[part]]

    x_rings = [
        (NX, lambda s, part: xraw.at[0, s, ax[part]], along_x),
        (NY, lambda s, part: xraw.at[s, 0, bx[part]], along_y),
        (NX, lambda s, part: xraw.at[0, s, bx[part]], along_x),
        (NY, lambda s, part: xraw.at[s, 0, ax[part]], along_y),
        (NY, lambda s, part: xraw.at[s, 1:, ax[part]], along_y),
        (NX, lambda s, part: xraw.at[1:, s, bx[part]], along_x),
        (NY, lambda s, part: xraw.at[s, :, ax[part]], along_y),
        (NX, lambda s, part: xraw.at[:, s, bx[part]], along_x),
    ]

    def x_go(r, d):
        n, ref, along = x_rings[r]
        ring_send(d, n, ref, x_send.at[r], x_recv.at[r], along)

    def x_wait(r, d):
        n, ref, along = x_rings[r]
        ring_wait(d, n, ref, x_send.at[r], x_recv.at[r])

    def y_go(d):
        ring_send(d, NZ, y_ring, y_send.at[0], y_recv.at[0], along_z)

    def y_wait(d):
        ring_wait(d, NZ, y_ring, y_send.at[0], y_recv.at[0])

    y_go(0)
    send(yraw.at[0, 0], yraw.at[0, 1], y_send.at[1, 0], y_recv.at[1, 0], sibling)
    for r in range(4):
        x_go(r, 0)

    def split(v):
        hi = v.astype(BF16).astype(F32)
        return hi, v - hi

    sub128 = lax.broadcasted_iota(jnp.int32, (8, YB), 0)

    def turn_y(slot):
        hi, lo = split(yraw[slot // 2, slot % 2, 0:DIM])
        t1, rest = split(yraw[slot // 2, slot % 2, DIM : DIM + 8])
        t2, t3 = split(rest)
        extra = jnp.where(sub128 == 0, t1, jnp.where(sub128 == 1, t2, jnp.where(sub128 == 2, t3, 0.0)))
        at = slice(slot * YB, (slot + 1) * YB)
        yt[at, 0 : 2 * DIM] = jnp.concatenate([hi, hi], axis=0).T.astype(BF16)
        yt[at, 2 * DIM :] = jnp.concatenate([lo, extra, jnp.zeros((DIM - 8, YB), F32)], axis=0).T.astype(BF16)

    def ready_x(pair):
        for h in range(2):
            v = xraw[pair // (NX // 2), (pair % (NX // 2)) * 2 + h]
            hi = v.astype(BF16)
            lo = (v - hi.astype(F32)).astype(BF16)
            at = slice(h * XB, (h + 1) * XB)
            xaug[pair, 0:DIM, at] = hi
            xaug[pair, DIM : 2 * DIM, at] = lo
            xaug[pair, 2 * DIM : 3 * DIM, at] = hi

    CH = 2 * YB
    PW = 2 * XB
    NPAIR = NQ // 2

    def rows_at(c):
        return pl.ds(pl.multiple_of(c * CH, CH), CH)

    def max_stage(pair, c, accs):
        block = scores.at[pair, rows_at(c)]
        accs = list(accs)
        for k in range(CH // 8):
            accs[k % 2] = jnp.maximum(accs[k % 2], block[k * 8 : k * 8 + 8])
        return accs

    def exp_stage(pair, c, top, accs):
        block = scores.at[pair, rows_at(c)]
        accs = list(accs)
        for k in range(CH // 8):
            accs[k % 2] = accs[k % 2] + jnp.exp2(block[k * 8 : k * 8 + 8] - top)
        return accs

    def dots(pair, lo, hi):
        at = slice(lo * CH, hi * CH)
        scores[pair, at] = jnp.dot(yt[at], xaug[pair], preferred_element_type=F32)

    def sibling_wait(dz):
        arrived(yraw.at[dz, 1], y_send.at[1, 0], y_recv.at[1, dz])
        turn_y(2 * dz + 1)

    turn_y(0)
    for d in range(NZ // 2):
        y_wait(d)
        y_go(d + 1)
        got = sorted({d + 1, NZ - d - 1})
        for dz in got:
            send(yraw.at[dz, 0], yraw.at[dz, 1], y_send.at[1, dz], y_recv.at[1, dz], sibling)
        if d == 0:
            for r in (0, 1):
                x_wait(r, 0)
                x_go(r, 1)
        if d == min(1, NZ // 2 - 1):
            for r in (0, 1):
                x_wait(r, 1)
                x_go(4 + r, 0)
        for dz in got:
            turn_y(2 * dz)
        if d == 0:
            sibling_wait(0)
            x_wait(2, 0)
            ready_x(0)
            dots(0, 0, 1)
        else:
            for dz in (d, NZ - d):
                sibling_wait(dz)
            dots(0, d, d + 1)
            dots(0, NZ - d, NZ - d + 1)
    for r in (3, 4, 5):
        x_wait(r, 0)
    for r in (6, 7):
        x_go(r, 1)
    sibling_wait(NZ // 2)
    dots(0, NZ // 2, NZ // 2 + 1)
    low = jnp.full((8, PW), -3e38, F32)
    zero = jnp.zeros((8, PW), F32)

    def row_step(one, two, three, top):
        tops, sums = (low, low), (zero, zero)
        for c in range(NZ):
            if one is not None and c % 4 == 0:
                dots(one, c, min(c + 4, NZ))
            if three is not None:
                sums = exp_stage(three, c, top, sums)
            if two is not None:
                tops = max_stage(two, c, tops)
        if three is not None:
            row8[three, 0] = top
            row8[three, 1] = sums[0] + sums[1]
        return jnp.maximum(*tops)

    early = [0] + ([NX // 2, NPAIR - NX // 2] if NX > 2 else [])
    pairs = early + [p for p in range(NPAIR) if p not in early]
    top = None
    for step in range(1, NPAIR + 2):
        if step == len(early):
            for r in (6, 7):
                x_wait(r, 1)
        one, two, three = [pairs[k] if 0 <= k < NPAIR else None for k in (step, step - 1, step - 2)]
        if one is not None:
            ready_x(one)
        top = row_step(one, two, three, top)

    def log2(v):
        return jnp.log(v) * LOG2E

    def lse(values):
        best = functools.reduce(jnp.maximum, values)
        return best + log2(functools.reduce(jnp.add, [jnp.exp2(v - best) for v in values]))

    for pair in range(NPAIR):
        best = jnp.max(row8[pair, 0], axis=0, keepdims=True)
        local = best + log2(jnp.sum(row8[pair, 1] * jnp.exp2(row8[pair, 0] - best), axis=0, keepdims=True))
        for h in range(2):
            rl[0, 2 * pair + h] = local[:, h * XB : (h + 1) * XB]
    rl[0, NQ] = log_a * LOG2E
    for e in others(NX):
        back = (NX - e) % NX
        send(rl.at[0, 0 : NQ + 1], rx.at[back], rx_send.at[e], rx_recv.at[back], along_x(e))
    for e in others(NX):
        arrived(rx.at[e], rx_send.at[e], rx_recv.at[e])
    for dy in range(NY):
        for dx in range(NX):
            rl[1, dy * NX + dx] = lse(
                [rl[0, dy * NX + dx]] + [rx[e, dy * NX + (dx - e) % NX] for e in range(1, NX)]
            )
    rl[1, NQ] = rl[0, NQ]
    for e in range(1, NX):
        rl[1, NQ + e] = rx[e, NQ]
    for e in others(NY):
        back = (NY - e) % NY
        send(rl.at[1], ry.at[back], ry_send.at[e], ry_recv.at[back], along_y(e))
    for e in others(NY):
        arrived(ry.at[e], ry_send.at[e], ry_recv.at[e])
    for dy in range(NY):
        for dx in range(NX):
            k = dy * NX + dx
            full = lse([rl[1, k]] + [ry[e, ((dy - e) % NY) * NX + dx] for e in range(1, NY)])
            mass = rl[1, NQ + dx] if dy == 0 else ry[dy, NQ + dx]
            rfull[:, k * XB : (k + 1) * XB] = jnp.broadcast_to(mass - full, (8, XB))
            if k == 0:
                row_out[...] = xsq - (EPSILON * LN2) * full

    eye = lax.broadcasted_iota(jnp.int32, (YB, YB), 0) == lax.broadcasted_iota(jnp.int32, (YB, YB), 1)
    per = PW // 128

    def across(v):
        return jnp.sum(jnp.where(eye, v, 0.0), axis=0, keepdims=True)

    def rows_of(b):
        return pl.ds(pl.multiple_of(b * YB, YB), YB)

    def lanes(l):
        return slice((l % per) * 128, (l % per + 1) * 128)

    def col_tiles(b):
        blocks = [scores.at[pair, rows_of(b)] for pair in range(NPAIR)]
        cblock, sblock = cstat.at[rows_of(b)], sstat.at[rows_of(b)]
        for t in range(YB // 8):
            r8 = slice(t * 8, (t + 1) * 8)
            vals = [blocks[l // per][r8, lanes(l)] + rfull[:, l * 128 : (l + 1) * 128] for l in range(NL)]
            tops = vals
            while len(tops) > 1:
                tops = [jnp.maximum(tops[i], tops[i + 1]) for i in range(0, len(tops), 2)]
            top = tops[0]
            sums = [None] * 4
            for l in range(NL):
                e = jnp.exp2(vals[l] - top)
                blocks[l // per][r8, lanes(l)] = e
                sums[l % 4] = e if l < 4 else sums[l % 4] + e
            cblock[r8] = top
            sblock[r8] = (sums[0] + sums[1]) + (sums[2] + sums[3])

    def put_stats(b):
        c = cstat[rows_of(b), :]
        best = jnp.max(c, axis=1, keepdims=True)
        summed = jnp.sum(sstat[rows_of(b), :] * jnp.exp2(c - best), axis=1, keepdims=True)
        cl[0, b] = across(best) + log2(across(summed))

    def col_loop(b):
        put_stats(b - 1)
        col_tiles(b)

    col_tiles(0)
    loop(1, NP, col_loop)
    put_stats(NP - 1)

    cl[0, NP] = log_b * LOG2E
    send(cl.at[0, 0 : NP + 1], cc, cc_send, cc_recv, sibling)
    arrived(cc, cc_send, cc_recv)
    for dz in range(NZ):
        for dc in range(2):
            cl[1, 2 * dz + dc] = lse([cl[0, 2 * dz + dc], cc[2 * dz + 1 - dc]])
    cl[1, NP] = cl[0, NP]
    cl[1, NP + 1] = cc[NP]
    for e in others(NZ):
        back = (NZ - e) % NZ
        send(cl.at[1], cz.at[back], cz_send.at[e], cz_recv.at[back], along_z(e))
    for e in others(NZ):
        arrived(cz.at[e], cz_send.at[e], cz_recv.at[e])
    for dz in range(NZ):
        for dc in range(2):
            k = 2 * dz + dc
            full = lse([cl[1, k]] + [cz[e, 2 * ((dz - e) % NZ) + dc] for e in range(1, NZ)])
            mass = cl[1, NP + dc] if dz == 0 else cz[dz, NP + dc]
            cl[2, k] = mass - full
            if k == 0:
                col_out[...] = previous[...] + EPSILON * log_b - (EPSILON * LN2) * full

    def factors(b):
        q = jnp.sum(jnp.where(eye, cl[2, b], 0.0), axis=1, keepdims=True)
        gbuf[b % 2] = jnp.exp2(cstat[rows_of(b), :] + q)

    def gap_loop(b, acc):
        blocks = [scores.at[pair, rows_of(b)] for pair in range(NPAIR)]
        gblock = gbuf.at[b % 2]
        for t in range(YB // 8):
            r8 = slice(t * 8, (t + 1) * 8)
            g = gblock[r8]
            acc = [acc[l] + blocks[l // per][r8, lanes(l)] * g for l in range(NL)]
            if t == YB // 16:
                factors(jnp.minimum(b + 1, NP - 1))
        return acc

    factors(0)
    acc = lax.fori_loop(0, NP, gap_loop, [jnp.zeros((8, 128), F32) for _ in range(NL)])
    for k in range(NQ):
        for h in range(2):
            w[k // NX, k % NX, :, h * 128 : (h + 1) * 128] = jnp.sum(acc[2 * k + h], axis=0, keepdims=True)
    for e in others(NX):
        back = (NX - e) % NX
        send(w.at[:, e], wx.at[back], wx_send.at[e], wx_recv.at[back], along_x(e))
    for e in others(NX):
        arrived(wx.at[e], wx_send.at[e], wx_recv.at[e])
    for dy in range(NY):
        w[dy, 0] = functools.reduce(jnp.add, [w[dy, 0]] + [wx[e, dy] for e in range(1, NX)])
    for e in others(NY):
        back = (NY - e) % NY
        send(w.at[e, 0], wy.at[back], wy_send.at[e], wy_recv.at[back], along_y(e))
    for e in others(NY):
        arrived(wy.at[e], wy_send.at[e], wy_recv.at[e])
    gap_out[...] = jnp.log(functools.reduce(jnp.add, [w[0, 0]] + [wy[e] for e in range(1, NY)])) - log_a

    for c in pending:
        c.wait_send()


def put_results(row, col, gap, row_out, col_out, gap_out, sem):
    copies = [
        pltpu.make_async_copy(src, dst, sem.at[n])
        for n, (src, dst) in enumerate([(row, row_out), (col, col_out), (gap, gap_out)])
    ]
    for c in copies:
        c.start()
    for c in copies:
        c.wait()


def body(measured, generated, previous, row_weight, col_weight):
    NZ, NY, NX = GRID["z"], GRID["y"], GRID["xh"] * GRID["xl"]
    NQ, NP = NX * NY, NZ * 2
    NJ, NI = NP * YB, NQ * XB
    dma = pltpu.SemaphoreType.DMA
    row, col, gap = pl.pallas_call(
        kernel,
        out_shape=(
            jax.ShapeDtypeStruct((1, XB), F32),
            jax.ShapeDtypeStruct((1, YB), F32),
            jax.ShapeDtypeStruct((1, XB), F32),
        ),
        in_specs=[pl.BlockSpec(memory_space=pltpu.HBM)] * 5,
        out_specs=(pl.BlockSpec(memory_space=pltpu.VMEM),) * 3,
        scratch_shapes=[
            pltpu.VMEM((DIM, XB), F32),
            pltpu.VMEM((DIM, YB), F32),
            pltpu.VMEM((1, YB), F32),
            pltpu.VMEM((1, XB), F32),
            pltpu.VMEM((1, YB), F32),
            pltpu.VMEM((NY, NX, DIM, XB), F32),
            pltpu.VMEM((NZ, 2, DIM + 8, YB), F32),
            pltpu.VMEM((NJ, 4 * DIM), BF16),
            pltpu.VMEM((NQ // 2, 4 * DIM, 2 * XB), BF16),
            pltpu.VMEM((NQ // 2, NJ, 2 * XB), F32),
            pltpu.VMEM((NQ // 2, 2, 8, 2 * XB), F32),
            pltpu.VMEM((NJ, 128), F32),
            pltpu.VMEM((NJ, 128), F32),
            pltpu.VMEM((2, YB, 128), F32),
            pltpu.VMEM((2, NQ + NX, 1, XB), F32),
            pltpu.VMEM((NX, NQ + 1, 1, XB), F32),
            pltpu.VMEM((NY, NQ + NX, 1, XB), F32),
            pltpu.VMEM((8, NI), F32),
            pltpu.VMEM((3, NP + 2, 1, YB), F32),
            pltpu.VMEM((NP + 1, 1, YB), F32),
            pltpu.VMEM((NZ, NP + 2, 1, YB), F32),
            pltpu.VMEM((NY, NX, 1, XB), F32),
            pltpu.VMEM((NX, NY, 1, XB), F32),
            pltpu.VMEM((NY, 1, XB), F32),
            dma((5,)),
            dma((8, NX)),
            dma((8, NX)),
            dma((2, NZ)),
            dma((2, NZ)),
            dma((NX,)),
            dma((NX,)),
            dma((NY,)),
            dma((NY,)),
            dma,
            dma,
            dma((NZ,)),
            dma((NZ,)),
            dma((NX,)),
            dma((NX,)),
            dma((NY,)),
            dma((NY,)),
        ],
        compiler_params=pltpu.CompilerParams(
            collective_id=0, has_side_effects=True, vmem_limit_bytes=46 * 1024 * 1024
        ),
    )(
        *[
            pltpu.with_memory_space_constraint(v, pltpu.HBM)
            for v in (
                measured,
                generated,
                previous.reshape(1, YB),
                row_weight.reshape(1, XB),
                col_weight.reshape(1, YB),
            )
        ]
    )
    row, col, gap = pl.pallas_call(
        put_results,
        out_shape=(
            jax.ShapeDtypeStruct((1, XB), F32),
            jax.ShapeDtypeStruct((1, YB), F32),
            jax.ShapeDtypeStruct((1, XB), F32),
        ),
        in_specs=[pl.BlockSpec(memory_space=pltpu.VMEM)] * 3,
        out_specs=(pl.BlockSpec(memory_space=pl.ANY),) * 3,
        scratch_shapes=[dma((3,))],
        compiler_params=pltpu.CompilerParams(vmem_limit_bytes=1024 * 1024),
    )(row, col, gap)
    return row.reshape(XB), col.reshape(YB), gap.reshape(XB)


def solution(mesh):
    placed = (
        P(None, ("row", "col")),
        P(None, ("col", "row")),
        P(("col", "row")),
        P(("row", "col")),
        P(("col", "row")),
    )
    return jax.shard_map(
        body,
        mesh=mesh,
        in_specs=placed,
        out_specs=(P(("row", "col")), P(("col", "row")), P(("row", "col"))),
        check_vma=False,
    )
```

```python
import functools
import math

import jax
import jax.numpy as jnp
from jax import lax
from jax.experimental import pallas as pl
from jax.experimental.pallas import tpu as pltpu
from jax.sharding import PartitionSpec as P

EPSILON = 0.1
LOG2E = 1.0 / math.log(2.0)
LN2 = math.log(2.0)
MESH = pl.DeviceIdType.MESH
F32 = jnp.float32
BF16 = jnp.bfloat16

GRID = {"z": 8, "y": 4, "xh": 2, "xl": 2}
XB = 256
YB = 128
DIM = 64


def kernel(
    measured_hbm,
    generated_hbm,
    previous_hbm,
    row_weight_hbm,
    col_weight_hbm,
    row_out,
    col_out,
    gap_out,
    measured,
    generated,
    previous,
    row_weight,
    col_weight,
    xraw,
    yraw,
    yt,
    xaug,
    scores,
    row8,
    cstat,
    sstat,
    gbuf,
    rl,
    rx,
    ry,
    rfull,
    cl,
    cc,
    cz,
    w,
    wx,
    wy,
    in_sem,
    x_send,
    x_recv,
    y_send,
    y_recv,
    rx_send,
    rx_recv,
    ry_send,
    ry_recv,
    cc_send,
    cc_recv,
    cz_send,
    cz_recv,
    wx_send,
    wx_recv,
    wy_send,
    wy_recv,
):
    NZ, NY, NXH, NXL = GRID["z"], GRID["y"], GRID["xh"], GRID["xl"]
    NX = NXH * NXL
    NQ, NP = NX * NY, NZ * 2
    NI = NQ * XB
    NL = NI // 128
    ndev = NQ * NP

    loads = [
        pltpu.make_async_copy(src, dst, in_sem.at[n])
        for n, (src, dst) in enumerate(
            [
                (generated_hbm, generated),
                (previous_hbm, previous),
                (col_weight_hbm, col_weight),
                (measured_hbm, measured),
                (row_weight_hbm, row_weight),
            ]
        )
    ]
    for c in loads:
        c.start()

    row = lax.axis_index("row")
    col = lax.axis_index("col")
    z = row // (NY * NXH)
    y = (row // NXH) % NY
    x = (row % NXH) * NXL + col // 2
    core = col % 2

    def device(dz, dy, dx, dc):
        zz, yy, xx = (z + dz) % NZ, (y + dy) % NY, (x + dx) % NX
        return ((zz * NY + yy) * NXH + xx // NXL, (xx % NXL) * 2 + (core + dc) % 2)

    def copy(src, dst, send, recv, dev):
        return pltpu.make_async_remote_copy(
            src_ref=src, dst_ref=dst, send_sem=send, recv_sem=recv, device_id=dev, device_id_type=MESH
        )

    def loop(lo, hi, fn):
        def step(k, carry):
            fn(k)
            return carry

        lax.fori_loop(lo, hi, step, 0)

    def others(size):
        return sorted(range(1, size), key=lambda d: min(d, size - d))

    def along_x(e):
        return device(0, 0, e, 0)

    def along_y(e):
        return device(0, e, 0, 0)

    def along_z(e):
        return device(e, 0, 0, 0)

    sibling = device(0, 0, 0, 1)
    partners = [along_x(e) for e in others(NX)] + [along_y(e) for e in others(NY)]
    partners += [along_z(e) for e in others(NZ)] + [sibling]
    barrier = pltpu.get_barrier_semaphore()
    for dev in partners:
        pl.semaphore_signal(barrier, inc=1, device_id=dev, device_id_type=MESH)

    for c in loads:
        c.wait()
    scale = 2.0 * LOG2E / EPSILON
    xraw[0, 0] = measured[...] * scale
    gen = generated[...]
    log_b = jnp.log(col_weight[...]) - math.log(YB * ndev)
    ysq = jnp.sum(gen * gen, axis=0, keepdims=True)
    u = (log_b + (previous[...] - ysq) / EPSILON) * LOG2E
    yraw[0, 0, 0:DIM] = gen
    yraw[0, 0, DIM : DIM + 8] = jnp.broadcast_to(u, (8, YB))
    log_a = jnp.log(row_weight[...]) - math.log(XB * ndev)
    xsq = jnp.sum(measured[...] * measured[...], axis=0, keepdims=True)
    xaug[:, 3 * DIM :] = jnp.ones((NQ // 2, DIM, 2 * XB), BF16)

    pl.semaphore_wait(barrier, len(partners))

    pending = []

    def send(src, dst, send_sem, recv_sem, dev):
        c = copy(src, dst, send_sem, recv_sem, dev)
        c.start()
        pending.append(c)

    def arrived(ref, send_sem, recv_sem):
        copy(ref, ref, send_sem, recv_sem, sibling).wait_recv()

    first, second = slice(0, DIM // 2), slice(DIM // 2, DIM)

    for e in others(NZ):
        back = (NZ - e) % NZ
        send(yraw.at[0, 0], yraw.at[back, 0], y_send.at[0, e], y_recv.at[back, 0], along_z(e))
    send(yraw.at[0, 0], yraw.at[0, 1], y_send.at[0, 0], y_recv.at[0, 1], sibling)
    for e in others(NX):
        back = (NX - e) % NX
        send(xraw.at[0, 0, first], xraw.at[0, back, first], x_send.at[0, e], x_recv.at[0, back], along_x(e))
        send(xraw.at[0, 0, second], xraw.at[back, 0, second], x_send.at[1, e], x_recv.at[1, back], along_y(e))
    for e in others(NX):
        back = (NX - e) % NX
        send(xraw.at[0, 0, second], xraw.at[0, back, second], x_send.at[2, e], x_recv.at[2, back], along_x(e))
        send(xraw.at[0, 0, first], xraw.at[back, 0, first], x_send.at[3, e], x_recv.at[3, back], along_y(e))

    def forward_x():
        for e in others(NX):
            arrived(xraw.at[0, e, first], x_send.at[0, e], x_recv.at[0, e])
            arrived(xraw.at[e, 0, second], x_send.at[1, e], x_recv.at[1, e])
        for e in others(NX):
            back = (NX - e) % NX
            send(xraw.at[0, 1:, first], xraw.at[back, 1:, first], x_send.at[4, e], x_recv.at[4, back], along_y(e))
            send(xraw.at[1:, 0, second], xraw.at[1:, back, second], x_send.at[5, e], x_recv.at[5, back], along_x(e))

    def split(v):
        hi = v.astype(BF16).astype(F32)
        return hi, v - hi

    sub128 = lax.broadcasted_iota(jnp.int32, (8, YB), 0)

    def turn_y(slot):
        hi, lo = split(yraw[slot // 2, slot % 2, 0:DIM])
        t1, rest = split(yraw[slot // 2, slot % 2, DIM : DIM + 8])
        t2, t3 = split(rest)
        extra = jnp.where(sub128 == 0, t1, jnp.where(sub128 == 1, t2, jnp.where(sub128 == 2, t3, 0.0)))
        at = slice(slot * YB, (slot + 1) * YB)
        yt[at, 0 : 2 * DIM] = jnp.concatenate([hi, hi], axis=0).T.astype(BF16)
        yt[at, 2 * DIM :] = jnp.concatenate([lo, extra, jnp.zeros((DIM - 8, YB), F32)], axis=0).T.astype(BF16)

    def ready_x(pair):
        for h in range(2):
            v = xraw[pair // (NX // 2), (pair % (NX // 2)) * 2 + h]
            hi = v.astype(BF16)
            lo = (v - hi.astype(F32)).astype(BF16)
            at = slice(h * XB, (h + 1) * XB)
            xaug[pair, 0:DIM, at] = hi
            xaug[pair, DIM : 2 * DIM, at] = lo
            xaug[pair, 2 * DIM : 3 * DIM, at] = hi

    CH = 2 * YB
    PW = 2 * XB
    NPAIR = NQ // 2

    def rows_at(c):
        return pl.ds(pl.multiple_of(c * CH, CH), CH)

    low = jnp.full((8, PW), -3e38, F32)
    zero = jnp.zeros((8, PW), F32)

    def dot_stage(pair, c, tops):
        res = jnp.dot(yt[rows_at(c)], xaug[pair], preferred_element_type=F32)
        scores[pair, rows_at(c)] = res
        tops = list(tops)
        for k in range(CH // 8):
            tops[k % 2] = jnp.maximum(tops[k % 2], res[k * 8 : k * 8 + 8])
        return tops

    def exp_stage(pair, c, top, accs):
        block = scores.at[pair, rows_at(c)]
        accs = list(accs)
        for k in range(CH // 8):
            accs[k % 2] = accs[k % 2] + jnp.exp2(block[k * 8 : k * 8 + 8] - top)
        return accs

    turn_y(0)
    tops0 = [low, low]
    batches = [(1, 3), (NZ - 2, NZ), (3, NZ - 2)] if NZ == 8 else [(1, NZ)]
    for n in range(len(batches) + 1):
        if n < len(batches):
            lo, hi = batches[n]
            for dz in range(lo, hi):
                arrived(yraw.at[dz, 0], y_send.at[0, dz], y_recv.at[dz, 0])
            send(yraw.at[lo:hi, 0], yraw.at[lo:hi, 1], y_send.at[1, lo], y_recv.at[lo, 1], sibling)
            for dz in range(lo, hi):
                turn_y(2 * dz)
        if n == 0:
            forward_x()
            for e in others(NX):
                arrived(xraw.at[0, e, second], x_send.at[2, e], x_recv.at[2, e])
            ready_x(0)
            if NX > 2:
                ready_x(1)
            arrived(yraw.at[0, 1], y_send.at[0, 0], y_recv.at[0, 1])
            turn_y(1)
            tops0 = dot_stage(0, 0, tops0)
        else:
            lo, hi = batches[n - 1]
            arrived(yraw.at[lo:hi, 1], y_send.at[1, lo], y_recv.at[lo, 1])
            for dz in range(lo, hi):
                turn_y(2 * dz + 1)
            for dz in range(lo, hi):
                tops0 = dot_stage(0, dz, tops0)

    def row_step(one, two, top):
        tops, sums = (low, low), (zero, zero)
        for c in range(NZ):
            sums = exp_stage(two, c, top, sums)
            if one is not None:
                tops = dot_stage(one, c, tops)
        row8[two, 0] = top
        row8[two, 1] = sums[0] + sums[1]
        return jnp.maximum(*tops)

    def row_loop(step, top):
        ready_x(step)
        return row_step(step, step - 1, top)

    def last_x():
        for e in others(NX):
            arrived(xraw.at[e, 0, first], x_send.at[3, e], x_recv.at[3, e])
            arrived(xraw.at[e, 1:, first], x_send.at[4, e], x_recv.at[4, e])
            arrived(xraw.at[1:, e, second], x_send.at[5, e], x_recv.at[5, e])

    if NX == 2:
        last_x()
        ready_x(1)
    top = row_step(1, 0, jnp.maximum(*tops0))
    if NX > 2:
        last_x()
    top = lax.fori_loop(2, NPAIR, row_loop, top)
    row_step(None, NPAIR - 1, top)

    def log2(v):
        return jnp.log(v) * LOG2E

    def lse(values):
        best = functools.reduce(jnp.maximum, values)
        return best + log2(functools.reduce(jnp.add, [jnp.exp2(v - best) for v in values]))

    for pair in range(NPAIR):
        best = jnp.max(row8[pair, 0], axis=0, keepdims=True)
        local = best + log2(jnp.sum(row8[pair, 1] * jnp.exp2(row8[pair, 0] - best), axis=0, keepdims=True))
        for h in range(2):
            rl[0, 2 * pair + h] = local[:, h * XB : (h + 1) * XB]
    rl[0, NQ] = log_a * LOG2E
    for e in others(NX):
        back = (NX - e) % NX
        send(rl.at[0, 0 : NQ + 1], rx.at[back], rx_send.at[e], rx_recv.at[back], along_x(e))
    for e in others(NX):
        arrived(rx.at[e], rx_send.at[e], rx_recv.at[e])
    for dy in range(NY):
        for dx in range(NX):
            rl[1, dy * NX + dx] = lse(
                [rl[0, dy * NX + dx]] + [rx[e, dy * NX + (dx - e) % NX] for e in range(1, NX)]
            )
    rl[1, NQ] = rl[0, NQ]
    for e in range(1, NX):
        rl[1, NQ + e] = rx[e, NQ]
    for e in others(NY):
        back = (NY - e) % NY
        send(rl.at[1], ry.at[back], ry_send.at[e], ry_recv.at[back], along_y(e))
    for e in others(NY):
        arrived(ry.at[e], ry_send.at[e], ry_recv.at[e])
    for dy in range(NY):
        for dx in range(NX):
            k = dy * NX + dx
            full = lse([rl[1, k]] + [ry[e, ((dy - e) % NY) * NX + dx] for e in range(1, NY)])
            mass = rl[1, NQ + dx] if dy == 0 else ry[dy, NQ + dx]
            rfull[:, k * XB : (k + 1) * XB] = jnp.broadcast_to(mass - full, (8, XB))
            if k == 0:
                row_out[...] = xsq - (EPSILON * LN2) * full

    eye = lax.broadcasted_iota(jnp.int32, (YB, YB), 0) == lax.broadcasted_iota(jnp.int32, (YB, YB), 1)
    per = PW // 128

    def across(v):
        return jnp.sum(jnp.where(eye, v, 0.0), axis=0, keepdims=True)

    def rows_of(b):
        return pl.ds(pl.multiple_of(b * YB, YB), YB)

    def lanes(l):
        return slice((l % per) * 128, (l % per + 1) * 128)

    def col_tiles(b):
        blocks = [scores.at[pair, rows_of(b)] for pair in range(NPAIR)]
        cblock, sblock = cstat.at[rows_of(b)], sstat.at[rows_of(b)]
        for t in range(YB // 8):
            r8 = slice(t * 8, (t + 1) * 8)
            vals = [blocks[l // per][r8, lanes(l)] + rfull[:, l * 128 : (l + 1) * 128] for l in range(NL)]
            tops = vals
            while len(tops) > 1:
                tops = [jnp.maximum(tops[i], tops[i + 1]) for i in range(0, len(tops), 2)]
            top = tops[0]
            sums = [None] * 4
            for l in range(NL):
                e = jnp.exp2(vals[l] - top)
                blocks[l // per][r8, lanes(l)] = e
                sums[l % 4] = e if l < 4 else sums[l % 4] + e
            cblock[r8] = top
            sblock[r8] = (sums[0] + sums[1]) + (sums[2] + sums[3])

    def put_stats(b):
        c = cstat[rows_of(b), :]
        best = jnp.max(c, axis=1, keepdims=True)
        summed = jnp.sum(sstat[rows_of(b), :] * jnp.exp2(c - best), axis=1, keepdims=True)
        cl[0, b] = across(best) + log2(across(summed))

    def col_loop(b):
        put_stats(b - 1)
        col_tiles(b)

    col_tiles(0)
    loop(1, NP, col_loop)
    put_stats(NP - 1)

    cl[0, NP] = log_b * LOG2E
    send(cl.at[0, 0 : NP + 1], cc, cc_send, cc_recv, sibling)
    arrived(cc, cc_send, cc_recv)
    for dz in range(NZ):
        for dc in range(2):
            cl[1, 2 * dz + dc] = lse([cl[0, 2 * dz + dc], cc[2 * dz + 1 - dc]])
    cl[1, NP] = cl[0, NP]
    cl[1, NP + 1] = cc[NP]
    for e in others(NZ):
        back = (NZ - e) % NZ
        send(cl.at[1], cz.at[back], cz_send.at[e], cz_recv.at[back], along_z(e))
    for e in others(NZ):
        arrived(cz.at[e], cz_send.at[e], cz_recv.at[e])
    for dz in range(NZ):
        for dc in range(2):
            k = 2 * dz + dc
            full = lse([cl[1, k]] + [cz[e, 2 * ((dz - e) % NZ) + dc] for e in range(1, NZ)])
            mass = cl[1, NP + dc] if dz == 0 else cz[dz, NP + dc]
            cl[2, k] = mass - full
            if k == 0:
                col_out[...] = previous[...] + EPSILON * log_b - (EPSILON * LN2) * full

    def factors(b):
        q = jnp.sum(jnp.where(eye, cl[2, b], 0.0), axis=1, keepdims=True)
        gbuf[b % 2] = jnp.exp2(cstat[rows_of(b), :] + q)

    def gap_loop(b, acc):
        blocks = [scores.at[pair, rows_of(b)] for pair in range(NPAIR)]
        gblock = gbuf.at[b % 2]
        for t in range(YB // 8):
            r8 = slice(t * 8, (t + 1) * 8)
            g = gblock[r8]
            acc = [acc[l] + blocks[l // per][r8, lanes(l)] * g for l in range(NL)]
            if t == YB // 16:
                factors(jnp.minimum(b + 1, NP - 1))
        return acc

    factors(0)
    acc = lax.fori_loop(0, NP, gap_loop, [jnp.zeros((8, 128), F32) for _ in range(NL)])
    for k in range(NQ):
        for h in range(2):
            w[k // NX, k % NX, :, h * 128 : (h + 1) * 128] = jnp.sum(acc[2 * k + h], axis=0, keepdims=True)
    for e in others(NX):
        back = (NX - e) % NX
        send(w.at[:, e], wx.at[back], wx_send.at[e], wx_recv.at[back], along_x(e))
    for e in others(NX):
        arrived(wx.at[e], wx_send.at[e], wx_recv.at[e])
    for dy in range(NY):
        w[dy, 0] = functools.reduce(jnp.add, [w[dy, 0]] + [wx[e, dy] for e in range(1, NX)])
    for e in others(NY):
        back = (NY - e) % NY
        send(w.at[e, 0], wy.at[back], wy_send.at[e], wy_recv.at[back], along_y(e))
    for e in others(NY):
        arrived(wy.at[e], wy_send.at[e], wy_recv.at[e])
    gap_out[...] = jnp.log(functools.reduce(jnp.add, [w[0, 0]] + [wy[e] for e in range(1, NY)])) - log_a

    for c in pending:
        c.wait_send()


def put_results(row, col, gap, row_out, col_out, gap_out, sem):
    copies = [
        pltpu.make_async_copy(src, dst, sem.at[n])
        for n, (src, dst) in enumerate([(row, row_out), (col, col_out), (gap, gap_out)])
    ]
    for c in copies:
        c.start()
    for c in copies:
        c.wait()


def body(measured, generated, previous, row_weight, col_weight):
    NZ, NY, NX = GRID["z"], GRID["y"], GRID["xh"] * GRID["xl"]
    NQ, NP = NX * NY, NZ * 2
    NJ, NI = NP * YB, NQ * XB
    dma = pltpu.SemaphoreType.DMA
    row, col, gap = pl.pallas_call(
        kernel,
        out_shape=(
            jax.ShapeDtypeStruct((1, XB), F32),
            jax.ShapeDtypeStruct((1, YB), F32),
            jax.ShapeDtypeStruct((1, XB), F32),
        ),
        in_specs=[pl.BlockSpec(memory_space=pltpu.HBM)] * 5,
        out_specs=(pl.BlockSpec(memory_space=pltpu.VMEM),) * 3,
        scratch_shapes=[
            pltpu.VMEM((DIM, XB), F32),
            pltpu.VMEM((DIM, YB), F32),
            pltpu.VMEM((1, YB), F32),
            pltpu.VMEM((1, XB), F32),
            pltpu.VMEM((1, YB), F32),
            pltpu.VMEM((NY, NX, DIM, XB), F32),
            pltpu.VMEM((NZ, 2, DIM + 8, YB), F32),
            pltpu.VMEM((NJ, 4 * DIM), BF16),
            pltpu.VMEM((NQ // 2, 4 * DIM, 2 * XB), BF16),
            pltpu.VMEM((NQ // 2, NJ, 2 * XB), F32),
            pltpu.VMEM((NQ // 2, 2, 8, 2 * XB), F32),
            pltpu.VMEM((NJ, 128), F32),
            pltpu.VMEM((NJ, 128), F32),
            pltpu.VMEM((2, YB, 128), F32),
            pltpu.VMEM((2, NQ + NX, 1, XB), F32),
            pltpu.VMEM((NX, NQ + 1, 1, XB), F32),
            pltpu.VMEM((NY, NQ + NX, 1, XB), F32),
            pltpu.VMEM((8, NI), F32),
            pltpu.VMEM((3, NP + 2, 1, YB), F32),
            pltpu.VMEM((NP + 1, 1, YB), F32),
            pltpu.VMEM((NZ, NP + 2, 1, YB), F32),
            pltpu.VMEM((NY, NX, 1, XB), F32),
            pltpu.VMEM((NX, NY, 1, XB), F32),
            pltpu.VMEM((NY, 1, XB), F32),
            dma((5,)),
            dma((6, NX)),
            dma((6, NX)),
            dma((2, NZ)),
            dma((NZ, 2)),
            dma((NX,)),
            dma((NX,)),
            dma((NY,)),
            dma((NY,)),
            dma,
            dma,
            dma((NZ,)),
            dma((NZ,)),
            dma((NX,)),
            dma((NX,)),
            dma((NY,)),
            dma((NY,)),
        ],
        compiler_params=pltpu.CompilerParams(
            collective_id=0, has_side_effects=True, vmem_limit_bytes=46 * 1024 * 1024
        ),
    )(
        *[
            pltpu.with_memory_space_constraint(v, pltpu.HBM)
            for v in (
                measured,
                generated,
                previous.reshape(1, YB),
                row_weight.reshape(1, XB),
                col_weight.reshape(1, YB),
            )
        ]
    )
    row, col, gap = pl.pallas_call(
        put_results,
        out_shape=(
            jax.ShapeDtypeStruct((1, XB), F32),
            jax.ShapeDtypeStruct((1, YB), F32),
            jax.ShapeDtypeStruct((1, XB), F32),
        ),
        in_specs=[pl.BlockSpec(memory_space=pltpu.VMEM)] * 3,
        out_specs=(pl.BlockSpec(memory_space=pl.ANY),) * 3,
        scratch_shapes=[dma((3,))],
        compiler_params=pltpu.CompilerParams(vmem_limit_bytes=1024 * 1024),
    )(row, col, gap)
    return row.reshape(XB), col.reshape(YB), gap.reshape(XB)


def solution(mesh):
    placed = (
        P(None, ("row", "col")),
        P(None, ("col", "row")),
        P(("col", "row")),
        P(("row", "col")),
        P(("col", "row")),
    )
    return jax.shard_map(
        body,
        mesh=mesh,
        in_specs=placed,
        out_specs=(P(("row", "col")), P(("col", "row")), P(("row", "col"))),
        check_vma=False,
    )
```

```python
import functools
import math

import jax
import jax.numpy as jnp
from jax import lax
from jax.experimental import pallas as pl
from jax.experimental.pallas import tpu as pltpu
from jax.sharding import PartitionSpec as P

EPSILON = 0.1
LOG2E = 1.0 / math.log(2.0)
LN2 = math.log(2.0)
MESH = pl.DeviceIdType.MESH
F32 = jnp.float32
BF16 = jnp.bfloat16

GRID = {"z": 8, "y": 4, "xh": 2, "xl": 2}
XB = 256
YB = 128
DIM = 64


def kernel(
    measured_hbm,
    generated_hbm,
    previous_hbm,
    row_weight_hbm,
    col_weight_hbm,
    row_out,
    col_out,
    gap_out,
    measured,
    generated,
    previous,
    row_weight,
    col_weight,
    xraw,
    yraw,
    yt,
    xaug,
    scores,
    row8,
    cstat,
    sstat,
    gbuf,
    rl,
    rx,
    ry,
    rfull,
    cl,
    cc,
    cz,
    w,
    wx,
    wy,
    in_sem,
    x_send,
    x_recv,
    y_send,
    y_recv,
    rx_send,
    rx_recv,
    ry_send,
    ry_recv,
    cc_send,
    cc_recv,
    cz_send,
    cz_recv,
    wx_send,
    wx_recv,
    wy_send,
    wy_recv,
):
    NZ, NY, NXH, NXL = GRID["z"], GRID["y"], GRID["xh"], GRID["xl"]
    NX = NXH * NXL
    NQ, NP = NX * NY, NZ * 2
    NI = NQ * XB
    NL = NI // 128
    ndev = NQ * NP

    loads = [
        pltpu.make_async_copy(src, dst, in_sem.at[n])
        for n, (src, dst) in enumerate(
            [
                (generated_hbm, generated),
                (previous_hbm, previous),
                (col_weight_hbm, col_weight),
                (measured_hbm, measured),
                (row_weight_hbm, row_weight),
            ]
        )
    ]
    for c in loads:
        c.start()

    row = lax.axis_index("row")
    col = lax.axis_index("col")
    z = row // (NY * NXH)
    y = (row // NXH) % NY
    x = (row % NXH) * NXL + col // 2
    core = col % 2

    def device(dz, dy, dx, dc):
        zz, yy, xx = (z + dz) % NZ, (y + dy) % NY, (x + dx) % NX
        return ((zz * NY + yy) * NXH + xx // NXL, (xx % NXL) * 2 + (core + dc) % 2)

    def copy(src, dst, send, recv, dev):
        return pltpu.make_async_remote_copy(
            src_ref=src, dst_ref=dst, send_sem=send, recv_sem=recv, device_id=dev, device_id_type=MESH
        )

    def loop(lo, hi, fn):
        def step(k, carry):
            fn(k)
            return carry

        lax.fori_loop(lo, hi, step, 0)

    def others(size):
        return sorted(range(1, size), key=lambda d: min(d, size - d))

    def along_x(e):
        return device(0, 0, e, 0)

    def along_y(e):
        return device(0, e, 0, 0)

    def along_z(e):
        return device(e, 0, 0, 0)

    sibling = device(0, 0, 0, 1)
    partners = [along_x(e) for e in others(NX)] + [along_y(e) for e in others(NY)]
    partners += [along_z(e) for e in others(NZ)] + [sibling]
    barrier = pltpu.get_barrier_semaphore()
    for dev in partners:
        pl.semaphore_signal(barrier, inc=1, device_id=dev, device_id_type=MESH)

    for c in loads:
        c.wait()
    scale = 2.0 * LOG2E / EPSILON
    xraw[0, 0] = measured[...] * scale
    gen = generated[...]
    log_b = jnp.log(col_weight[...]) - math.log(YB * ndev)
    ysq = jnp.sum(gen * gen, axis=0, keepdims=True)
    u = (log_b + (previous[...] - ysq) / EPSILON) * LOG2E
    yraw[0, 0, 0:DIM] = gen
    yraw[0, 0, DIM : DIM + 8] = jnp.broadcast_to(u, (8, YB))
    log_a = jnp.log(row_weight[...]) - math.log(XB * ndev)
    xsq = jnp.sum(measured[...] * measured[...], axis=0, keepdims=True)
    xaug[:, 3 * DIM :] = jnp.ones((NQ // 2, DIM, 2 * XB), BF16)

    pl.semaphore_wait(barrier, len(partners))

    pending = []

    def send(src, dst, send_sem, recv_sem, dev):
        c = copy(src, dst, send_sem, recv_sem, dev)
        c.start()
        pending.append(c)

    def arrived(ref, send_sem, recv_sem):
        copy(ref, ref, send_sem, recv_sem, sibling).wait_recv()

    first, second = slice(0, DIM // 2), slice(DIM // 2, DIM)

    for e in others(NZ):
        back = (NZ - e) % NZ
        send(yraw.at[0, 0], yraw.at[back, 0], y_send.at[0, e], y_recv.at[back, 0], along_z(e))
    send(yraw.at[0, 0], yraw.at[0, 1], y_send.at[0, 0], y_recv.at[0, 1], sibling)
    for e in others(NX):
        back = (NX - e) % NX
        send(xraw.at[0, 0, first], xraw.at[0, back, first], x_send.at[0, e], x_recv.at[0, back], along_x(e))
        send(xraw.at[0, 0, second], xraw.at[back, 0, second], x_send.at[1, e], x_recv.at[1, back], along_y(e))
    for e in others(NX):
        back = (NX - e) % NX
        send(xraw.at[0, 0, second], xraw.at[0, back, second], x_send.at[2, e], x_recv.at[2, back], along_x(e))
        send(xraw.at[0, 0, first], xraw.at[back, 0, first], x_send.at[3, e], x_recv.at[3, back], along_y(e))

    def forward_x():
        for e in others(NX):
            arrived(xraw.at[0, e, first], x_send.at[0, e], x_recv.at[0, e])
            arrived(xraw.at[e, 0, second], x_send.at[1, e], x_recv.at[1, e])
        for e in others(NX):
            back = (NX - e) % NX
            send(xraw.at[0, 1:, first], xraw.at[back, 1:, first], x_send.at[4, e], x_recv.at[4, back], along_y(e))
            send(xraw.at[1:, 0, second], xraw.at[1:, back, second], x_send.at[5, e], x_recv.at[5, back], along_x(e))

    def split(v):
        hi = v.astype(BF16).astype(F32)
        return hi, v - hi

    sub128 = lax.broadcasted_iota(jnp.int32, (8, YB), 0)

    def turn_y(slot):
        hi, lo = split(yraw[slot // 2, slot % 2, 0:DIM])
        t1, rest = split(yraw[slot // 2, slot % 2, DIM : DIM + 8])
        t2, t3 = split(rest)
        extra = jnp.where(sub128 == 0, t1, jnp.where(sub128 == 1, t2, jnp.where(sub128 == 2, t3, 0.0)))
        at = slice(slot * YB, (slot + 1) * YB)
        yt[at, 0 : 2 * DIM] = jnp.concatenate([hi, hi], axis=0).astype(BF16).T
        yt[at, 2 * DIM :] = jnp.concatenate([lo, extra, jnp.zeros((DIM - 8, YB), F32)], axis=0).astype(BF16).T

    def ready_x(pair):
        for h in range(2):
            v = xraw[pair // (NX // 2), (pair % (NX // 2)) * 2 + h]
            hi = v.astype(BF16)
            lo = (v - hi.astype(F32)).astype(BF16)
            at = slice(h * XB, (h + 1) * XB)
            xaug[pair, 0:DIM, at] = hi
            xaug[pair, DIM : 2 * DIM, at] = lo
            xaug[pair, 2 * DIM : 3 * DIM, at] = hi

    CH = 2 * YB
    PW = 2 * XB
    NPAIR = NQ // 2

    def rows_at(c):
        return pl.ds(pl.multiple_of(c * CH, CH), CH)

    low = jnp.full((8, PW), -3e38, F32)
    zero = jnp.zeros((8, PW), F32)

    def dot_stage(pair, c, tops):
        res = jnp.dot(yt[rows_at(c)], xaug[pair], preferred_element_type=F32)
        scores[pair, rows_at(c)] = res
        tops = list(tops)
        for k in range(CH // 8):
            tops[k % 2] = jnp.maximum(tops[k % 2], res[k * 8 : k * 8 + 8])
        return tops

    def exp_stage(pair, c, top, accs):
        block = scores.at[pair, rows_at(c)]
        accs = list(accs)
        for k in range(CH // 8):
            accs[k % 2] = accs[k % 2] + jnp.exp2(block[k * 8 : k * 8 + 8] - top)
        return accs

    turn_y(0)
    tops0 = [low, low]
    batches = [(1, 3), (NZ - 2, NZ), (3, NZ - 2)] if NZ == 8 else [(1, NZ)]
    for n in range(len(batches) + 1):
        if n < len(batches):
            lo, hi = batches[n]
            for dz in range(lo, hi):
                arrived(yraw.at[dz, 0], y_send.at[0, dz], y_recv.at[dz, 0])
            send(yraw.at[lo:hi, 0], yraw.at[lo:hi, 1], y_send.at[1, lo], y_recv.at[lo, 1], sibling)
            for dz in range(lo, hi):
                turn_y(2 * dz)
        if n == 0:
            forward_x()
            for e in others(NX):
                arrived(xraw.at[0, e, second], x_send.at[2, e], x_recv.at[2, e])
            ready_x(0)
            if NX > 2:
                ready_x(1)
            arrived(yraw.at[0, 1], y_send.at[0, 0], y_recv.at[0, 1])
            turn_y(1)
            tops0 = dot_stage(0, 0, tops0)
        else:
            lo, hi = batches[n - 1]
            arrived(yraw.at[lo:hi, 1], y_send.at[1, lo], y_recv.at[lo, 1])
            for dz in range(lo, hi):
                turn_y(2 * dz + 1)
            for dz in range(lo, hi):
                tops0 = dot_stage(0, dz, tops0)

    def row_step(one, two, top):
        tops, sums = (low, low), (zero, zero)
        for c in range(NZ):
            sums = exp_stage(two, c, top, sums)
            if one is not None:
                tops = dot_stage(one, c, tops)
        row8[two, 0] = top
        row8[two, 1] = sums[0] + sums[1]
        return jnp.maximum(*tops)

    def row_loop(step, top):
        ready_x(step)
        return row_step(step, step - 1, top)

    def last_x():
        for e in others(NX):
            arrived(xraw.at[e, 0, first], x_send.at[3, e], x_recv.at[3, e])
            arrived(xraw.at[e, 1:, first], x_send.at[4, e], x_recv.at[4, e])
            arrived(xraw.at[1:, e, second], x_send.at[5, e], x_recv.at[5, e])

    if NX == 2:
        last_x()
        ready_x(1)
    top = row_step(1, 0, jnp.maximum(*tops0))
    if NX > 2:
        last_x()
    for step in range(2, NPAIR):
        top = row_loop(step, top)
    row_step(None, NPAIR - 1, top)

    def log2(v):
        return jnp.log(v) * LOG2E

    def lse(values):
        best = functools.reduce(jnp.maximum, values)
        return best + log2(functools.reduce(jnp.add, [jnp.exp2(v - best) for v in values]))

    for pair in range(NPAIR):
        best = jnp.max(row8[pair, 0], axis=0, keepdims=True)
        local = best + log2(jnp.sum(row8[pair, 1] * jnp.exp2(row8[pair, 0] - best), axis=0, keepdims=True))
        for h in range(2):
            rl[0, 2 * pair + h] = local[:, h * XB : (h + 1) * XB]
    rl[0, NQ] = log_a * LOG2E
    for e in others(NX):
        back = (NX - e) % NX
        send(rl.at[0, 0 : NQ + 1], rx.at[back], rx_send.at[e], rx_recv.at[back], along_x(e))
    for e in others(NX):
        arrived(rx.at[e], rx_send.at[e], rx_recv.at[e])
    for dy in range(NY):
        for dx in range(NX):
            rl[1, dy * NX + dx] = lse(
                [rl[0, dy * NX + dx]] + [rx[e, dy * NX + (dx - e) % NX] for e in range(1, NX)]
            )
    rl[1, NQ] = rl[0, NQ]
    for e in range(1, NX):
        rl[1, NQ + e] = rx[e, NQ]
    for e in others(NY):
        back = (NY - e) % NY
        send(rl.at[1], ry.at[back], ry_send.at[e], ry_recv.at[back], along_y(e))
    for e in others(NY):
        arrived(ry.at[e], ry_send.at[e], ry_recv.at[e])
    for dy in range(NY):
        for dx in range(NX):
            k = dy * NX + dx
            full = lse([rl[1, k]] + [ry[e, ((dy - e) % NY) * NX + dx] for e in range(1, NY)])
            mass = rl[1, NQ + dx] if dy == 0 else ry[dy, NQ + dx]
            rfull[:, k * XB : (k + 1) * XB] = jnp.broadcast_to(mass - full, (8, XB))
            if k == 0:
                row_out[...] = xsq - (EPSILON * LN2) * full

    eye = lax.broadcasted_iota(jnp.int32, (YB, YB), 0) == lax.broadcasted_iota(jnp.int32, (YB, YB), 1)
    per = PW // 128

    def across(v):
        return jnp.sum(jnp.where(eye, v, 0.0), axis=0, keepdims=True)

    def rows_of(b):
        return pl.ds(pl.multiple_of(b * YB, YB), YB)

    def lanes(l):
        return slice((l % per) * 128, (l % per + 1) * 128)

    def col_tiles(b):
        blocks = [scores.at[pair, rows_of(b)] for pair in range(NPAIR)]
        cblock, sblock = cstat.at[rows_of(b)], sstat.at[rows_of(b)]
        for t in range(YB // 8):
            r8 = slice(t * 8, (t + 1) * 8)
            vals = [blocks[l // per][r8, lanes(l)] + rfull[:, l * 128 : (l + 1) * 128] for l in range(NL)]
            tops = vals
            while len(tops) > 1:
                tops = [jnp.maximum(tops[i], tops[i + 1]) for i in range(0, len(tops), 2)]
            top = tops[0]
            sums = [None] * 4
            for l in range(NL):
                e = jnp.exp2(vals[l] - top)
                blocks[l // per][r8, lanes(l)] = e
                sums[l % 4] = e if l < 4 else sums[l % 4] + e
            cblock[r8] = top
            sblock[r8] = (sums[0] + sums[1]) + (sums[2] + sums[3])

    def put_stats(b):
        c = cstat[rows_of(b), :]
        best = jnp.max(c, axis=1, keepdims=True)
        summed = jnp.sum(sstat[rows_of(b), :] * jnp.exp2(c - best), axis=1, keepdims=True)
        cl[0, b] = across(best) + log2(across(summed))

    def col_loop(b):
        put_stats(b - 1)
        col_tiles(b)

    col_tiles(0)
    loop(1, NP, col_loop)
    put_stats(NP - 1)

    cl[0, NP] = log_b * LOG2E
    send(cl.at[0, 0 : NP + 1], cc, cc_send, cc_recv, sibling)
    arrived(cc, cc_send, cc_recv)
    for dz in range(NZ):
        for dc in range(2):
            cl[1, 2 * dz + dc] = lse([cl[0, 2 * dz + dc], cc[2 * dz + 1 - dc]])
    cl[1, NP] = cl[0, NP]
    cl[1, NP + 1] = cc[NP]
    for e in others(NZ):
        back = (NZ - e) % NZ
        send(cl.at[1], cz.at[back], cz_send.at[e], cz_recv.at[back], along_z(e))
    for e in others(NZ):
        arrived(cz.at[e], cz_send.at[e], cz_recv.at[e])
    for dz in range(NZ):
        for dc in range(2):
            k = 2 * dz + dc
            full = lse([cl[1, k]] + [cz[e, 2 * ((dz - e) % NZ) + dc] for e in range(1, NZ)])
            mass = cl[1, NP + dc] if dz == 0 else cz[dz, NP + dc]
            cl[2, k] = mass - full
            if k == 0:
                col_out[...] = previous[...] + EPSILON * log_b - (EPSILON * LN2) * full

    def factors(b):
        q = jnp.sum(jnp.where(eye, cl[2, b], 0.0), axis=1, keepdims=True)
        gbuf[b % 2] = jnp.exp2(cstat[rows_of(b), :] + q)

    def gap_loop(b, acc):
        blocks = [scores.at[pair, rows_of(b)] for pair in range(NPAIR)]
        gblock = gbuf.at[b % 2]
        for t in range(YB // 8):
            r8 = slice(t * 8, (t + 1) * 8)
            g = gblock[r8]
            acc = [acc[l] + blocks[l // per][r8, lanes(l)] * g for l in range(NL)]
            if t == YB // 16:
                factors(jnp.minimum(b + 1, NP - 1))
        return acc

    factors(0)
    acc = lax.fori_loop(0, NP, gap_loop, [jnp.zeros((8, 128), F32) for _ in range(NL)])
    for k in range(NQ):
        for h in range(2):
            w[k // NX, k % NX, :, h * 128 : (h + 1) * 128] = jnp.sum(acc[2 * k + h], axis=0, keepdims=True)
    for e in others(NX):
        back = (NX - e) % NX
        send(w.at[:, e], wx.at[back], wx_send.at[e], wx_recv.at[back], along_x(e))
    for e in others(NX):
        arrived(wx.at[e], wx_send.at[e], wx_recv.at[e])
    for dy in range(NY):
        w[dy, 0] = functools.reduce(jnp.add, [w[dy, 0]] + [wx[e, dy] for e in range(1, NX)])
    for e in others(NY):
        back = (NY - e) % NY
        send(w.at[e, 0], wy.at[back], wy_send.at[e], wy_recv.at[back], along_y(e))
    for e in others(NY):
        arrived(wy.at[e], wy_send.at[e], wy_recv.at[e])
    gap_out[...] = jnp.log(functools.reduce(jnp.add, [w[0, 0]] + [wy[e] for e in range(1, NY)])) - log_a

    for c in pending:
        c.wait_send()


def put_results(row, col, gap, row_out, col_out, gap_out, sem):
    copies = [
        pltpu.make_async_copy(src, dst, sem.at[n])
        for n, (src, dst) in enumerate([(row, row_out), (col, col_out), (gap, gap_out)])
    ]
    for c in copies:
        c.start()
    for c in copies:
        c.wait()


def body(measured, generated, previous, row_weight, col_weight):
    NZ, NY, NX = GRID["z"], GRID["y"], GRID["xh"] * GRID["xl"]
    NQ, NP = NX * NY, NZ * 2
    NJ, NI = NP * YB, NQ * XB
    dma = pltpu.SemaphoreType.DMA
    row, col, gap = pl.pallas_call(
        kernel,
        out_shape=(
            jax.ShapeDtypeStruct((1, XB), F32),
            jax.ShapeDtypeStruct((1, YB), F32),
            jax.ShapeDtypeStruct((1, XB), F32),
        ),
        in_specs=[pl.BlockSpec(memory_space=pltpu.HBM)] * 5,
        out_specs=(pl.BlockSpec(memory_space=pltpu.VMEM),) * 3,
        scratch_shapes=[
            pltpu.VMEM((DIM, XB), F32),
            pltpu.VMEM((DIM, YB), F32),
            pltpu.VMEM((1, YB), F32),
            pltpu.VMEM((1, XB), F32),
            pltpu.VMEM((1, YB), F32),
            pltpu.VMEM((NY, NX, DIM, XB), F32),
            pltpu.VMEM((NZ, 2, DIM + 8, YB), F32),
            pltpu.VMEM((NJ, 4 * DIM), BF16),
            pltpu.VMEM((NQ // 2, 4 * DIM, 2 * XB), BF16),
            pltpu.VMEM((NQ // 2, NJ, 2 * XB), F32),
            pltpu.VMEM((NQ // 2, 2, 8, 2 * XB), F32),
            pltpu.VMEM((NJ, 128), F32),
            pltpu.VMEM((NJ, 128), F32),
            pltpu.VMEM((2, YB, 128), F32),
            pltpu.VMEM((2, NQ + NX, 1, XB), F32),
            pltpu.VMEM((NX, NQ + 1, 1, XB), F32),
            pltpu.VMEM((NY, NQ + NX, 1, XB), F32),
            pltpu.VMEM((8, NI), F32),
            pltpu.VMEM((3, NP + 2, 1, YB), F32),
            pltpu.VMEM((NP + 1, 1, YB), F32),
            pltpu.VMEM((NZ, NP + 2, 1, YB), F32),
            pltpu.VMEM((NY, NX, 1, XB), F32),
            pltpu.VMEM((NX, NY, 1, XB), F32),
            pltpu.VMEM((NY, 1, XB), F32),
            dma((5,)),
            dma((6, NX)),
            dma((6, NX)),
            dma((2, NZ)),
            dma((NZ, 2)),
            dma((NX,)),
            dma((NX,)),
            dma((NY,)),
            dma((NY,)),
            dma,
            dma,
            dma((NZ,)),
            dma((NZ,)),
            dma((NX,)),
            dma((NX,)),
            dma((NY,)),
            dma((NY,)),
        ],
        compiler_params=pltpu.CompilerParams(
            collective_id=0, has_side_effects=True, vmem_limit_bytes=46 * 1024 * 1024
        ),
    )(
        *[
            pltpu.with_memory_space_constraint(v, pltpu.HBM)
            for v in (
                measured,
                generated,
                previous.reshape(1, YB),
                row_weight.reshape(1, XB),
                col_weight.reshape(1, YB),
            )
        ]
    )
    row, col, gap = pl.pallas_call(
        put_results,
        out_shape=(
            jax.ShapeDtypeStruct((1, XB), F32),
            jax.ShapeDtypeStruct((1, YB), F32),
            jax.ShapeDtypeStruct((1, XB), F32),
        ),
        in_specs=[pl.BlockSpec(memory_space=pltpu.VMEM)] * 3,
        out_specs=(pl.BlockSpec(memory_space=pl.ANY),) * 3,
        scratch_shapes=[dma((3,))],
        compiler_params=pltpu.CompilerParams(vmem_limit_bytes=1024 * 1024),
    )(row, col, gap)
    return row.reshape(XB), col.reshape(YB), gap.reshape(XB)


def solution(mesh):
    placed = (
        P(None, ("row", "col")),
        P(None, ("col", "row")),
        P(("col", "row")),
        P(("row", "col")),
        P(("col", "row")),
    )
    return jax.shard_map(
        body,
        mesh=mesh,
        in_specs=placed,
        out_specs=(P(("row", "col")), P(("col", "row")), P(("row", "col"))),
        check_vma=False,
    )
```
